256 devices in a mesh: row: 16 (over x, z_lo, core), col: 16 (over y, z_hi).
Axes of the slice: x: 4, y: 4, z: 8 (z_hi: 4, z_lo: 2; z = z_hi * 2 + z_lo), core: 2. Of those that a mesh axis runs over, the one named last changes fastest.
Arguments:
- matrix: float32 [16384, 16384], P('row', 'col'), as said below
- pivots: int32 [256], replicated, may hold values from 256 to 16383, as said below
- coupling: float32 [256, 256], replicated, as said below
Outputs:
- trailing: float32 [16384, 16384], P('row', 'col')
The draws below stay inside these ranges and needn't reach their ends.
Inputs may be any that keep to these rules, and one draw needn't show every extreme that they name: `pivots`: 256 distinct row indices, all at or beyond 256; among them are the last row and row 8192. `matrix`: exactly symmetric. `coupling`: exactly symmetric.
All inputs are finite; a program needn't handle non-finite values.
Results may differ from the reference program's by a relative error of at most 0.000053.
Values sent between devices are 32-bit elements; how exact they have to be, the bound alone decides.
A program may use at most 64 MiB of HBM per device.

```python
import jax
import jax.numpy as jnp
from jax import lax

N = 16384
B = 256


def draw_matrix(key, part):
    key = jax.random.fold_in(key, 11)
    base = jax.random.normal(key, (N, N), jnp.float32)
    return (base + base.T) * 0.7071


def draw_pivots(key, part):
    key = jax.random.fold_in(key, 12)
    values = jax.random.permutation(key, N - 2 - B)[:B - 2].astype(jnp.int32) + B
    others = values + (values >= N // 2).astype(jnp.int32)
    return jnp.concatenate([jnp.array([N - 1, N // 2], jnp.int32), others])


def draw_coupling(key, part):
    key = jax.random.fold_in(key, 13)
    base = jax.random.normal(key, (B, B), jnp.float32)
    return (base + base.T) * (0.7071 / B)


def setup_inputs(seed: int = 0) -> dict:
    splits = jax.random.split(jax.random.key(seed), 4)
    return {
        "matrix": draw_matrix(jax.random.fold_in(splits[3], 71), 0),
        "pivots": draw_pivots(jax.random.fold_in(splits[3], 71), 0),
        "coupling": draw_coupling(jax.random.fold_in(splits[3], 71), 0),
    }


def reference(matrix, pivots, coupling):
    order = jnp.arange(N, dtype=jnp.int32)
    order = order.at[pivots].set(jnp.arange(B, dtype=jnp.int32))
    order = order.at[:B].set(pivots)
    permuted = matrix[order][:, order]
    panel = permuted[:, :B]
    scaled = jnp.dot(panel, coupling, precision=lax.Precision.HIGHEST, preferred_element_type=jnp.float32)
    update = jnp.dot(scaled, panel.T, precision=lax.Precision.HIGHEST, preferred_element_type=jnp.float32)
    rows_idx = jnp.arange(N, dtype=jnp.int32)[:, None]
    cols_idx = jnp.arange(N, dtype=jnp.int32)[None, :]
    return jnp.where(rows_idx >= cols_idx, permuted - update, jnp.float32(0.0))
```

```python
import functools

import jax
import jax.numpy as jnp
from jax import lax
from jax.experimental import pallas as pl
from jax.experimental.pallas import tpu as pltpu
from jax.sharding import PartitionSpec as P

MESH = pl.DeviceIdType.MESH
F32 = jnp.float32
BF16 = jnp.bfloat16
HIGHEST = lax.Precision.HIGHEST


def one_hot(index, start, shape, axis):
    return lax.broadcasted_iota(jnp.int32, shape, axis) + start == index


def pick_kernel(piv, matrix, picked, sem):
    rows = matrix.shape[0]
    count = picked.shape[0]
    start = lax.axis_index("row") * rows
    picked[...] = jnp.zeros_like(picked)

    def copy(k):
        local = jnp.clip(piv[k] - start, 0, rows - 1)
        return pltpu.make_async_copy(matrix.at[pl.ds(local, 1)], picked.at[pl.ds(k, 1)], sem)

    def go(k, _):
        @pl.when((piv[k] >= start) & (piv[k] < start + rows))
        def _():
            copy(k).start()

        return 0

    def wait(k, _):
        @pl.when((piv[k] >= start) & (piv[k] < start + rows))
        def _():
            copy(k).wait()

        return 0

    lax.fori_loop(0, count, go, 0)
    lax.fori_loop(0, count, wait, 0)


def pick(matrix, pivots):
    return pl.pallas_call(
        pick_kernel,
        out_shape=jax.ShapeDtypeStruct((pivots.shape[0], matrix.shape[1]), F32),
        in_specs=[pl.BlockSpec(memory_space=pltpu.SMEM), pl.BlockSpec(memory_space=pl.ANY)],
        out_specs=pl.BlockSpec(memory_space=pltpu.VMEM),
        scratch_shapes=[pltpu.SemaphoreType.DMA],
        name="pick",
    )(pivots, matrix)


def exchange_kernel(
    picked, matrix, piv_col, piv_row, qc, qr,
    a1buf, sums, a2buf, raw, piece, corner, w0buf, w0mine,
    s_a1, r_a1, s_a2, r_a2, s_ld, r_ld, s_w, r_w, s_w0, r_w0,
    s_b, r_b, s_f, s_t, r_t, s_y, r_y, local,
):
    r, c = lax.axis_index("row"), lax.axis_index("col")
    width, cols = picked.shape
    own = raw.shape[1]
    q, core = lax.div(r, 2), lax.rem(r, 2)
    x, y, zh = lax.div(r, 4), lax.div(c, 4), lax.rem(c, 4)
    sib = r + 1 - 2 * core
    col_start = c * cols

    def remote(src, dst, ssem, rsem, row, col):
        return pltpu.make_async_remote_copy(
            src_ref=src, dst_ref=dst, send_sem=ssem, recv_sem=rsem,
            device_id=(row, col), device_id_type=MESH,
        )

    def arrived(dst, rsem):
        remote(dst, dst, rsem, rsem, sib, c).wait_recv()

    def signal(row, col):
        pl.semaphore_signal(barrier, inc=1, device_id=(row, col), device_id_type=MESH)

    def slots(g, n=1):
        return pl.ds(pl.multiple_of(g * own, own), n * own)

    barrier = pltpu.get_barrier_semaphore()
    for d in range(1, 16):
        signal(lax.rem(r + d, 16), c)
    for d in range(1, 4):
        signal(r, lax.rem(y + d, 4) * 4 + zh)
    for j in range(4):
        @pl.when((r != c) | (4 * y + j != r))
        def _():
            signal(4 * y + j, r)

    @pl.when(c != 0)
    def _():
        signal(r, 0)

    @pl.when(c == 0)
    def _():
        for b in range(1, 16):
            signal(r, b)

    greeted = 15 + 3 + 4 - jnp.where(r == c, 1, 0) + jnp.where(c == 0, 15, 1)
    pl.semaphore_wait(barrier, greeted)

    def lead_copies(act):
        @pl.when(r == 0)
        def _():
            for g in range(1, 16):
                act(remote(matrix.at[slots(g)], raw.at[1], s_ld.at[g], r_ld.at[0], g, c))
            act(pltpu.make_async_copy(matrix.at[slots(0)], raw.at[1], local.at[0]))

    lead_copies(lambda copy: copy.start())

    def a1(p):
        return remote(
            picked.at[slots(2 * p + 1 - core)], a1buf.at[p], s_a1.at[p], r_a1.at[p], sib, c
        )

    def a2(p):
        return remote(sums.at[p], a2buf.at[q], s_a2.at[p], r_a2.at[q], 2 * p + core, c)

    for d in range(1, 9):
        a1(lax.rem(q + d, 8)).start()
    for d in range(1, 9):
        p = lax.rem(q + d, 8)
        arrived(a1buf.at[p], r_a1.at[p])
        total = picked[slots(2 * p + core)] + a1buf[p]
        if d < 8:
            sums[p] = total
            a2(p).start()
        else:
            a2buf[q] = total

    hot_t = one_hot(piv_col[...], col_start, (width, cols), 1).astype(F32)
    swapped = jnp.max(hot_t, axis=0, keepdims=True) > 0

    def fixed(part):
        placed = jnp.dot(corner[part], hot_t, precision=HIGHEST, preferred_element_type=F32)
        return jnp.where(swapped, placed, raw[part])

    def send_corner(part, act):
        for b in range(1, 16):
            act(remote(corner.at[part], corner.at[part], s_w.at[part, b], r_w.at[part], r, b))

    def get_corner(part):
        @pl.when(c == 0)
        def _():
            corner[part] = raw[part, :, :width]
            send_corner(part, lambda copy: copy.start())

        @pl.when(c != 0)
        def _():
            arrived(corner.at[part], r_w.at[part])

    def b_copy(part, d):
        p = lax.rem(q + d, 8)
        return p, remote(
            piece.at[part], qc.at[part, slots(r)], s_b.at[part, d], r_b.at[part, r], 2 * p + core, c
        )

    def b_copies(part, act):
        for d in range(1, 8):
            p, copy = b_copy(part, d)

            @pl.when(2 * p + 1 >= c)
            def _():
                act(copy)

    def f_copy(part, d):
        if d == 0:
            return remote(
                piece.at[part], qc.at[part, slots(r)], s_f.at[part, 0], r_b.at[part, r], sib, c
            )
        g = 2 * lax.rem(q + d, 8) + core
        return remote(
            qc.at[part, slots(g)], qc.at[part, slots(g)], s_f.at[part, d], r_b.at[part, g], sib, c
        )

    def t_copies(part, act):
        for k in range(4):
            col = 4 * x + k
            here = (r == c) & (k == zh)

            @pl.when(jnp.logical_not(here))
            def _():
                act(
                    remote(
                        piece.at[part], qr.at[part, slots(r)],
                        s_t.at[part, k], r_t.at[part, lax.rem(r, 4)], c, col,
                    )
                )

            @pl.when(here)
            def _():
                act(
                    pltpu.make_async_copy(
                        piece.at[part], qr.at[part, slots(r)], local.at[3 + part]
                    )
                )

    def send_piece(part):
        b_copies(part, lambda copy: copy.start())
        t_copies(part, lambda copy: copy.start())

        @pl.when(sib >= c)
        def _():
            f_copy(part, 0).start()

        pltpu.make_async_copy(piece.at[part], qc.at[part, slots(r)], local.at[1 + part]).start()

    @pl.when(r == 0)
    def _():
        pltpu.make_async_copy(matrix.at[slots(0)], raw.at[1], local.at[0]).wait()

    @pl.when(r != 0)
    def _():
        arrived(raw.at[1], r_ld.at[0])

    get_corner(1)
    piece[1] = fixed(1)
    send_piece(1)

    for d in range(1, 8):
        p = lax.rem(q + d, 8)
        arrived(a2buf.at[p], r_a2.at[p])
    total = a2buf[0]
    for p in range(1, 8):
        total = total + a2buf[p]
    raw[0] = total
    get_corner(0)
    hot = one_hot(piv_row[...], col_start, (cols, width), 0).astype(F32)
    mine = jnp.dot(total, hot, precision=HIGHEST, preferred_element_type=F32)

    def w0_copy(col):
        return remote(w0mine, w0buf.at[col], s_w0.at[0], r_w0.at[col], r, 0)

    @pl.when(c != 0)
    def _():
        w0mine[...] = mine
        w0_copy(c).start()

    piece[0] = fixed(0)

    @pl.when(c == 0)
    def _():
        w0 = mine
        for b in range(1, 16):
            arrived(w0buf.at[b], r_w0.at[b])
            w0 = w0 + w0buf[b]
        piece[0, :, :width] = w0

    send_piece(0)

    def y_copies(part, act):
        for d in range(1, 4):
            col = lax.rem(y + d, 4) * 4 + zh

            @pl.when(col <= r)
            def _():
                block = qr.at[part, slots(4 * y, 4)]
                act(remote(block, block, s_y.at[part, d], r_y.at[part, y], r, col))

    def run_y(part):
        for j in range(4):
            here = (r == c) & (4 * y + j == r)

            @pl.when(jnp.logical_not(here))
            def _():
                arrived(qr.at[part, slots(4 * y + j)], r_t.at[part, j])

            @pl.when(here)
            def _():
                pltpu.make_async_copy(
                    piece.at[part], qr.at[part, slots(r)], local.at[3 + part]
                ).wait()

        y_copies(part, lambda copy: copy.start())

    def run_f(part):
        for d in range(1, 8):
            g = 2 * lax.rem(q + d, 8) + core

            @pl.when(2 * q + 1 >= c)
            def _():
                arrived(qc.at[part, slots(g)], r_b.at[part, g])

            @pl.when(sib >= c)
            def _():
                f_copy(part, d).start()

    run_y(1)
    run_y(0)
    run_f(1)
    run_f(0)

    for part in (1, 0):
        for d in range(8):
            g = 2 * lax.rem(q + d, 8) + 1 - core

            @pl.when(r >= c)
            def _():
                arrived(qc.at[part, slots(g)], r_b.at[part, g])

        for d in range(1, 4):
            there = lax.rem(y + d, 4)

            @pl.when(c <= r)
            def _():
                arrived(qr.at[part, slots(4 * there, 4)], r_y.at[part, there])

        pltpu.make_async_copy(piece.at[part], qc.at[part, slots(r)], local.at[1 + part]).wait()

    lead_copies(lambda copy: copy.wait_send() if copy.is_remote else None)
    for d in range(1, 9):
        a1(lax.rem(q + d, 8)).wait_send()
    for d in range(1, 8):
        a2(lax.rem(q + d, 8)).wait_send()

    @pl.when(c != 0)
    def _():
        w0_copy(c).wait_send()

    for part in (1, 0):
        @pl.when(c == 0)
        def _():
            send_corner(part, lambda copy: copy.wait_send())

        b_copies(part, lambda copy: copy.wait_send())
        t_copies(part, lambda copy: copy.wait_send() if copy.is_remote else None)
        y_copies(part, lambda copy: copy.wait_send())

        @pl.when(sib >= c)
        def _():
            for d in range(8):
                f_copy(part, d).wait_send()


def exchange(picked, matrix, piv_col, piv_row):
    width, cols = picked.shape
    own = width // 16
    dma = pltpu.SemaphoreType.DMA
    out = jax.ShapeDtypeStruct((2, width, cols), F32)
    any_spec = pl.BlockSpec(memory_space=pl.ANY)
    vmem = pl.BlockSpec(memory_space=pltpu.VMEM)
    return pl.pallas_call(
        exchange_kernel,
        out_shape=(out, out),
        in_specs=[vmem, any_spec, vmem, vmem],
        out_specs=(any_spec, any_spec),
        scratch_shapes=[
            pltpu.VMEM((8, own, cols), F32),
            pltpu.VMEM((8, own, cols), F32),
            pltpu.VMEM((8, own, cols), F32),
            pltpu.VMEM((2, own, cols), F32),
            pltpu.VMEM((2, own, cols), F32),
            pltpu.VMEM((2, own, width), F32),
            pltpu.VMEM((16, own, width), F32),
            pltpu.VMEM((own, width), F32),
            dma((8,)), dma((8,)), dma((8,)), dma((8,)),
            dma((16,)), dma((1,)), dma((2, 16)), dma((2,)), dma((1,)), dma((16,)),
            dma((2, 8)), dma((2, 16)), dma((2, 8)), dma((2, 4)), dma((2, 4)), dma((2, 4)), dma((2, 4)),
            dma((5,)),
        ],
        compiler_params=pltpu.CompilerParams(
            collective_id=0, has_side_effects=True, vmem_limit_bytes=32 * 1024 * 1024
        ),
        name="exchange",
    )(picked, matrix, piv_col, piv_row)


def split(value, n):
    terms = []
    for _ in range(n):
        term = value.astype(BF16)
        terms.append(term)
        value = value - term.astype(F32)
    return terms


def update_kernel(piv_col, piv_row, m, qc, qr, coupling, out, hot_t, panel, lead):
    r, c = lax.axis_index("row"), lax.axis_index("col")
    tile, cols = out.shape
    width = coupling.shape[0]
    step = pl.program_id(0)
    row_start = r * cols + step * tile
    col_start = c * cols

    @pl.when(r < c)
    def _():
        out[...] = jnp.zeros_like(out)

    @pl.when((r >= c) & (step == 0))
    def _():
        hot_t[...] = one_hot(piv_col[...], col_start, (width, cols), 1).astype(BF16)
        for i, term in enumerate(split(qc[0], 2)):
            panel[i] = term
        for i, term in enumerate(split(qc[1], 3)):
            lead[i] = term

    def dot(a, b):
        return jnp.dot(a, b, preferred_element_type=F32)

    @pl.when(r >= c)
    def _():
        panel_rows = qr[0].T
        scaled = jnp.dot(panel_rows, coupling[...], precision=HIGHEST, preferred_element_type=F32)
        s_hi, s_lo = split(scaled, 2)
        update = dot(s_hi, panel[0]) + dot(s_hi, panel[1]) + dot(s_lo, panel[0])
        hot = one_hot(piv_row[...], row_start, (tile, width), 0)
        hit_row = jnp.max(hot.astype(F32), axis=1, keepdims=True) > 0
        hit_col = jnp.max(hot_t[...].astype(F32), axis=0, keepdims=True) > 0
        hot = hot.astype(F32).astype(BF16)
        new_rows = dot(hot, lead[0]) + dot(hot, lead[1]) + dot(hot, lead[2])
        lead_cols = jnp.where(hit_row, 0.0, qr[1].T)
        new_cols = sum(dot(term, hot_t[...]) for term in split(lead_cols, 3))
        value = jnp.where(hit_row | hit_col, 0.0, m[...]) + new_rows + new_cols
        spread = jnp.concatenate([panel_rows, jnp.zeros((tile, cols - width), F32)], axis=1)
        places = lax.broadcasted_iota(jnp.int32, (tile, cols), 1)
        value = jnp.where((places < width) & (c == 0), spread, value)
        below = lax.broadcasted_iota(jnp.int32, (tile, cols), 0) + row_start >= places + col_start
        out[...] = jnp.where(below, value - update, 0.0)


def update(piv_col, piv_row, matrix, qc, qr, coupling):
    rows, cols = matrix.shape
    width = coupling.shape[0]
    tile = min(rows, 256)

    def whole(shape):
        return pl.BlockSpec(shape, lambda i: (0,) * len(shape))

    return pl.pallas_call(
        update_kernel,
        grid=(rows // tile,),
        out_shape=jax.ShapeDtypeStruct((rows, cols), F32),
        in_specs=[
            whole((width, 1)),
            whole((1, width)),
            pl.BlockSpec((tile, cols), lambda i: (i, 0)),
            whole((2, width, cols)),
            pl.BlockSpec((2, width, tile), lambda i: (0, 0, i)),
            whole((width, width)),
        ],
        out_specs=pl.BlockSpec((tile, cols), lambda i: (i, 0)),
        scratch_shapes=[
            pltpu.VMEM((width, cols), BF16),
            pltpu.VMEM((2, width, cols), BF16),
            pltpu.VMEM((3, width, cols), BF16),
        ],
        compiler_params=pltpu.CompilerParams(vmem_limit_bytes=48 * 1024 * 1024),
        name="update",
    )(piv_col, piv_row, matrix, qc, qr, coupling)


def per_device(matrix, pivots, coupling):
    width = coupling.shape[0]
    piv_col, piv_row = pivots.reshape(width, 1), pivots.reshape(1, width)
    picked = pick(matrix, pivots)
    qc, qr = exchange(picked, matrix, piv_col, piv_row)
    return update(piv_col, piv_row, matrix, qc, qr, coupling)


def solution(mesh):
    return jax.shard_map(
        per_device,
        mesh=mesh,
        in_specs=(P("row", "col"), P(), P()),
        out_specs=P("row", "col"),
        check_vma=False,
    )
```

```python
import functools

import jax
import jax.numpy as jnp
from jax import lax
from jax.experimental import pallas as pl
from jax.experimental.pallas import tpu as pltpu
from jax.sharding import PartitionSpec as P

MESH = pl.DeviceIdType.MESH
F32 = jnp.float32
BF16 = jnp.bfloat16
HIGHEST = lax.Precision.HIGHEST
CAP = 32


def one_hot(index, start, shape, axis):
    return lax.broadcasted_iota(jnp.int32, shape, axis) + start == index


def pick_kernel(piv, matrix, picked, sem):
    rows = matrix.shape[0]
    count = picked.shape[0]
    start = lax.axis_index("row") * rows
    picked[...] = jnp.zeros_like(picked)

    def copy(k):
        local = jnp.clip(piv[k] - start, 0, rows - 1)
        return pltpu.make_async_copy(matrix.at[pl.ds(local, 1)], picked.at[pl.ds(k, 1)], sem)

    def go(k, _):
        @pl.when((piv[k] >= start) & (piv[k] < start + rows))
        def _():
            copy(k).start()

        return 0

    def wait(k, _):
        @pl.when((piv[k] >= start) & (piv[k] < start + rows))
        def _():
            copy(k).wait()

        return 0

    lax.fori_loop(0, count, go, 0)
    lax.fori_loop(0, count, wait, 0)


def pick(matrix, pivots):
    return pl.pallas_call(
        pick_kernel,
        out_shape=jax.ShapeDtypeStruct((pivots.shape[0], matrix.shape[1]), F32),
        in_specs=[pl.BlockSpec(memory_space=pltpu.SMEM), pl.BlockSpec(memory_space=pl.ANY)],
        out_specs=pl.BlockSpec(memory_space=pltpu.VMEM),
        scratch_shapes=[pltpu.SemaphoreType.DMA],
        name="pick",
    )(pivots, matrix)


def exchange_kernel(
    picked, matrix, piv_col, piv_row, qc, qr,
    a1buf, sums, a2buf, raw, piece, corner, w0buf, w0mine,
    s_a1, r_a1, s_a2, r_a2, s_ld, r_ld, s_w, r_w, s_w0, r_w0,
    s_b, r_b, s_f, s_t, r_t, s_y, r_y, local,
):
    r, c = lax.axis_index("row"), lax.axis_index("col")
    width, cols = picked.shape
    own = raw.shape[1]
    q, core = lax.div(r, 2), lax.rem(r, 2)
    x, y, zh = lax.div(r, 4), lax.div(c, 4), lax.rem(c, 4)
    sib = r + 1 - 2 * core
    col_start = c * cols

    def remote(src, dst, ssem, rsem, row, col):
        return pltpu.make_async_remote_copy(
            src_ref=src, dst_ref=dst, send_sem=ssem, recv_sem=rsem,
            device_id=(row, col), device_id_type=MESH,
        )

    def arrived(dst, rsem):
        remote(dst, dst, rsem, rsem, sib, c).wait_recv()

    def signal(row, col):
        pl.semaphore_signal(barrier, inc=1, device_id=(row, col), device_id_type=MESH)

    def slots(g, n=1):
        return pl.ds(pl.multiple_of(g * own, own), n * own)

    barrier = pltpu.get_barrier_semaphore()
    for d in range(1, 16):
        signal(lax.rem(r + d, 16), c)
    for d in range(1, 4):
        signal(r, lax.rem(y + d, 4) * 4 + zh)
    for j in range(4):
        @pl.when((r != c) | (4 * y + j != r))
        def _():
            signal(4 * y + j, r)

    @pl.when(c != 0)
    def _():
        signal(r, 0)

    @pl.when(c == 0)
    def _():
        for b in range(1, 16):
            signal(r, b)

    greeted = 15 + 3 + 4 - jnp.where(r == c, 1, 0) + jnp.where(c == 0, 15, 1)
    pl.semaphore_wait(barrier, greeted)

    def lead_copies(act):
        @pl.when(r == 0)
        def _():
            for g in range(1, 16):
                act(remote(matrix.at[slots(g)], raw.at[1], s_ld.at[g], r_ld.at[0], g, c))
            act(pltpu.make_async_copy(matrix.at[slots(0)], raw.at[1], local.at[0]))

    lead_copies(lambda copy: copy.start())

    def a1(p):
        return remote(
            picked.at[slots(2 * p + 1 - core)], a1buf.at[p], s_a1.at[p], r_a1.at[p], sib, c
        )

    def a2(p):
        return remote(sums.at[p], a2buf.at[q], s_a2.at[p], r_a2.at[q], 2 * p + core, c)

    for d in range(1, 9):
        a1(lax.rem(q + d, 8)).start()
    for d in range(1, 9):
        p = lax.rem(q + d, 8)
        arrived(a1buf.at[p], r_a1.at[p])
        total = picked[slots(2 * p + core)] + a1buf[p]
        if d < 8:
            sums[p] = total
            a2(p).start()
        else:
            a2buf[q] = total

    hot_t = one_hot(piv_col[...], col_start, (width, cols), 1).astype(F32)
    swapped = jnp.max(hot_t, axis=0, keepdims=True) > 0

    def fixed(part):
        placed = jnp.dot(corner[part], hot_t, precision=HIGHEST, preferred_element_type=F32)
        return jnp.where(swapped, placed, raw[part])

    def send_corner(part, act):
        for b in range(1, 16):
            act(remote(corner.at[part], corner.at[part], s_w.at[part, b], r_w.at[part], r, b))

    def get_corner(part):
        @pl.when(c == 0)
        def _():
            corner[part] = raw[part, :, :width]
            send_corner(part, lambda copy: copy.start())

        @pl.when(c != 0)
        def _():
            arrived(corner.at[part], r_w.at[part])

    def b_copy(part, d):
        p = lax.rem(q + d, 8)
        return p, remote(
            piece.at[part], qc.at[part, slots(r)], s_b.at[part, d], r_b.at[part, r], 2 * p + core, c
        )

    def b_copies(part, act):
        for d in range(1, 8):
            p, copy = b_copy(part, d)

            @pl.when(2 * p + 1 >= c)
            def _():
                act(copy)

    def f_copy(part, d):
        if d == 0:
            return remote(
                piece.at[part], qc.at[part, slots(r)], s_f.at[part, 0], r_b.at[part, r], sib, c
            )
        g = 2 * lax.rem(q + d, 8) + core
        return remote(
            qc.at[part, slots(g)], qc.at[part, slots(g)], s_f.at[part, d], r_b.at[part, g], sib, c
        )

    def t_copies(part, act):
        for k in range(4):
            col = 4 * x + k
            here = (r == c) & (k == zh)

            @pl.when(jnp.logical_not(here))
            def _():
                act(
                    remote(
                        piece.at[part], qr.at[part, slots(r)],
                        s_t.at[part, k], r_t.at[part, lax.rem(r, 4)], c, col,
                    )
                )

            @pl.when(here)
            def _():
                act(
                    pltpu.make_async_copy(
                        piece.at[part], qr.at[part, slots(r)], local.at[3 + part]
                    )
                )

    def send_piece(part):
        b_copies(part, lambda copy: copy.start())
        t_copies(part, lambda copy: copy.start())

        @pl.when(sib >= c)
        def _():
            f_copy(part, 0).start()

        pltpu.make_async_copy(piece.at[part], qc.at[part, slots(r)], local.at[1 + part]).start()

    @pl.when(r == 0)
    def _():
        pltpu.make_async_copy(matrix.at[slots(0)], raw.at[1], local.at[0]).wait()

    @pl.when(r != 0)
    def _():
        arrived(raw.at[1], r_ld.at[0])

    get_corner(1)
    piece[1] = fixed(1)
    send_piece(1)

    for d in range(1, 8):
        p = lax.rem(q + d, 8)
        arrived(a2buf.at[p], r_a2.at[p])
    total = a2buf[0]
    for p in range(1, 8):
        total = total + a2buf[p]
    raw[0] = total
    get_corner(0)
    hot = one_hot(piv_row[...], col_start, (cols, width), 0).astype(F32)
    mine = jnp.dot(total, hot, precision=HIGHEST, preferred_element_type=F32)

    def w0_copy(col):
        return remote(w0mine, w0buf.at[col], s_w0.at[0], r_w0.at[col], r, 0)

    @pl.when(c != 0)
    def _():
        w0mine[...] = mine
        w0_copy(c).start()

    piece[0] = fixed(0)

    @pl.when(c == 0)
    def _():
        w0 = mine
        for b in range(1, 16):
            arrived(w0buf.at[b], r_w0.at[b])
            w0 = w0 + w0buf[b]
        piece[0, :, :width] = w0

    send_piece(0)

    def y_copies(part, act):
        for d in range(1, 4):
            col = lax.rem(y + d, 4) * 4 + zh

            @pl.when(col <= r)
            def _():
                block = qr.at[part, slots(4 * y, 4)]
                act(remote(block, block, s_y.at[part, d], r_y.at[part, y], r, col))

    def run_y(part):
        for j in range(4):
            here = (r == c) & (4 * y + j == r)

            @pl.when(jnp.logical_not(here))
            def _():
                arrived(qr.at[part, slots(4 * y + j)], r_t.at[part, j])

            @pl.when(here)
            def _():
                pltpu.make_async_copy(
                    piece.at[part], qr.at[part, slots(r)], local.at[3 + part]
                ).wait()

        y_copies(part, lambda copy: copy.start())

    def run_f(part):
        for d in range(1, 8):
            g = 2 * lax.rem(q + d, 8) + core

            @pl.when(2 * q + 1 >= c)
            def _():
                arrived(qc.at[part, slots(g)], r_b.at[part, g])

            @pl.when(sib >= c)
            def _():
                f_copy(part, d).start()

    run_y(1)
    run_y(0)
    run_f(1)
    run_f(0)

    for part in (1, 0):
        for d in range(8):
            g = 2 * lax.rem(q + d, 8) + 1 - core

            @pl.when(r >= c)
            def _():
                arrived(qc.at[part, slots(g)], r_b.at[part, g])

        for d in range(1, 4):
            there = lax.rem(y + d, 4)

            @pl.when(c <= r)
            def _():
                arrived(qr.at[part, slots(4 * there, 4)], r_y.at[part, there])

        pltpu.make_async_copy(piece.at[part], qc.at[part, slots(r)], local.at[1 + part]).wait()

    lead_copies(lambda copy: copy.wait_send() if copy.is_remote else None)
    for d in range(1, 9):
        a1(lax.rem(q + d, 8)).wait_send()
    for d in range(1, 8):
        a2(lax.rem(q + d, 8)).wait_send()

    @pl.when(c != 0)
    def _():
        w0_copy(c).wait_send()

    for part in (1, 0):
        @pl.when(c == 0)
        def _():
            send_corner(part, lambda copy: copy.wait_send())

        b_copies(part, lambda copy: copy.wait_send())
        t_copies(part, lambda copy: copy.wait_send() if copy.is_remote else None)
        y_copies(part, lambda copy: copy.wait_send())

        @pl.when(sib >= c)
        def _():
            for d in range(8):
                f_copy(part, d).wait_send()


def exchange(picked, matrix, piv_col, piv_row):
    width, cols = picked.shape
    own = width // 16
    dma = pltpu.SemaphoreType.DMA
    out = jax.ShapeDtypeStruct((2, width, cols), F32)
    any_spec = pl.BlockSpec(memory_space=pl.ANY)
    vmem = pl.BlockSpec(memory_space=pltpu.VMEM)
    return pl.pallas_call(
        exchange_kernel,
        out_shape=(out, out),
        in_specs=[vmem, any_spec, vmem, vmem],
        out_specs=(any_spec, any_spec),
        scratch_shapes=[
            pltpu.VMEM((8, own, cols), F32),
            pltpu.VMEM((8, own, cols), F32),
            pltpu.VMEM((8, own, cols), F32),
            pltpu.VMEM((2, own, cols), F32),
            pltpu.VMEM((2, own, cols), F32),
            pltpu.VMEM((2, own, width), F32),
            pltpu.VMEM((16, own, width), F32),
            pltpu.VMEM((own, width), F32),
            dma((8,)), dma((8,)), dma((8,)), dma((8,)),
            dma((16,)), dma((1,)), dma((2, 16)), dma((2,)), dma((1,)), dma((16,)),
            dma((2, 8)), dma((2, 16)), dma((2, 8)), dma((2, 4)), dma((2, 4)), dma((2, 4)), dma((2, 4)),
            dma((5,)),
        ],
        compiler_params=pltpu.CompilerParams(
            collective_id=0, has_side_effects=True, vmem_limit_bytes=32 * 1024 * 1024
        ),
        name="exchange",
    )(picked, matrix, piv_col, piv_row)


def split(value, n):
    terms = []
    for _ in range(n):
        term = value.astype(BF16)
        terms.append(term)
        value = value - term.astype(F32)
    return terms


def update_kernel(piv_col, piv_row, m, qc, qr, coupling, out, hot_t, panel, lead):
    r, c = lax.axis_index("row"), lax.axis_index("col")
    tile, cols = out.shape
    width = coupling.shape[0]
    step = pl.program_id(0)
    row_start = r * cols + step * tile
    col_start = c * cols

    @pl.when(r < c)
    def _():
        out[...] = jnp.zeros_like(out)

    @pl.when((r >= c) & (step == 0))
    def _():
        hot_t[...] = one_hot(piv_col[...], col_start, (width, cols), 1).astype(BF16)
        for i, term in enumerate(split(qc[0], 2)):
            panel[i] = term
        for i, term in enumerate(split(qc[1], 3)):
            lead[i] = term

    def dot(a, b):
        return jnp.dot(a, b, preferred_element_type=F32)

    @pl.when(r >= c)
    def _():
        panel_rows = qr[0].T
        scaled = jnp.dot(panel_rows, coupling[...], precision=HIGHEST, preferred_element_type=F32)
        s_hi, s_lo = split(scaled, 2)
        update = dot(s_hi, panel[0]) + dot(s_hi, panel[1]) + dot(s_lo, panel[0])
        hot = one_hot(piv_row[...], row_start, (tile, width), 0)
        hit_row = jnp.max(hot.astype(F32), axis=1, keepdims=True) > 0
        hit_col = jnp.max(hot_t[...].astype(F32), axis=0, keepdims=True) > 0
        hot = hot.astype(F32).astype(BF16)
        new_rows = dot(hot, lead[0]) + dot(hot, lead[1]) + dot(hot, lead[2])
        lead_cols = jnp.where(hit_row, 0.0, qr[1].T)
        new_cols = sum(dot(term, hot_t[...]) for term in split(lead_cols, 3))
        value = jnp.where(hit_row | hit_col, 0.0, m[...]) + new_rows + new_cols
        spread = jnp.concatenate([panel_rows, jnp.zeros((tile, cols - width), F32)], axis=1)
        places = lax.broadcasted_iota(jnp.int32, (tile, cols), 1)
        value = jnp.where((places < width) & (c == 0), spread, value)
        below = lax.broadcasted_iota(jnp.int32, (tile, cols), 0) + row_start >= places + col_start
        out[...] = jnp.where(below, value - update, 0.0)


def update(piv_col, piv_row, matrix, qc, qr, coupling):
    rows, cols = matrix.shape
    width = coupling.shape[0]
    tile = min(rows, 256)

    def whole(shape):
        return pl.BlockSpec(shape, lambda i: (0,) * len(shape))

    return pl.pallas_call(
        update_kernel,
        grid=(rows // tile,),
        out_shape=jax.ShapeDtypeStruct((rows, cols), F32),
        in_specs=[
            whole((width, 1)),
            whole((1, width)),
            pl.BlockSpec((tile, cols), lambda i: (i, 0)),
            whole((2, width, cols)),
            pl.BlockSpec((2, width, tile), lambda i: (0, 0, i)),
            whole((width, width)),
        ],
        out_specs=pl.BlockSpec((tile, cols), lambda i: (i, 0)),
        scratch_shapes=[
            pltpu.VMEM((width, cols), BF16),
            pltpu.VMEM((2, width, cols), BF16),
            pltpu.VMEM((3, width, cols), BF16),
        ],
        compiler_params=pltpu.CompilerParams(vmem_limit_bytes=48 * 1024 * 1024),
        name="update",
    )(piv_col, piv_row, matrix, qc, qr, coupling)


def order(s):
    return lax.rem(s, 2) * 8 + lax.div(s, 2)


def blocks_of(piv, rows):
    block = jnp.right_shift(piv, rows.bit_length() - 1)
    return jnp.bitwise_and(block, 1) * 8 + jnp.right_shift(block, 1)


def places(piv_col, piv_row, rows):
    width = piv_col.shape[0]
    first = lax.broadcasted_iota(jnp.int32, (width, width), 0)
    second = lax.broadcasted_iota(jnp.int32, (width, width), 1)
    block_col, block_row = blocks_of(piv_col, rows), blocks_of(piv_row, rows)
    same = block_col == block_row
    rank_col = jnp.sum(jnp.where(same & (second < first), 1, 0), axis=1, keepdims=True)
    rank_row = jnp.sum(jnp.where(same & (first < second), 1, 0), axis=0, keepdims=True)
    return block_col * CAP + rank_col, block_row * CAP + rank_row


def listed(place_row, piv_row, start, count):
    spot = lax.broadcasted_iota(jnp.int32, (count, place_row.shape[1]), 0) + start
    return jnp.sum(jnp.where(spot == place_row, piv_row + 1, 0), axis=1, keepdims=True) - 1


def compact_kernel(
    matrix, piv_col, piv_row, qc, qr, swaps, corner,
    block, picked, fixed, hall, abuf, lead, piece, kout, kin, w0out, w0in, lout,
    s_a, r_a, s_sib, r_sib, s_ld, r_ld, s_k, r_k, s_w0, r_w0, s_l, r_l,
    s_b, r_b, s_f, s_t, r_t, s_y, s_z, r_y, local,
):
    r, c = lax.axis_index("row"), lax.axis_index("col")
    rows, cols = matrix.shape
    width = piv_col.shape[0]
    half, part = width // 2, cols // 8
    q, core = lax.div(r, 2), lax.rem(r, 2)
    x, y, zh = lax.div(r, 4), lax.div(c, 4), lax.rem(c, 4)
    sib = r + 1 - 2 * core
    chunk = lax.div(order(c), 4)

    def remote(src, dst, ssem, rsem, row, col):
        return pltpu.make_async_remote_copy(
            src_ref=src, dst_ref=dst, send_sem=ssem, recv_sem=rsem,
            device_id=(row, col), device_id_type=MESH,
        )

    def arrived(dst, rsem):
        remote(dst, dst, rsem, rsem, sib, c).wait_recv()

    def start(copy):
        copy.start()

    def sent(copy):
        copy.wait_send()

    def dot(a, b):
        return jnp.dot(a, b, precision=HIGHEST, preferred_element_type=F32)

    load = pltpu.make_async_copy(matrix, block, local.at[0])
    load.start()

    barrier = pltpu.get_barrier_semaphore()

    def signal(row, col):
        pl.semaphore_signal(barrier, inc=1, device_id=(row, col), device_id_type=MESH)

    for d in range(1, 16):
        signal(lax.rem(r + d, 16), c)
    for d in (1, 3):
        signal(r, lax.rem(y + d, 4) * 4 + zh)
    for j in range(4):
        @pl.when((r != c) | (4 * y + j != r))
        def _():
            signal(4 * y + j, r)

    @pl.when(c != 0)
    def _():
        signal(r, 0)

    @pl.when(c == 0)
    def _():
        for b in range(1, 16):
            signal(r, b)

    @pl.when(r > c)
    def _():
        for j in range(8):
            signal(2 * j + lax.rem(c, 2), r)

    greeted = 15 + 2 + 4 - jnp.where(r == c, 1, 0) + jnp.where(c == 0, 15, 1)
    greeted = greeted + lax.div(c - core + 1, 2)

    place_col, place_row = places(piv_col[...], piv_row[...], rows)
    spots = lax.broadcasted_iota(jnp.int32, (16 * CAP, width), 0)
    hall[...] = (spots == place_row).astype(F32)
    mine = order(r) * CAP
    have = listed(place_row, piv_row[...], mine, CAP) >= 0
    load.wait()
    for t in range(CAP):
        local_row = jnp.sum(jnp.where(place_row == mine + t, piv_row[...] - r * rows, 0))
        picked[pl.ds(t, 1)] = block[pl.ds(jnp.clip(local_row, 0, rows - 1), 1)]
    picked[...] = jnp.where(have, picked[...], 0.0)

    pl.semaphore_wait(barrier, greeted)

    def lead_copy(p):
        return remote(
            block.at[pl.ds(0, width), pl.ds(p * part, part)], lead, s_ld.at[p], r_ld.at[0], 2 * p, c
        )

    @pl.when(r == 0)
    def _():
        for p in range(1, 8):
            lead_copy(p).start()

    here_piv = listed(place_row, piv_row[...], chunk * 128, 128)
    spread = one_hot(here_piv, c * cols, (128, cols), 1).astype(F32)
    swapped = jnp.max(spread, axis=0, keepdims=True) > 0

    def k_copy(i, b):
        return remote(
            kout.at[i, lax.div(order(b), 4)], kin.at[i], s_k.at[i, b], r_k.at[i], r, b
        )

    def k_copies(i, act):
        for b in range(1, 16):
            act(k_copy(i, b))

    def k_lists(i, value):
        compact = lax.dot_general(
            value, hall[...], (((1,), (1,)), ((), ())),
            precision=HIGHEST, preferred_element_type=F32,
        )
        for j in range(4):
            kout[i, j] = compact[:, 128 * j : 128 * (j + 1)]

    def w0_copy(b):
        return remote(w0out, w0in.at[b], s_w0.at[0], r_w0.at[b], r, 0)

    @pl.when(c == 0)
    def _():
        k_lists(0, picked[:, :width])
        k_copies(0, start)
        kin[0] = kout[0, 0]

    w0out[...] = lax.dot_general(
        picked[...], spread, (((1,), (1,)), ((), ())),
        precision=HIGHEST, preferred_element_type=F32,
    )

    @pl.when(c != 0)
    def _():
        w0_copy(c).start()
        arrived(kin.at[0], r_k.at[0])

    fixed[...] = jnp.where(swapped, dot(kin[0], spread), picked[...])

    @pl.when(c == 0)
    def _():
        for b in range(1, 16):
            arrived(w0in.at[b], r_w0.at[b])
        w0in[0] = w0out[...]
        total = jnp.zeros((CAP, width), F32)
        for j in range(4):
            listing = sum(
                w0in[b] for b in range(16) if ((b % 2) * 8 + b // 2) // 4 == j
            )
            total = total + dot(listing, hall[128 * j : 128 * (j + 1)])
        fixed[:, :width] = total

    def a_copy(d):
        p = lax.rem(q + d, 8)
        cut = pl.ds(pl.multiple_of(p * part, part), part)
        return remote(fixed.at[:, cut], abuf.at[core, q], s_a.at[d], r_a.at[q], 2 * p + core, c)

    for d in range(1, 8):
        a_copy(d).start()
    abuf[core, q] = fixed[:, pl.ds(pl.multiple_of(q * part, part), part)]

    lead_sib = remote(lead, lead, s_sib.at[0], r_sib.at[0], sib, c)

    @pl.when(r == 0)
    def _():
        lead[...] = block[:width, :part]

    @pl.when((core == 0) & (r != 0))
    def _():
        arrived(lead, r_ld.at[0])

    @pl.when(core == 0)
    def _():
        lead_sib.start()

    for d in range(1, 8):
        p = lax.rem(q + d, 8)
        arrived(abuf.at[core, p], r_a.at[p])
    a_sib = remote(abuf.at[core], abuf.at[core], s_sib.at[1], r_sib.at[1], sib, c)
    a_sib.start()
    arrived(abuf.at[1 - core], r_sib.at[1])

    lay = jnp.where(core == 0, hall[:, :half], hall[:, half:])
    piece[...] = lax.dot_general(
        lay, abuf[...].reshape(16 * CAP, part), (((0,), (0,)), ((), ())),
        precision=HIGHEST, preferred_element_type=F32,
    )

    def slot(k):
        return pl.ds(pl.multiple_of(k * half, half), half)

    def t_copies(act, act_here):
        for k in range(4):
            here = (r == c) & (k == zh)

            @pl.when(jnp.logical_not(here))
            def _():
                act(
                    remote(
                        piece, qr.at[q, slot(core)], s_t.at[k], r_t.at[lax.rem(r, 4)], c, 4 * x + k
                    )
                )

            @pl.when(here)
            def _():
                act_here(pltpu.make_async_copy(piece, qr.at[q, slot(core)], local.at[1]))

    def b_copies(act):
        for d in range(1, 8):
            p = lax.rem(q + d, 8)

            @pl.when(2 * p + 1 >= c)
            def _():
                act(remote(piece, qc.at[q, slot(core)], s_b.at[d], r_b.at[core, q], 2 * p + core, c))

    def f_copy(d):
        p = lax.rem(q + d, 8)
        src = piece if d == 0 else qc.at[p, slot(core)]
        return remote(src, qc.at[p, slot(core)], s_f.at[d], r_b.at[core, p], sib, c)

    t_copies(start, start)

    @pl.when(sib >= c)
    def _():
        f_copy(0).start()

    b_copies(start)
    keep = pltpu.make_async_copy(piece, qc.at[q, slot(core)], local.at[2])
    keep.start()

    @pl.when(core == 1)
    def _():
        arrived(lead, r_sib.at[0])

    lists = hall[pl.ds(pl.multiple_of(core * 8 * CAP, 8 * CAP), 8 * CAP)]
    lout[...] = dot(lists, lead[...]).reshape(8, CAP, part)

    def l_copies(act, act_here):
        for j in range(8):
            s = 2 * j + core
            as_row = s >= c
            row, col = jnp.where(as_row, s, c), jnp.where(as_row, c, s)
            dst = swaps.at[jnp.where(as_row, 0, 1), q]
            here = as_row & (s == r)

            @pl.when(jnp.logical_not(here))
            def _():
                act(
                    remote(lout.at[j], dst, s_l.at[j], r_l.at[jnp.where(as_row, 0, 1), q], row, col)
                )

            @pl.when(here)
            def _():
                act_here(j)

    def keep_lead(j):
        swaps[0, q] = lout[j]

    l_copies(start, keep_lead)

    def need(there):
        return 4 * there + zh <= r

    up, down, across = lax.rem(y + 1, 4), lax.rem(y + 3, 4), lax.rem(y + 2, 4)

    def y_ref(owner, j):
        return qr.at[2 * owner + j // 2, slot(j % 2)]

    def y_copy(j, way):
        col = (up if way == 0 else down) * 4 + zh
        return remote(y_ref(y, j), y_ref(y, j), s_y.at[way, j], r_y.at[y, j], r, col)

    def z_copy(j):
        owner, to = (down, up) if j < 2 else (up, down)
        return remote(y_ref(owner, j), y_ref(owner, j), s_z.at[j], r_y.at[owner, j], r, 4 * to + zh)

    def y_copies(j, act):
        on_up = need(up) | need(across) if j < 2 else need(up)
        on_down = need(down) | need(across) if j >= 2 else need(down)

        @pl.when(on_up)
        def _():
            act(y_copy(j, 0))

        @pl.when(on_down)
        def _():
            act(y_copy(j, 1))

    def z_copies(j, act):
        @pl.when(need(up) if j < 2 else need(down))
        def _():
            act(z_copy(j))

    for j in range(4):
        here = (r == c) & (4 * y + j == r)

        @pl.when(jnp.logical_not(here))
        def _():
            arrived(y_ref(y, j), r_t.at[j])

        @pl.when(here)
        def _():
            pltpu.make_async_copy(piece, qr.at[q, slot(core)], local.at[1]).wait()

        y_copies(j, start)

    @pl.when((r >= c))
    def _():
        for p in range(8):
            @pl.when(p != q)
            def _():
                arrived(swaps.at[0, p], r_l.at[0, p])

    @pl.when(c == 0)
    def _():
        k_lists(1, jnp.concatenate([swaps[0, p] for p in range(width // part)], axis=1))
        k_copies(1, start)
        kin[1] = kout[1, 0]

    for j in (0, 1, 2, 3):
        owner = down if j < 2 else up

        @pl.when(need(y) | (need(up) if j < 2 else need(down)))
        def _():
            arrived(y_ref(owner, j), r_y.at[owner, j])

        z_copies(j, start)

    for d in range(1, 8):
        p = lax.rem(q + d, 8)

        @pl.when(2 * q + 1 >= c)
        def _():
            arrived(qc.at[p, slot(core)], r_b.at[core, p])

        @pl.when(sib >= c)
        def _():
            f_copy(d).start()

    @pl.when(r >= c)
    def _():
        for p in range(8):
            arrived(qc.at[p, slot(1 - core)], r_b.at[1 - core, p])
        for j in range(4):
            owner = up if j < 2 else down
            arrived(y_ref(owner, j), r_y.at[owner, j])
            arrived(y_ref(across, j), r_y.at[across, j])

    @pl.when(r > c)
    def _():
        for p in range(8):
            arrived(swaps.at[1, p], r_l.at[1, p])

    @pl.when(c != 0)
    def _():
        arrived(kin.at[1], r_k.at[1])
        w0_copy(c).wait_send()

    corner[...] = kin[1]
    keep.wait()

    @pl.when(r == 0)
    def _():
        for p in range(1, 8):
            lead_copy(p).wait_send()

    @pl.when(core == 0)
    def _():
        lead_sib.wait_send()

    a_sib.wait_send()
    for d in range(1, 8):
        a_copy(d).wait_send()

    @pl.when(c == 0)
    def _():
        k_copies(0, sent)
        k_copies(1, sent)

    t_copies(sent, lambda copy: None)
    b_copies(sent)
    l_copies(sent, lambda j: None)
    for j in range(4):
        y_copies(j, sent)
        z_copies(j, sent)

    @pl.when(sib >= c)
    def _():
        for d in range(8):
            f_copy(d).wait_send()


def compact_exchange(matrix, piv_col, piv_row):
    rows, cols = matrix.shape
    width = piv_col.shape[0]
    half, part = width // 2, cols // 8
    dma = pltpu.SemaphoreType.DMA
    any_spec = pl.BlockSpec(memory_space=pl.ANY)
    vmem = pl.BlockSpec(memory_space=pltpu.VMEM)
    panel = jax.ShapeDtypeStruct((8, width, part), F32)
    return pl.pallas_call(
        compact_kernel,
        out_shape=(
            panel,
            panel,
            jax.ShapeDtypeStruct((2, 8, CAP, part), F32),
            jax.ShapeDtypeStruct((CAP, 128), F32),
        ),
        in_specs=[any_spec, vmem, vmem],
        out_specs=(any_spec, any_spec, vmem, vmem),
        scratch_shapes=[
            pltpu.VMEM((rows, cols), F32),
            pltpu.VMEM((CAP, cols), F32),
            pltpu.VMEM((CAP, cols), F32),
            pltpu.VMEM((16 * CAP, width), F32),
            pltpu.VMEM((2, 8, CAP, part), F32),
            pltpu.VMEM((width, part), F32),
            pltpu.VMEM((half, part), F32),
            pltpu.VMEM((2, 4, CAP, 128), F32),
            pltpu.VMEM((2, CAP, 128), F32),
            pltpu.VMEM((CAP, 128), F32),
            pltpu.VMEM((16, CAP, 128), F32),
            pltpu.VMEM((8, CAP, part), F32),
            dma((8,)), dma((8,)), dma((2,)), dma((2,)), dma((8,)), dma((1,)),
            dma((2, 16)), dma((2,)), dma((1,)), dma((16,)), dma((8,)), dma((2, 8)),
            dma((8,)), dma((2, 8)), dma((8,)), dma((4,)), dma((4,)), dma((2, 4)), dma((4,)), dma((4, 4)),
            dma((3,)),
        ],
        compiler_params=pltpu.CompilerParams(
            collective_id=1, has_side_effects=True, vmem_limit_bytes=32 * 1024 * 1024
        ),
        name="compact_exchange",
    )(matrix, piv_col, piv_row)


def compact_update_kernel(
    piv_col, piv_row, m, qc, qr, swaps, corner, coupling, out, panel, right, left
):
    r, c = lax.axis_index("row"), lax.axis_index("col")
    tile, cols = out.shape
    rows = tile * pl.num_programs(0)
    width = coupling.shape[0]
    part = qc.shape[2]
    step = pl.program_id(0)
    row_start = r * rows + step * tile
    col_start = c * cols

    def dot(a, b):
        return lax.dot_general(a, b, (((0,), (0,)), ((), ())), preferred_element_type=F32)

    @pl.when(r < c)
    def _():
        out[...] = jnp.zeros_like(out)

    @pl.when((r >= c) & (step == 0))
    def _():
        _, place_row = places(piv_col[...], piv_row[...], rows)
        for i in range(8):
            for j, term in enumerate(split(qc[i], 2)):
                panel[j, :, i * part : (i + 1) * part] = term
        here_piv = listed(place_row, piv_row[...], lax.div(order(c), 4) * 128, 128)
        spread = one_hot(here_piv, col_start, (128, cols), 1).astype(F32)
        swapped = jnp.max(spread, axis=0, keepdims=True) > 0
        lead = jnp.concatenate([swaps[0, i] for i in range(8)], axis=1)
        placed = jnp.dot(corner[...], spread, precision=HIGHEST, preferred_element_type=F32)
        lead = jnp.where(swapped, placed, lead)
        for j, term in enumerate(split(lead, 3)):
            right[j * CAP : (j + 1) * CAP] = term
        col_piv = listed(place_row, piv_row[...], order(c) * CAP, CAP)
        hot = one_hot(col_piv, col_start, (CAP, cols), 1).astype(F32).astype(BF16)
        for j in range(3):
            right[(3 + j) * CAP : (4 + j) * CAP] = hot
        left[...] = listed(place_row, piv_row[...], order(r) * CAP, CAP)

    @pl.when(r >= c)
    def _():
        rows_t = jnp.concatenate([qr[0], qr[1]], axis=1)
        scaled = lax.dot_general(
            coupling[...], rows_t, (((0,), (0,)), ((), ())),
            precision=HIGHEST, preferred_element_type=F32,
        )
        s_hi, s_lo = split(scaled, 2)
        change = dot(s_hi, panel[0]) + dot(s_hi, panel[1]) + dot(s_lo, panel[0])
        hot = one_hot(left[...], row_start, (CAP, tile), 1).astype(F32)
        hit = jnp.max(hot, axis=0, keepdims=True)
        which = jnp.where(r == c, 0, 1)
        lead = jnp.concatenate([swaps[which, 2 * step + i] for i in range(2)], axis=1)
        lead = jnp.where(hit > 0, 0.0, lead)
        hot = hot.astype(BF16)
        lhs = jnp.concatenate([hot, hot, hot] + split(lead, 3), axis=0)
        moved = dot(lhs, right[...])
        hit_row = jnp.broadcast_to(hit, (8, tile)).T[:, :1] > 0
        hit_col = jnp.max(right[3 * CAP : 4 * CAP].astype(F32), axis=0, keepdims=True) > 0
        value = jnp.where(hit_row | hit_col, 0.0, m[...]) + moved
        places_col = lax.broadcasted_iota(jnp.int32, (tile, cols), 1) + col_start
        below = lax.broadcasted_iota(jnp.int32, (tile, cols), 0) + row_start >= places_col
        out[...] = jnp.where(below, value - change, 0.0)

        @pl.when(c == 0)
        def _():
            out[:, :width] = jnp.where(
                below[:, :width], rows_t.T - change[:, :width], 0.0
            )


def compact_update(piv_col, piv_row, matrix, qc, qr, swaps, corner, coupling):
    rows, cols = matrix.shape
    width = coupling.shape[0]
    part = cols // 8
    tile = 2 * part

    def whole(shape):
        return pl.BlockSpec(shape, lambda i: (0,) * len(shape))

    return pl.pallas_call(
        compact_update_kernel,
        grid=(rows // tile,),
        out_shape=jax.ShapeDtypeStruct((rows, cols), F32),
        in_specs=[
            whole((width, 1)),
            whole((1, width)),
            pl.BlockSpec((tile, cols), lambda i: (i, 0)),
            whole((8, width, part)),
            pl.BlockSpec((2, width, part), lambda i: (i, 0, 0)),
            whole((2, 8, CAP, part)),
            whole((CAP, 128)),
            whole((width, width)),
        ],
        out_specs=pl.BlockSpec((tile, cols), lambda i: (i, 0)),
        scratch_shapes=[
            pltpu.VMEM((2, width, cols), BF16),
            pltpu.VMEM((6 * CAP, cols), BF16),
            pltpu.VMEM((CAP, 1), jnp.int32),
        ],
        compiler_params=pltpu.CompilerParams(vmem_limit_bytes=48 * 1024 * 1024),
        name="compact_update",
    )(piv_col, piv_row, matrix, qc, qr, swaps, corner, coupling)


def per_device(matrix, pivots, coupling):
    width = coupling.shape[0]
    rows = matrix.shape[0]
    piv_col, piv_row = pivots.reshape(width, 1), pivots.reshape(1, width)

    def compact(matrix, pivots, coupling):
        parts = compact_exchange(matrix, piv_col, piv_row)
        return compact_update(piv_col, piv_row, matrix, *parts, coupling)

    def general(matrix, pivots, coupling):
        picked = pick(matrix, pivots)
        qc, qr = exchange(picked, matrix, piv_col, piv_row)
        return update(piv_col, piv_row, matrix, qc, qr, coupling)

    blocks = jnp.arange(16, dtype=jnp.int32)[:, None]
    counts = jnp.sum((piv_row // rows == blocks).astype(jnp.int32), axis=1)
    return lax.cond(jnp.max(counts) <= CAP, compact, general, matrix, pivots, coupling)


def solution(mesh):
    return jax.shard_map(
        per_device,
        mesh=mesh,
        in_specs=(P("row", "col"), P(), P()),
        out_specs=P("row", "col"),
        check_vma=False,
    )
```

```python
import functools

import jax
import jax.numpy as jnp
from jax import lax
from jax.experimental import pallas as pl
from jax.experimental.pallas import tpu as pltpu
from jax.sharding import PartitionSpec as P

MESH = pl.DeviceIdType.MESH
F32 = jnp.float32
BF16 = jnp.bfloat16
HIGHEST = lax.Precision.HIGHEST
CAP = 32


def one_hot(index, start, shape, axis):
    return lax.broadcasted_iota(jnp.int32, shape, axis) + start == index


def pick_kernel(piv, matrix, picked, sem):
    rows = matrix.shape[0]
    count = picked.shape[0]
    start = lax.axis_index("row") * rows
    picked[...] = jnp.zeros_like(picked)

    def copy(k):
        local = jnp.clip(piv[k] - start, 0, rows - 1)
        return pltpu.make_async_copy(matrix.at[pl.ds(local, 1)], picked.at[pl.ds(k, 1)], sem)

    def go(k, _):
        @pl.when((piv[k] >= start) & (piv[k] < start + rows))
        def _():
            copy(k).start()

        return 0

    def wait(k, _):
        @pl.when((piv[k] >= start) & (piv[k] < start + rows))
        def _():
            copy(k).wait()

        return 0

    lax.fori_loop(0, count, go, 0)
    lax.fori_loop(0, count, wait, 0)


def pick(matrix, pivots):
    return pl.pallas_call(
        pick_kernel,
        out_shape=jax.ShapeDtypeStruct((pivots.shape[0], matrix.shape[1]), F32),
        in_specs=[pl.BlockSpec(memory_space=pltpu.SMEM), pl.BlockSpec(memory_space=pl.ANY)],
        out_specs=pl.BlockSpec(memory_space=pltpu.VMEM),
        scratch_shapes=[pltpu.SemaphoreType.DMA],
        name="pick",
    )(pivots, matrix)


def exchange_kernel(
    picked, matrix, piv_col, piv_row, qc, qr,
    a1buf, sums, a2buf, raw, piece, corner, w0buf, w0mine,
    s_a1, r_a1, s_a2, r_a2, s_ld, r_ld, s_w, r_w, s_w0, r_w0,
    s_b, r_b, s_f, s_t, r_t, s_y, r_y, local,
):
    r, c = lax.axis_index("row"), lax.axis_index("col")
    width, cols = picked.shape
    own = raw.shape[1]
    q, core = lax.div(r, 2), lax.rem(r, 2)
    x, y, zh = lax.div(r, 4), lax.div(c, 4), lax.rem(c, 4)
    sib = r + 1 - 2 * core
    col_start = c * cols

    def remote(src, dst, ssem, rsem, row, col):
        return pltpu.make_async_remote_copy(
            src_ref=src, dst_ref=dst, send_sem=ssem, recv_sem=rsem,
            device_id=(row, col), device_id_type=MESH,
        )

    def arrived(dst, rsem):
        remote(dst, dst, rsem, rsem, sib, c).wait_recv()

    def signal(row, col):
        pl.semaphore_signal(barrier, inc=1, device_id=(row, col), device_id_type=MESH)

    def slots(g, n=1):
        return pl.ds(pl.multiple_of(g * own, own), n * own)

    barrier = pltpu.get_barrier_semaphore()
    for d in range(1, 16):
        signal(lax.rem(r + d, 16), c)
    for d in range(1, 4):
        signal(r, lax.rem(y + d, 4) * 4 + zh)
    for j in range(4):
        @pl.when((r != c) | (4 * y + j != r))
        def _():
            signal(4 * y + j, r)

    @pl.when(c != 0)
    def _():
        signal(r, 0)

    @pl.when(c == 0)
    def _():
        for b in range(1, 16):
            signal(r, b)

    greeted = 15 + 3 + 4 - jnp.where(r == c, 1, 0) + jnp.where(c == 0, 15, 1)
    pl.semaphore_wait(barrier, greeted)

    def lead_copies(act):
        @pl.when(r == 0)
        def _():
            for g in range(1, 16):
                act(remote(matrix.at[slots(g)], raw.at[1], s_ld.at[g], r_ld.at[0], g, c))
            act(pltpu.make_async_copy(matrix.at[slots(0)], raw.at[1], local.at[0]))

    lead_copies(lambda copy: copy.start())

    def a1(p):
        return remote(
            picked.at[slots(2 * p + 1 - core)], a1buf.at[p], s_a1.at[p], r_a1.at[p], sib, c
        )

    def a2(p):
        return remote(sums.at[p], a2buf.at[q], s_a2.at[p], r_a2.at[q], 2 * p + core, c)

    for d in range(1, 9):
        a1(lax.rem(q + d, 8)).start()
    for d in range(1, 9):
        p = lax.rem(q + d, 8)
        arrived(a1buf.at[p], r_a1.at[p])
        total = picked[slots(2 * p + core)] + a1buf[p]
        if d < 8:
            sums[p] = total
            a2(p).start()
        else:
            a2buf[q] = total

    hot_t = one_hot(piv_col[...], col_start, (width, cols), 1).astype(F32)
    swapped = jnp.max(hot_t, axis=0, keepdims=True) > 0

    def fixed(part):
        placed = jnp.dot(corner[part], hot_t, precision=HIGHEST, preferred_element_type=F32)
        return jnp.where(swapped, placed, raw[part])

    def send_corner(part, act):
        for b in range(1, 16):
            act(remote(corner.at[part], corner.at[part], s_w.at[part, b], r_w.at[part], r, b))

    def get_corner(part):
        @pl.when(c == 0)
        def _():
            corner[part] = raw[part, :, :width]
            send_corner(part, lambda copy: copy.start())

        @pl.when(c != 0)
        def _():
            arrived(corner.at[part], r_w.at[part])

    def b_copy(part, d):
        p = lax.rem(q + d, 8)
        return p, remote(
            piece.at[part], qc.at[part, slots(r)], s_b.at[part, d], r_b.at[part, r], 2 * p + core, c
        )

    def b_copies(part, act):
        for d in range(1, 8):
            p, copy = b_copy(part, d)

            @pl.when(2 * p + 1 >= c)
            def _():
                act(copy)

    def f_copy(part, d):
        if d == 0:
            return remote(
                piece.at[part], qc.at[part, slots(r)], s_f.at[part, 0], r_b.at[part, r], sib, c
            )
        g = 2 * lax.rem(q + d, 8) + core
        return remote(
            qc.at[part, slots(g)], qc.at[part, slots(g)], s_f.at[part, d], r_b.at[part, g], sib, c
        )

    def t_copies(part, act):
        for k in range(4):
            col = 4 * x + k
            here = (r == c) & (k == zh)

            @pl.when(jnp.logical_not(here))
            def _():
                act(
                    remote(
                        piece.at[part], qr.at[part, slots(r)],
                        s_t.at[part, k], r_t.at[part, lax.rem(r, 4)], c, col,
                    )
                )

            @pl.when(here)
            def _():
                act(
                    pltpu.make_async_copy(
                        piece.at[part], qr.at[part, slots(r)], local.at[3 + part]
                    )
                )

    def send_piece(part):
        b_copies(part, lambda copy: copy.start())
        t_copies(part, lambda copy: copy.start())

        @pl.when(sib >= c)
        def _():
            f_copy(part, 0).start()

        pltpu.make_async_copy(piece.at[part], qc.at[part, slots(r)], local.at[1 + part]).start()

    @pl.when(r == 0)
    def _():
        pltpu.make_async_copy(matrix.at[slots(0)], raw.at[1], local.at[0]).wait()

    @pl.when(r != 0)
    def _():
        arrived(raw.at[1], r_ld.at[0])

    get_corner(1)
    piece[1] = fixed(1)
    send_piece(1)

    for d in range(1, 8):
        p = lax.rem(q + d, 8)
        arrived(a2buf.at[p], r_a2.at[p])
    total = a2buf[0]
    for p in range(1, 8):
        total = total + a2buf[p]
    raw[0] = total
    get_corner(0)
    hot = one_hot(piv_row[...], col_start, (cols, width), 0).astype(F32)
    mine = jnp.dot(total, hot, precision=HIGHEST, preferred_element_type=F32)

    def w0_copy(col):
        return remote(w0mine, w0buf.at[col], s_w0.at[0], r_w0.at[col], r, 0)

    @pl.when(c != 0)
    def _():
        w0mine[...] = mine
        w0_copy(c).start()

    piece[0] = fixed(0)

    @pl.when(c == 0)
    def _():
        w0 = mine
        for b in range(1, 16):
            arrived(w0buf.at[b], r_w0.at[b])
            w0 = w0 + w0buf[b]
        piece[0, :, :width] = w0

    send_piece(0)

    def y_copies(part, act):
        for d in range(1, 4):
            col = lax.rem(y + d, 4) * 4 + zh

            @pl.when(col <= r)
            def _():
                block = qr.at[part, slots(4 * y, 4)]
                act(remote(block, block, s_y.at[part, d], r_y.at[part, y], r, col))

    def run_y(part):
        for j in range(4):
            here = (r == c) & (4 * y + j == r)

            @pl.when(jnp.logical_not(here))
            def _():
                arrived(qr.at[part, slots(4 * y + j)], r_t.at[part, j])

            @pl.when(here)
            def _():
                pltpu.make_async_copy(
                    piece.at[part], qr.at[part, slots(r)], local.at[3 + part]
                ).wait()

        y_copies(part, lambda copy: copy.start())

    def run_f(part):
        for d in range(1, 8):
            g = 2 * lax.rem(q + d, 8) + core

            @pl.when(2 * q + 1 >= c)
            def _():
                arrived(qc.at[part, slots(g)], r_b.at[part, g])

            @pl.when(sib >= c)
            def _():
                f_copy(part, d).start()

    run_y(1)
    run_y(0)
    run_f(1)
    run_f(0)

    for part in (1, 0):
        for d in range(8):
            g = 2 * lax.rem(q + d, 8) + 1 - core

            @pl.when(r >= c)
            def _():
                arrived(qc.at[part, slots(g)], r_b.at[part, g])

        for d in range(1, 4):
            there = lax.rem(y + d, 4)

            @pl.when(c <= r)
            def _():
                arrived(qr.at[part, slots(4 * there, 4)], r_y.at[part, there])

        pltpu.make_async_copy(piece.at[part], qc.at[part, slots(r)], local.at[1 + part]).wait()

    lead_copies(lambda copy: copy.wait_send() if copy.is_remote else None)
    for d in range(1, 9):
        a1(lax.rem(q + d, 8)).wait_send()
    for d in range(1, 8):
        a2(lax.rem(q + d, 8)).wait_send()

    @pl.when(c != 0)
    def _():
        w0_copy(c).wait_send()

    for part in (1, 0):
        @pl.when(c == 0)
        def _():
            send_corner(part, lambda copy: copy.wait_send())

        b_copies(part, lambda copy: copy.wait_send())
        t_copies(part, lambda copy: copy.wait_send() if copy.is_remote else None)
        y_copies(part, lambda copy: copy.wait_send())

        @pl.when(sib >= c)
        def _():
            for d in range(8):
                f_copy(part, d).wait_send()


def exchange(picked, matrix, piv_col, piv_row):
    width, cols = picked.shape
    own = width // 16
    dma = pltpu.SemaphoreType.DMA
    out = jax.ShapeDtypeStruct((2, width, cols), F32)
    any_spec = pl.BlockSpec(memory_space=pl.ANY)
    vmem = pl.BlockSpec(memory_space=pltpu.VMEM)
    return pl.pallas_call(
        exchange_kernel,
        out_shape=(out, out),
        in_specs=[vmem, any_spec, vmem, vmem],
        out_specs=(any_spec, any_spec),
        scratch_shapes=[
            pltpu.VMEM((8, own, cols), F32),
            pltpu.VMEM((8, own, cols), F32),
            pltpu.VMEM((8, own, cols), F32),
            pltpu.VMEM((2, own, cols), F32),
            pltpu.VMEM((2, own, cols), F32),
            pltpu.VMEM((2, own, width), F32),
            pltpu.VMEM((16, own, width), F32),
            pltpu.VMEM((own, width), F32),
            dma((8,)), dma((8,)), dma((8,)), dma((8,)),
            dma((16,)), dma((1,)), dma((2, 16)), dma((2,)), dma((1,)), dma((16,)),
            dma((2, 8)), dma((2, 16)), dma((2, 8)), dma((2, 4)), dma((2, 4)), dma((2, 4)), dma((2, 4)),
            dma((5,)),
        ],
        compiler_params=pltpu.CompilerParams(
            collective_id=0, has_side_effects=True, vmem_limit_bytes=32 * 1024 * 1024
        ),
        name="exchange",
    )(picked, matrix, piv_col, piv_row)


def split(value, n):
    terms = []
    for _ in range(n):
        term = value.astype(BF16)
        terms.append(term)
        value = value - term.astype(F32)
    return terms


def update_kernel(piv_col, piv_row, m, qc, qr, coupling, out, hot_t, panel, lead):
    r, c = lax.axis_index("row"), lax.axis_index("col")
    tile, cols = out.shape
    width = coupling.shape[0]
    step = pl.program_id(0)
    row_start = r * cols + step * tile
    col_start = c * cols

    @pl.when(r < c)
    def _():
        out[...] = jnp.zeros_like(out)

    @pl.when((r >= c) & (step == 0))
    def _():
        hot_t[...] = one_hot(piv_col[...], col_start, (width, cols), 1).astype(BF16)
        for i, term in enumerate(split(qc[0], 2)):
            panel[i] = term
        for i, term in enumerate(split(qc[1], 3)):
            lead[i] = term

    def dot(a, b):
        return jnp.dot(a, b, preferred_element_type=F32)

    @pl.when(r >= c)
    def _():
        panel_rows = qr[0].T
        scaled = jnp.dot(panel_rows, coupling[...], precision=HIGHEST, preferred_element_type=F32)
        s_hi, s_lo = split(scaled, 2)
        update = dot(s_hi, panel[0]) + dot(s_hi, panel[1]) + dot(s_lo, panel[0])
        hot = one_hot(piv_row[...], row_start, (tile, width), 0)
        hit_row = jnp.max(hot.astype(F32), axis=1, keepdims=True) > 0
        hit_col = jnp.max(hot_t[...].astype(F32), axis=0, keepdims=True) > 0
        hot = hot.astype(F32).astype(BF16)
        new_rows = dot(hot, lead[0]) + dot(hot, lead[1]) + dot(hot, lead[2])
        lead_cols = jnp.where(hit_row, 0.0, qr[1].T)
        new_cols = sum(dot(term, hot_t[...]) for term in split(lead_cols, 3))
        value = jnp.where(hit_row | hit_col, 0.0, m[...]) + new_rows + new_cols
        spread = jnp.concatenate([panel_rows, jnp.zeros((tile, cols - width), F32)], axis=1)
        places = lax.broadcasted_iota(jnp.int32, (tile, cols), 1)
        value = jnp.where((places < width) & (c == 0), spread, value)
        below = lax.broadcasted_iota(jnp.int32, (tile, cols), 0) + row_start >= places + col_start
        out[...] = jnp.where(below, value - update, 0.0)


def update(piv_col, piv_row, matrix, qc, qr, coupling):
    rows, cols = matrix.shape
    width = coupling.shape[0]
    tile = min(rows, 256)

    def whole(shape):
        return pl.BlockSpec(shape, lambda i: (0,) * len(shape))

    return pl.pallas_call(
        update_kernel,
        grid=(rows // tile,),
        out_shape=jax.ShapeDtypeStruct((rows, cols), F32),
        in_specs=[
            whole((width, 1)),
            whole((1, width)),
            pl.BlockSpec((tile, cols), lambda i: (i, 0)),
            whole((2, width, cols)),
            pl.BlockSpec((2, width, tile), lambda i: (0, 0, i)),
            whole((width, width)),
        ],
        out_specs=pl.BlockSpec((tile, cols), lambda i: (i, 0)),
        scratch_shapes=[
            pltpu.VMEM((width, cols), BF16),
            pltpu.VMEM((2, width, cols), BF16),
            pltpu.VMEM((3, width, cols), BF16),
        ],
        compiler_params=pltpu.CompilerParams(vmem_limit_bytes=48 * 1024 * 1024),
        name="update",
    )(piv_col, piv_row, matrix, qc, qr, coupling)


def order(s):
    return lax.rem(s, 2) * 8 + lax.div(s, 2)


def blocks_of(piv, rows):
    block = jnp.right_shift(piv, rows.bit_length() - 1)
    return jnp.bitwise_and(block, 1) * 8 + jnp.right_shift(block, 1)


def column(row):
    return jnp.broadcast_to(row, (8, row.shape[1])).T[:, :1]


def places(piv_row, rows):
    width = piv_row.shape[1]
    first = lax.broadcasted_iota(jnp.int32, (width, width), 0)
    second = lax.broadcasted_iota(jnp.int32, (width, width), 1)
    block_row = blocks_of(piv_row, rows)
    before = (column(block_row) == block_row) & (first < second)
    return block_row * CAP + jnp.sum(jnp.where(before, 1, 0), axis=0, keepdims=True)


def listed(place_row, piv_row, start, count):
    spot = lax.broadcasted_iota(jnp.int32, (count, place_row.shape[1]), 0) + start
    return jnp.sum(jnp.where(spot == place_row, piv_row + 1, 0), axis=1, keepdims=True) - 1


def compact_kernel(
    matrix, piv_row, qc, qr, swaps, corner, w1,
    block, picked, hall, abuf, lead, piece, wbuf, w0out, w0in, lout,
    s_a, r_a, s_sib, r_sib, s_ld, r_ld, s_k, r_k, s_w0, r_w0, s_w, r_w, s_l, r_l,
    s_b, s_x, r_b, s_f, s_t, r_t, s_z, r_z, s_y, s_r, r_y, local,
):
    r, c = lax.axis_index("row"), lax.axis_index("col")
    rows, cols = matrix.shape
    width = piv_row.shape[1]
    half, part = width // 2, cols // 8
    q, core = lax.div(r, 2), lax.rem(r, 2)
    zl = lax.rem(q, 2)
    y, zh = lax.div(c, 4), lax.rem(c, 4)
    sib = r + 1 - 2 * core
    pair = q + 1 - 2 * zl
    chunk = lax.div(order(c), 4)

    def remote(src, dst, ssem, rsem, row, col):
        return pltpu.make_async_remote_copy(
            src_ref=src, dst_ref=dst, send_sem=ssem, recv_sem=rsem,
            device_id=(row, col), device_id_type=MESH,
        )

    def arrived(dst, rsem):
        remote(dst, dst, rsem, rsem, sib, c).wait_recv()

    def start(copy):
        copy.start()

    def sent(copy):
        copy.wait_send()

    def dot(a, b, dims=((1,), (0,))):
        return lax.dot_general(
            a, b, (dims, ((), ())), precision=HIGHEST, preferred_element_type=F32
        )

    load = pltpu.make_async_copy(matrix, block, local.at[0])
    load.start()

    barrier = pltpu.get_barrier_semaphore()

    def signal(row, col):
        pl.semaphore_signal(barrier, inc=1, device_id=(row, col), device_id_type=MESH)

    for d in range(1, 16):
        signal(lax.rem(r + d, 16), c)
    for d in (1, 3):
        signal(r, lax.rem(y + d, 4) * 4 + zh)
    for d in (1, 2, 3):
        signal(r, 4 * y + lax.rem(zh + d, 4))

    @pl.when(r != c)
    def _():
        signal(c, r)

    @pl.when(c != 0)
    def _():
        signal(r, 0)

    @pl.when(c == 0)
    def _():
        for b in range(1, 16):
            signal(r, b)

    @pl.when(r > c)
    def _():
        for j in range(8):
            signal(2 * j + lax.rem(c, 2), r)

    greeted = 15 + 2 + 3 + jnp.where(r == c, 0, 1) + jnp.where(c == 0, 15, 1)
    greeted = greeted + lax.div(c - core + 1, 2)

    place_row = places(piv_row[...], rows)
    spots = lax.broadcasted_iota(jnp.int32, (16 * CAP, width), 0)
    hall[...] = (spots == place_row).astype(F32)
    mine = order(r) * CAP
    have = listed(place_row, piv_row[...], mine, CAP) >= 0
    here_piv = listed(place_row, piv_row[...], chunk * 128, 128)
    load.wait()
    for t in range(CAP):
        local_row = jnp.sum(jnp.where(place_row == mine + t, piv_row[...] - r * rows, 0))
        picked[pl.ds(t, 1)] = block[pl.ds(jnp.clip(local_row, 0, rows - 1), 1)]
    picked[...] = jnp.where(have, picked[...], 0.0)

    @pl.when(c == 0)
    def _():
        wbuf[core, q] = picked[:, :width]

    pl.semaphore_wait(barrier, greeted)

    def a_copy(d):
        p = lax.rem(q + d, 8)
        cut = pl.ds(pl.multiple_of(p * part, part), part)
        return p, remote(picked.at[:, cut], abuf.at[core, q], s_a.at[d], r_a.at[q], 2 * p + core, c)

    for d in range(1, 8):
        p, copy = a_copy(d)

        @pl.when((c != 0) | (p >= width // part))
        def _():
            copy.start()

    def k_copy(i, b):
        src = wbuf.at[core, q] if i == 0 else corner
        return remote(src, src, s_k.at[i, b], r_k.at[i], r, b)

    def k_copies(i, act):
        for b in range(1, 16):
            act(k_copy(i, b))

    @pl.when(c == 0)
    def _():
        k_copies(0, start)

    def w0_copy(b):
        return remote(w0out, w0in.at[b], s_w0.at[0], r_w0.at[b], r, 0)

    spread = one_hot(here_piv, c * cols, (128, cols), 1).astype(F32)
    w0out[...] = dot(picked[...], spread, ((1,), (1,)))

    @pl.when(c != 0)
    def _():
        w0_copy(c).start()

    @pl.when(c == 0)
    def _():
        for b in range(1, 16):
            arrived(w0in.at[b], r_w0.at[b])
        w0in[0] = w0out[...]
        total = jnp.zeros((CAP, width), F32)
        for j in range(4):
            listing = sum(
                w0in[b] for b in range(16) if ((b % 2) * 8 + b // 2) // 4 == j
            )
            total = total + dot(listing, hall[128 * j : 128 * (j + 1)])
        picked[:, :width] = total
        for d in range(1, 8):
            p, copy = a_copy(d)

            @pl.when(p < width // part)
            def _():
                copy.start()

    abuf[core, q] = picked[:, pl.ds(pl.multiple_of(q * part, part), part)]

    def lead_copy(p):
        return remote(
            block.at[pl.ds(0, width), pl.ds(p * part, part)], lead, s_ld.at[p], r_ld.at[0], 2 * p, c
        )

    @pl.when(r == 0)
    def _():
        for p in range(1, 8):
            lead_copy(p).start()

    for d in range(1, 8):
        p = lax.rem(q + d, 8)
        arrived(abuf.at[core, p], r_a.at[p])
    a_sib = remote(abuf.at[core], abuf.at[core], s_sib.at[1], r_sib.at[1], sib, c)
    a_sib.start()
    arrived(abuf.at[1 - core], r_sib.at[1])

    lay = jnp.where(core == 0, hall[:, :half], hall[:, half:])
    piece[...] = dot(lay, abuf[...].reshape(16 * CAP, part), ((0,), (0,)))

    def slot(k):
        return pl.ds(pl.multiple_of(k * half, half), half)

    t_copy = remote(piece, qr.at[q, slot(core)], s_t.at[0], r_t.at[0], c, r)
    t_here = pltpu.make_async_copy(piece, qr.at[q, slot(core)], local.at[1])

    @pl.when(r != c)
    def _():
        t_copy.start()

    @pl.when(r == c)
    def _():
        t_here.start()

    def wanted(p):
        return 2 * p + 1 >= c

    def b_copies(act):
        @pl.when(wanted(6 + 1 - zl))
        def _():
            act(
                remote(piece, qc.at[q, slot(core)], s_b.at[0], r_b.at[core, q], 2 * pair + core, c)
            )

        for d in range(1, 4):
            p = lax.rem(q + 2 * d, 8)

            @pl.when(wanted(p))
            def _():
                act(remote(piece, qc.at[q, slot(core)], s_b.at[d], r_b.at[core, q], 2 * p + core, c))

    def x_copies(act):
        for d in range(1, 4):
            p = lax.rem(q + 2 * d, 8)
            ref = qc.at[pair, slot(core)]

            @pl.when(wanted(p))
            def _():
                act(remote(ref, ref, s_x.at[d], r_b.at[core, pair], 2 * p + core, c))

    def f_copy(d):
        p = lax.rem(q + d, 8)
        src = piece if d == 0 else qc.at[p, slot(core)]
        return remote(src, qc.at[p, slot(core)], s_f.at[d], r_b.at[core, p], sib, c)

    b_copies(start)

    @pl.when(sib >= c)
    def _():
        f_copy(0).start()

    keep = pltpu.make_async_copy(piece, qc.at[q, slot(core)], local.at[2])
    keep.start()

    def w_copies(act):
        for d in range(1, 8):
            p = lax.rem(q + d, 8)

            @pl.when(wanted(p))
            def _():
                act(
                    remote(
                        wbuf.at[core, q], wbuf.at[core, q], s_w.at[d], r_w.at[q], 2 * p + core, c
                    )
                )

    @pl.when(c != 0)
    def _():
        arrived(wbuf.at[core, q], r_k.at[0])

    w_copies(start)

    lead_sib = remote(lead, lead, s_sib.at[0], r_sib.at[0], sib, c)

    @pl.when(r == 0)
    def _():
        lead[...] = block[:width, :part]

    @pl.when((core == 0) & (r != 0))
    def _():
        arrived(lead, r_ld.at[0])

    @pl.when(core == 0)
    def _():
        lead_sib.start()

    def need(there):
        return 4 * there + zh <= r

    up, down, across = lax.rem(y + 1, 4), lax.rem(y + 3, 4), lax.rem(y + 2, 4)

    def y_ref(owner, k):
        j = lax.rem(zh + k, 4)
        return qr.at[2 * owner + lax.div(j, 2), slot(lax.rem(j, 2))]

    def z_copies(act):
        for d in (1, 3, 2):
            there = lax.rem(zh + d, 4)

            @pl.when(there <= r)
            def _():
                act(
                    remote(
                        y_ref(y, 0), y_ref(y, 0), s_z.at[d], r_z.at[(4 - d) % 4], r, 4 * y + there
                    )
                )

    def y_copies(k, act):
        onward = need(across)

        def one(way, to):
            ref = y_ref(y, k)
            act(remote(ref, ref, s_y.at[way, k], r_y.at[y, k], r, 4 * to + zh))

        @pl.when(need(up) | onward if k % 2 == 0 else need(up))
        def _():
            one(0, up)

        @pl.when(need(down) | onward if k % 2 == 1 else need(down))
        def _():
            one(1, down)

    def relay(k, act):
        owner, to = (down, up) if k % 2 == 0 else (up, down)
        ref = y_ref(owner, k)

        @pl.when(need(to))
        def _():
            act(remote(ref, ref, s_r.at[k], r_y.at[owner, k], r, 4 * to + zh))

    def run_relay(k):
        owner, to = (down, up) if k % 2 == 0 else (up, down)

        @pl.when(need(y) | need(to))
        def _():
            arrived(y_ref(owner, k), r_y.at[owner, k])

        relay(k, start)

    @pl.when(r != c)
    def _():
        arrived(y_ref(y, 0), r_t.at[0])

    @pl.when(r == c)
    def _():
        t_here.wait()

    y_copies(0, start)
    z_copies(start)

    @pl.when(core == 1)
    def _():
        arrived(lead, r_sib.at[0])

    lists = hall[pl.ds(pl.multiple_of(core * 8 * CAP, 8 * CAP), 8 * CAP)]
    lout[...] = dot(lists, lead[...]).reshape(8, CAP, part)

    def l_copies(act, act_here):
        for j in range(8):
            s = 2 * j + core
            as_row = s >= c
            row, col = jnp.where(as_row, s, c), jnp.where(as_row, c, s)
            kind = jnp.where(as_row, 0, 1)
            here = as_row & (s == r)

            @pl.when(jnp.logical_not(here))
            def _():
                act(remote(lout.at[j], swaps.at[kind, q], s_l.at[j], r_l.at[kind, q], row, col))

            @pl.when(here)
            def _():
                act_here(j)

    def keep_lead(j):
        swaps[0, q] = lout[j]

    l_copies(start, keep_lead)

    def run_y(k):
        @pl.when(zh <= r)
        def _():
            arrived(y_ref(y, k), r_z.at[k])

        y_copies(k, start)

    run_relay(0)
    run_y(1)
    run_y(3)
    run_relay(1)
    run_relay(3)
    run_y(2)

    @pl.when(wanted(6 + zl))
    def _():
        arrived(qc.at[pair, slot(core)], r_b.at[core, pair])

    x_copies(start)
    run_relay(2)

    @pl.when(r >= c)
    def _():
        for p in range(8):
            @pl.when(p != q)
            def _():
                arrived(swaps.at[0, p], r_l.at[0, p])

    @pl.when(c == 0)
    def _():
        for p in range(width // part):
            corner[:, p * part : (p + 1) * part] = swaps[0, p]
        k_copies(1, start)

    @pl.when(wanted(q))
    def _():
        for d in range(1, 8):
            p = lax.rem(q + d, 8)
            arrived(wbuf.at[core, p], r_w.at[p])

    w_sib = remote(wbuf.at[core], wbuf.at[core], s_sib.at[2], r_sib.at[2], sib, c)

    @pl.when(sib >= c)
    def _():
        w_sib.start()

    for d in range(1, 8):
        p = lax.rem(q + d, 8)

        @pl.when(wanted(q) & (p != pair))
        def _():
            arrived(qc.at[p, slot(core)], r_b.at[core, p])

        @pl.when(sib >= c)
        def _():
            f_copy(d).start()

    @pl.when(r >= c)
    def _():
        arrived(wbuf.at[1 - core], r_sib.at[2])
        w1[...] = dot(hall[...], wbuf[...].reshape(16 * CAP, width), ((0,), (0,)))

    @pl.when(r >= c)
    def _():
        for p in range(8):
            arrived(qc.at[p, slot(1 - core)], r_b.at[1 - core, p])
        for k in range(4):
            owner = up if k % 2 == 0 else down
            arrived(y_ref(owner, k), r_y.at[owner, k])
            arrived(y_ref(across, k), r_y.at[across, k])

    @pl.when(r > c)
    def _():
        for p in range(8):
            arrived(swaps.at[1, p], r_l.at[1, p])

    @pl.when(c != 0)
    def _():
        arrived(corner, r_k.at[1])
        w0_copy(c).wait_send()

    keep.wait()

    @pl.when(r == 0)
    def _():
        for p in range(1, 8):
            lead_copy(p).wait_send()

    @pl.when(core == 0)
    def _():
        lead_sib.wait_send()

    a_sib.wait_send()
    for d in range(1, 8):
        a_copy(d)[1].wait_send()

    @pl.when(c == 0)
    def _():
        k_copies(0, sent)
        k_copies(1, sent)

    @pl.when(r != c)
    def _():
        t_copy.wait_send()

    b_copies(sent)
    x_copies(sent)
    w_copies(sent)
    z_copies(sent)
    l_copies(sent, lambda j: None)
    for k in range(4):
        y_copies(k, sent)
        relay(k, sent)

    @pl.when(sib >= c)
    def _():
        w_sib.wait_send()
        for d in range(8):
            f_copy(d).wait_send()


def compact_exchange(matrix, piv_row):
    rows, cols = matrix.shape
    width = piv_row.shape[1]
    half, part = width // 2, cols // 8
    dma = pltpu.SemaphoreType.DMA
    any_spec = pl.BlockSpec(memory_space=pl.ANY)
    vmem = pl.BlockSpec(memory_space=pltpu.VMEM)
    panel = jax.ShapeDtypeStruct((8, width, part), F32)
    return pl.pallas_call(
        compact_kernel,
        out_shape=(
            panel,
            panel,
            jax.ShapeDtypeStruct((2, 8, CAP, part), F32),
            jax.ShapeDtypeStruct((CAP, width), F32),
            jax.ShapeDtypeStruct((width, width), F32),
        ),
        in_specs=[any_spec, vmem],
        out_specs=(any_spec, any_spec, vmem, vmem, vmem),
        scratch_shapes=[
            pltpu.VMEM((rows, cols), F32),
            pltpu.VMEM((CAP, cols), F32),
            pltpu.VMEM((16 * CAP, width), F32),
            pltpu.VMEM((2, 8, CAP, part), F32),
            pltpu.VMEM((width, part), F32),
            pltpu.VMEM((half, part), F32),
            pltpu.VMEM((2, 8, CAP, width), F32),
            pltpu.VMEM((CAP, 128), F32),
            pltpu.VMEM((16, CAP, 128), F32),
            pltpu.VMEM((8, CAP, part), F32),
            dma((8,)), dma((8,)), dma((3,)), dma((3,)), dma((8,)), dma((1,)),
            dma((2, 16)), dma((2,)), dma((1,)), dma((16,)), dma((8,)), dma((8,)), dma((8,)), dma((2, 8)),
            dma((4,)), dma((4,)), dma((2, 8)), dma((8,)), dma((1,)), dma((1,)), dma((4,)), dma((4,)),
            dma((2, 4)), dma((4,)), dma((4, 4)),
            dma((3,)),
        ],
        compiler_params=pltpu.CompilerParams(
            collective_id=1, has_side_effects=True, vmem_limit_bytes=32 * 1024 * 1024
        ),
        name="compact_exchange",
    )(matrix, piv_row)


def compact_update_kernel(
    piv_row, m, qc, qr, swaps, corner, w1, coupling, result, panel, right, left, piv_col, w1s,
    outs, sems,
):
    r, c = lax.axis_index("row"), lax.axis_index("col")
    tile, cols = m.shape
    rows = tile * pl.num_programs(0)
    width = coupling.shape[0]
    part = qc.shape[2]
    step = pl.program_id(0)
    row_start = r * rows + step * tile
    col_start = c * cols

    def dot(a, b, dims=((0,), (0,))):
        return lax.dot_general(a, b, (dims, ((), ())), preferred_element_type=F32)

    across = ((1,), (0,))
    slot = lax.rem(step, 2)
    out = outs.at[slot]

    def put(i):
        at = pl.ds(pl.multiple_of(i * tile, tile), tile)
        return pltpu.make_async_copy(outs.at[lax.rem(i, 2)], result.at[at], sems.at[lax.rem(i, 2)])

    @pl.when(step >= 2)
    def _():
        put(step - 2).wait()

    @pl.when(r < c)
    def _():
        out[...] = jnp.zeros_like(out)

    @pl.when((r >= c) & (step == 0))
    def _():
        place_row = places(piv_row[...], rows)
        piv_col[...] = column(piv_row[...])
        spread = one_hot(piv_col[...], col_start, (width, cols), 1).astype(F32)
        hit = jnp.max(spread, axis=0, keepdims=True) > 0
        spread = spread.astype(BF16)
        for i, term in enumerate(split(w1[...], 3)):
            w1s[i] = term
        placed = [dot(w1s[i], spread, across) for i in range(2)]
        for i in range(8):
            cut = slice(i * part, (i + 1) * part)
            for j, term in enumerate(split(qc[i], 2)):
                term = jnp.where(hit[:, cut], placed[j][:, cut], term.astype(F32))
                panel[j, :, cut] = term.astype(BF16)
        lead = jnp.concatenate([swaps[0, i] for i in range(8)], axis=1)
        placed = sum(dot(term, spread, across) for term in split(corner[...], 3))
        lead = jnp.where(hit, placed, lead)
        for j, term in enumerate(split(lead, 3)):
            right[j * CAP : (j + 1) * CAP] = term
        col_piv = listed(place_row, piv_row[...], order(c) * CAP, CAP)
        hot = one_hot(col_piv, col_start, (CAP, cols), 1).astype(F32).astype(BF16)
        for j in range(3):
            right[(3 + j) * CAP : (4 + j) * CAP] = hot
        left[...] = listed(place_row, piv_row[...], order(r) * CAP, CAP)

    @pl.when(r >= c)
    def _():
        hot = one_hot(left[...], row_start, (CAP, tile), 1).astype(F32)
        hit = jnp.max(hot, axis=0, keepdims=True)
        rows_t = jnp.concatenate([qr[0], qr[1]], axis=1)
        spread = one_hot(piv_col[...], row_start, (width, tile), 1).astype(F32).astype(BF16)
        placed = sum(dot(w1s[i], spread, across) for i in range(3))
        rows_t = jnp.where(hit > 0, placed, rows_t)
        scaled = lax.dot_general(
            coupling[...], rows_t, (((0,), (0,)), ((), ())),
            precision=HIGHEST, preferred_element_type=F32,
        )
        s_hi, s_lo = split(scaled, 2)
        change = dot(s_hi, panel[0]) + dot(s_hi, panel[1]) + dot(s_lo, panel[0])
        which = jnp.where(r == c, 0, 1)
        lead = jnp.concatenate([swaps[which, 2 * step + i] for i in range(2)], axis=1)
        lead = jnp.where(hit > 0, 0.0, lead)
        hot = hot.astype(BF16)
        lhs = jnp.concatenate([hot, hot, hot] + split(lead, 3), axis=0)
        moved = dot(lhs, right[...])
        hit_row = column(hit) > 0
        hit_col = jnp.max(right[3 * CAP : 4 * CAP].astype(F32), axis=0, keepdims=True) > 0
        value = jnp.where(hit_row | hit_col, 0.0, m[...]) + moved
        places_col = lax.broadcasted_iota(jnp.int32, (tile, cols), 1) + col_start
        below = lax.broadcasted_iota(jnp.int32, (tile, cols), 0) + row_start >= places_col
        out[...] = jnp.where(below, value - change, 0.0)

        @pl.when(c == 0)
        def _():
            out[:, :width] = jnp.where(
                below[:, :width], rows_t.T - change[:, :width], 0.0
            )

    put(step).start()

    @pl.when(step == pl.num_programs(0) - 1)
    def _():
        put(step - 1).wait()
        put(step).wait()


def compact_update(piv_row, matrix, qc, qr, swaps, corner, w1, coupling):
    rows, cols = matrix.shape
    width = coupling.shape[0]
    part = cols // 8
    tile = 2 * part

    def whole(shape):
        return pl.BlockSpec(shape, lambda i: (0,) * len(shape))

    return pl.pallas_call(
        compact_update_kernel,
        grid=(rows // tile,),
        out_shape=jax.ShapeDtypeStruct((rows, cols), F32),
        in_specs=[
            whole((1, width)),
            pl.BlockSpec((tile, cols), lambda i: (i, 0)),
            whole((8, width, part)),
            pl.BlockSpec((2, width, part), lambda i: (i, 0, 0)),
            whole((2, 8, CAP, part)),
            whole((CAP, width)),
            whole((width, width)),
            whole((width, width)),
        ],
        out_specs=pl.BlockSpec(memory_space=pltpu.HBM),
        scratch_shapes=[
            pltpu.VMEM((2, width, cols), BF16),
            pltpu.VMEM((6 * CAP, cols), BF16),
            pltpu.VMEM((CAP, 1), jnp.int32),
            pltpu.VMEM((width, 1), jnp.int32),
            pltpu.VMEM((3, width, width), BF16),
            pltpu.VMEM((2, tile, cols), F32),
            pltpu.SemaphoreType.DMA((2,)),
        ],
        compiler_params=pltpu.CompilerParams(vmem_limit_bytes=32 * 1024 * 1024),
        name="compact_update",
    )(piv_row, matrix, qc, qr, swaps, corner, w1, coupling)


def per_device(matrix, pivots, coupling):
    width = coupling.shape[0]
    rows = matrix.shape[0]
    piv_row = pivots.reshape(1, width)

    def compact(matrix, pivots, coupling):
        parts = compact_exchange(matrix, piv_row)
        return compact_update(piv_row, matrix, *parts, coupling)

    def general(matrix, pivots, coupling):
        piv_col = pivots.reshape(width, 1)
        picked = pick(matrix, pivots)
        qc, qr = exchange(picked, matrix, piv_col, piv_row)
        return update(piv_col, piv_row, matrix, qc, qr, coupling)

    blocks = jnp.arange(16, dtype=jnp.int32)[:, None]
    counts = jnp.sum((piv_row // rows == blocks).astype(jnp.int32), axis=1)
    return lax.cond(jnp.max(counts) <= CAP, compact, general, matrix, pivots, coupling)


def solution(mesh):
    return jax.shard_map(
        per_device,
        mesh=mesh,
        in_specs=(P("row", "col"), P(), P()),
        out_specs=P("row", "col"),
        check_vma=False,
    )
```

```python
import functools

import jax
import jax.numpy as jnp
from jax import lax
from jax.experimental import pallas as pl
from jax.experimental.pallas import tpu as pltpu
from jax.sharding import PartitionSpec as P

MESH = pl.DeviceIdType.MESH
F32 = jnp.float32
BF16 = jnp.bfloat16
HIGHEST = lax.Precision.HIGHEST
CAP = 32


def one_hot(index, start, shape, axis):
    return lax.broadcasted_iota(jnp.int32, shape, axis) + start == index


def pick_kernel(piv, matrix, picked, sem):
    rows = matrix.shape[0]
    count = picked.shape[0]
    start = lax.axis_index("row") * rows
    picked[...] = jnp.zeros_like(picked)

    def copy(k):
        local = jnp.clip(piv[k] - start, 0, rows - 1)
        return pltpu.make_async_copy(matrix.at[pl.ds(local, 1)], picked.at[pl.ds(k, 1)], sem)

    def go(k, _):
        @pl.when((piv[k] >= start) & (piv[k] < start + rows))
        def _():
            copy(k).start()

        return 0

    def wait(k, _):
        @pl.when((piv[k] >= start) & (piv[k] < start + rows))
        def _():
            copy(k).wait()

        return 0

    lax.fori_loop(0, count, go, 0)
    lax.fori_loop(0, count, wait, 0)


def pick(matrix, pivots):
    return pl.pallas_call(
        pick_kernel,
        out_shape=jax.ShapeDtypeStruct((pivots.shape[0], matrix.shape[1]), F32),
        in_specs=[pl.BlockSpec(memory_space=pltpu.SMEM), pl.BlockSpec(memory_space=pl.ANY)],
        out_specs=pl.BlockSpec(memory_space=pltpu.VMEM),
        scratch_shapes=[pltpu.SemaphoreType.DMA],
        name="pick",
    )(pivots, matrix)


def exchange_kernel(
    picked, matrix, piv_col, piv_row, qc, qr,
    a1buf, sums, a2buf, raw, piece, corner, w0buf, w0mine,
    s_a1, r_a1, s_a2, r_a2, s_ld, r_ld, s_w, r_w, s_w0, r_w0,
    s_b, r_b, s_f, s_t, r_t, s_y, r_y, local,
):
    r, c = lax.axis_index("row"), lax.axis_index("col")
    width, cols = picked.shape
    own = raw.shape[1]
    q, core = lax.div(r, 2), lax.rem(r, 2)
    x, y, zh = lax.div(r, 4), lax.div(c, 4), lax.rem(c, 4)
    sib = r + 1 - 2 * core
    col_start = c * cols

    def remote(src, dst, ssem, rsem, row, col):
        return pltpu.make_async_remote_copy(
            src_ref=src, dst_ref=dst, send_sem=ssem, recv_sem=rsem,
            device_id=(row, col), device_id_type=MESH,
        )

    def arrived(dst, rsem):
        remote(dst, dst, rsem, rsem, sib, c).wait_recv()

    def signal(row, col):
        pl.semaphore_signal(barrier, inc=1, device_id=(row, col), device_id_type=MESH)

    def slots(g, n=1):
        return pl.ds(pl.multiple_of(g * own, own), n * own)

    barrier = pltpu.get_barrier_semaphore()
    for d in range(1, 16):
        signal(lax.rem(r + d, 16), c)
    for d in range(1, 4):
        signal(r, lax.rem(y + d, 4) * 4 + zh)
    for j in range(4):
        @pl.when((r != c) | (4 * y + j != r))
        def _():
            signal(4 * y + j, r)

    @pl.when(c != 0)
    def _():
        signal(r, 0)

    @pl.when(c == 0)
    def _():
        for b in range(1, 16):
            signal(r, b)

    greeted = 15 + 3 + 4 - jnp.where(r == c, 1, 0) + jnp.where(c == 0, 15, 1)
    pl.semaphore_wait(barrier, greeted)

    def lead_copies(act):
        @pl.when(r == 0)
        def _():
            for g in range(1, 16):
                act(remote(matrix.at[slots(g)], raw.at[1], s_ld.at[g], r_ld.at[0], g, c))
            act(pltpu.make_async_copy(matrix.at[slots(0)], raw.at[1], local.at[0]))

    lead_copies(lambda copy: copy.start())

    def a1(p):
        return remote(
            picked.at[slots(2 * p + 1 - core)], a1buf.at[p], s_a1.at[p], r_a1.at[p], sib, c
        )

    def a2(p):
        return remote(sums.at[p], a2buf.at[q], s_a2.at[p], r_a2.at[q], 2 * p + core, c)

    for d in range(1, 9):
        a1(lax.rem(q + d, 8)).start()
    for d in range(1, 9):
        p = lax.rem(q + d, 8)
        arrived(a1buf.at[p], r_a1.at[p])
        total = picked[slots(2 * p + core)] + a1buf[p]
        if d < 8:
            sums[p] = total
            a2(p).start()
        else:
            a2buf[q] = total

    hot_t = one_hot(piv_col[...], col_start, (width, cols), 1).astype(F32)
    swapped = jnp.max(hot_t, axis=0, keepdims=True) > 0

    def fixed(part):
        placed = jnp.dot(corner[part], hot_t, precision=HIGHEST, preferred_element_type=F32)
        return jnp.where(swapped, placed, raw[part])

    def send_corner(part, act):
        for b in range(1, 16):
            act(remote(corner.at[part], corner.at[part], s_w.at[part, b], r_w.at[part], r, b))

    def get_corner(part):
        @pl.when(c == 0)
        def _():
            corner[part] = raw[part, :, :width]
            send_corner(part, lambda copy: copy.start())

        @pl.when(c != 0)
        def _():
            arrived(corner.at[part], r_w.at[part])

    def b_copy(part, d):
        p = lax.rem(q + d, 8)
        return p, remote(
            piece.at[part], qc.at[part, slots(r)], s_b.at[part, d], r_b.at[part, r], 2 * p + core, c
        )

    def b_copies(part, act):
        for d in range(1, 8):
            p, copy = b_copy(part, d)

            @pl.when(2 * p + 1 >= c)
            def _():
                act(copy)

    def f_copy(part, d):
        if d == 0:
            return remote(
                piece.at[part], qc.at[part, slots(r)], s_f.at[part, 0], r_b.at[part, r], sib, c
            )
        g = 2 * lax.rem(q + d, 8) + core
        return remote(
            qc.at[part, slots(g)], qc.at[part, slots(g)], s_f.at[part, d], r_b.at[part, g], sib, c
        )

    def t_copies(part, act):
        for k in range(4):
            col = 4 * x + k
            here = (r == c) & (k == zh)

            @pl.when(jnp.logical_not(here))
            def _():
                act(
                    remote(
                        piece.at[part], qr.at[part, slots(r)],
                        s_t.at[part, k], r_t.at[part, lax.rem(r, 4)], c, col,
                    )
                )

            @pl.when(here)
            def _():
                act(
                    pltpu.make_async_copy(
                        piece.at[part], qr.at[part, slots(r)], local.at[3 + part]
                    )
                )

    def send_piece(part):
        b_copies(part, lambda copy: copy.start())
        t_copies(part, lambda copy: copy.start())

        @pl.when(sib >= c)
        def _():
            f_copy(part, 0).start()

        pltpu.make_async_copy(piece.at[part], qc.at[part, slots(r)], local.at[1 + part]).start()

    @pl.when(r == 0)
    def _():
        pltpu.make_async_copy(matrix.at[slots(0)], raw.at[1], local.at[0]).wait()

    @pl.when(r != 0)
    def _():
        arrived(raw.at[1], r_ld.at[0])

    get_corner(1)
    piece[1] = fixed(1)
    send_piece(1)

    for d in range(1, 8):
        p = lax.rem(q + d, 8)
        arrived(a2buf.at[p], r_a2.at[p])
    total = a2buf[0]
    for p in range(1, 8):
        total = total + a2buf[p]
    raw[0] = total
    get_corner(0)
    hot = one_hot(piv_row[...], col_start, (cols, width), 0).astype(F32)
    mine = jnp.dot(total, hot, precision=HIGHEST, preferred_element_type=F32)

    def w0_copy(col):
        return remote(w0mine, w0buf.at[col], s_w0.at[0], r_w0.at[col], r, 0)

    @pl.when(c != 0)
    def _():
        w0mine[...] = mine
        w0_copy(c).start()

    piece[0] = fixed(0)

    @pl.when(c == 0)
    def _():
        w0 = mine
        for b in range(1, 16):
            arrived(w0buf.at[b], r_w0.at[b])
            w0 = w0 + w0buf[b]
        piece[0, :, :width] = w0

    send_piece(0)

    def y_copies(part, act):
        for d in range(1, 4):
            col = lax.rem(y + d, 4) * 4 + zh

            @pl.when(col <= r)
            def _():
                block = qr.at[part, slots(4 * y, 4)]
                act(remote(block, block, s_y.at[part, d], r_y.at[part, y], r, col))

    def run_y(part):
        for j in range(4):
            here = (r == c) & (4 * y + j == r)

            @pl.when(jnp.logical_not(here))
            def _():
                arrived(qr.at[part, slots(4 * y + j)], r_t.at[part, j])

            @pl.when(here)
            def _():
                pltpu.make_async_copy(
                    piece.at[part], qr.at[part, slots(r)], local.at[3 + part]
                ).wait()

        y_copies(part, lambda copy: copy.start())

    def run_f(part):
        for d in range(1, 8):
            g = 2 * lax.rem(q + d, 8) + core

            @pl.when(2 * q + 1 >= c)
            def _():
                arrived(qc.at[part, slots(g)], r_b.at[part, g])

            @pl.when(sib >= c)
            def _():
                f_copy(part, d).start()

    run_y(1)
    run_y(0)
    run_f(1)
    run_f(0)

    for part in (1, 0):
        for d in range(8):
            g = 2 * lax.rem(q + d, 8) + 1 - core

            @pl.when(r >= c)
            def _():
                arrived(qc.at[part, slots(g)], r_b.at[part, g])

        for d in range(1, 4):
            there = lax.rem(y + d, 4)

            @pl.when(c <= r)
            def _():
                arrived(qr.at[part, slots(4 * there, 4)], r_y.at[part, there])

        pltpu.make_async_copy(piece.at[part], qc.at[part, slots(r)], local.at[1 + part]).wait()

    lead_copies(lambda copy: copy.wait_send() if copy.is_remote else None)
    for d in range(1, 9):
        a1(lax.rem(q + d, 8)).wait_send()
    for d in range(1, 8):
        a2(lax.rem(q + d, 8)).wait_send()

    @pl.when(c != 0)
    def _():
        w0_copy(c).wait_send()

    for part in (1, 0):
        @pl.when(c == 0)
        def _():
            send_corner(part, lambda copy: copy.wait_send())

        b_copies(part, lambda copy: copy.wait_send())
        t_copies(part, lambda copy: copy.wait_send() if copy.is_remote else None)
        y_copies(part, lambda copy: copy.wait_send())

        @pl.when(sib >= c)
        def _():
            for d in range(8):
                f_copy(part, d).wait_send()


def exchange(picked, matrix, piv_col, piv_row):
    width, cols = picked.shape
    own = width // 16
    dma = pltpu.SemaphoreType.DMA
    out = jax.ShapeDtypeStruct((2, width, cols), F32)
    any_spec = pl.BlockSpec(memory_space=pl.ANY)
    vmem = pl.BlockSpec(memory_space=pltpu.VMEM)
    return pl.pallas_call(
        exchange_kernel,
        out_shape=(out, out),
        in_specs=[vmem, any_spec, vmem, vmem],
        out_specs=(any_spec, any_spec),
        scratch_shapes=[
            pltpu.VMEM((8, own, cols), F32),
            pltpu.VMEM((8, own, cols), F32),
            pltpu.VMEM((8, own, cols), F32),
            pltpu.VMEM((2, own, cols), F32),
            pltpu.VMEM((2, own, cols), F32),
            pltpu.VMEM((2, own, width), F32),
            pltpu.VMEM((16, own, width), F32),
            pltpu.VMEM((own, width), F32),
            dma((8,)), dma((8,)), dma((8,)), dma((8,)),
            dma((16,)), dma((1,)), dma((2, 16)), dma((2,)), dma((1,)), dma((16,)),
            dma((2, 8)), dma((2, 16)), dma((2, 8)), dma((2, 4)), dma((2, 4)), dma((2, 4)), dma((2, 4)),
            dma((5,)),
        ],
        compiler_params=pltpu.CompilerParams(
            collective_id=0, has_side_effects=True, vmem_limit_bytes=32 * 1024 * 1024
        ),
        name="exchange",
    )(picked, matrix, piv_col, piv_row)


def split(value, n):
    terms = []
    for _ in range(n):
        term = value.astype(BF16)
        terms.append(term)
        value = value - term.astype(F32)
    return terms


def update_kernel(piv_col, piv_row, m, qc, qr, coupling, out, hot_t, panel, lead):
    r, c = lax.axis_index("row"), lax.axis_index("col")
    tile, cols = out.shape
    width = coupling.shape[0]
    step = pl.program_id(0)
    row_start = r * cols + step * tile
    col_start = c * cols

    @pl.when(r < c)
    def _():
        out[...] = jnp.zeros_like(out)

    @pl.when((r >= c) & (step == 0))
    def _():
        hot_t[...] = one_hot(piv_col[...], col_start, (width, cols), 1).astype(BF16)
        for i, term in enumerate(split(qc[0], 2)):
            panel[i] = term
        for i, term in enumerate(split(qc[1], 3)):
            lead[i] = term

    def dot(a, b):
        return jnp.dot(a, b, preferred_element_type=F32)

    @pl.when(r >= c)
    def _():
        panel_rows = qr[0].T
        scaled = jnp.dot(panel_rows, coupling[...], precision=HIGHEST, preferred_element_type=F32)
        s_hi, s_lo = split(scaled, 2)
        update = dot(s_hi, panel[0]) + dot(s_hi, panel[1]) + dot(s_lo, panel[0])
        hot = one_hot(piv_row[...], row_start, (tile, width), 0)
        hit_row = jnp.max(hot.astype(F32), axis=1, keepdims=True) > 0
        hit_col = jnp.max(hot_t[...].astype(F32), axis=0, keepdims=True) > 0
        hot = hot.astype(F32).astype(BF16)
        new_rows = dot(hot, lead[0]) + dot(hot, lead[1]) + dot(hot, lead[2])
        lead_cols = jnp.where(hit_row, 0.0, qr[1].T)
        new_cols = sum(dot(term, hot_t[...]) for term in split(lead_cols, 3))
        value = jnp.where(hit_row | hit_col, 0.0, m[...]) + new_rows + new_cols
        spread = jnp.concatenate([panel_rows, jnp.zeros((tile, cols - width), F32)], axis=1)
        places = lax.broadcasted_iota(jnp.int32, (tile, cols), 1)
        value = jnp.where((places < width) & (c == 0), spread, value)
        below = lax.broadcasted_iota(jnp.int32, (tile, cols), 0) + row_start >= places + col_start
        out[...] = jnp.where(below, value - update, 0.0)


def update(piv_col, piv_row, matrix, qc, qr, coupling):
    rows, cols = matrix.shape
    width = coupling.shape[0]
    tile = min(rows, 256)

    def whole(shape):
        return pl.BlockSpec(shape, lambda i: (0,) * len(shape))

    return pl.pallas_call(
        update_kernel,
        grid=(rows // tile,),
        out_shape=jax.ShapeDtypeStruct((rows, cols), F32),
        in_specs=[
            whole((width, 1)),
            whole((1, width)),
            pl.BlockSpec((tile, cols), lambda i: (i, 0)),
            whole((2, width, cols)),
            pl.BlockSpec((2, width, tile), lambda i: (0, 0, i)),
            whole((width, width)),
        ],
        out_specs=pl.BlockSpec((tile, cols), lambda i: (i, 0)),
        scratch_shapes=[
            pltpu.VMEM((width, cols), BF16),
            pltpu.VMEM((2, width, cols), BF16),
            pltpu.VMEM((3, width, cols), BF16),
        ],
        compiler_params=pltpu.CompilerParams(vmem_limit_bytes=48 * 1024 * 1024),
        name="update",
    )(piv_col, piv_row, matrix, qc, qr, coupling)


def order(s):
    return lax.rem(s, 2) * 8 + lax.div(s, 2)


def blocks_of(piv, rows):
    block = jnp.right_shift(piv, rows.bit_length() - 1)
    return jnp.bitwise_and(block, 1) * 8 + jnp.right_shift(block, 1)


def column(row):
    return jnp.broadcast_to(row, (8, row.shape[1])).T[:, :1]


def places(piv_row, rows):
    width = piv_row.shape[1]
    first = lax.broadcasted_iota(jnp.int32, (width, width), 0)
    second = lax.broadcasted_iota(jnp.int32, (width, width), 1)
    block_row = blocks_of(piv_row, rows)
    before = (column(block_row) == block_row) & (first < second)
    return block_row * CAP + jnp.sum(jnp.where(before, 1, 0), axis=0, keepdims=True)


def listed(place_row, piv_row, start, count):
    spot = lax.broadcasted_iota(jnp.int32, (count, place_row.shape[1]), 0) + start
    return jnp.sum(jnp.where(spot == place_row, piv_row + 1, 0), axis=1, keepdims=True) - 1


def hot16(mask):
    return mask.astype(F32).astype(BF16)


def dot16(a, b, dims=((1,), (0,))):
    return lax.dot_general(a, b, (dims, ((), ())), preferred_element_type=F32)


def choose(hot, value):
    return sum(dot16(hot, term) for term in split(value, 3))


def compact_kernel(
    matrix, piv_row, coupling, out,
    block, picked, hall, hall_t, piv_col, spread, hit_col,
    abuf, lead, piece, wbuf, vbuf, w0out, w0in, w2out, corner, lout, swaps, qc, qr,
    w1s, w0, panel, right, left,
    s_a, r_a, s_sib, r_sib, s_ld, r_ld, s_k, r_k, s_w0, r_w0, s_w2, r_w2, s_w, r_w, s_v, r_v,
    s_l, r_l, s_b, s_x, r_b, s_f, s_t, r_t, s_z, r_z, s_y, s_r, r_y, local,
):
    r, c = lax.axis_index("row"), lax.axis_index("col")
    rows, cols = matrix.shape
    width = piv_row.shape[1]
    half, part = width // 2, cols // 8
    tile = 2 * part
    q, core = lax.div(r, 2), lax.rem(r, 2)
    zl = lax.rem(q, 2)
    y, zh = lax.div(c, 4), lax.rem(c, 4)
    sib = r + 1 - 2 * core
    pair = q + 1 - 2 * zl
    chunk = lax.div(order(c), 4)
    col_start = c * cols

    def remote(src, dst, ssem, rsem, row, col):
        return pltpu.make_async_remote_copy(
            src_ref=src, dst_ref=dst, send_sem=ssem, recv_sem=rsem,
            device_id=(row, col), device_id_type=MESH,
        )

    def arrived(dst, rsem):
        remote(dst, dst, rsem, rsem, sib, c).wait_recv()

    def start(copy):
        copy.start()

    def sent(copy):
        copy.wait_send()

    load = pltpu.make_async_copy(matrix, block, local.at[0])
    load.start()

    barrier = pltpu.get_barrier_semaphore()

    def signal(row, col):
        pl.semaphore_signal(barrier, inc=1, device_id=(row, col), device_id_type=MESH)

    for d in (1, 3):
        signal(r, lax.rem(y + d, 4) * 4 + zh)
    for d in (1, 2, 3):
        signal(r, 4 * y + lax.rem(zh + d, 4))

    @pl.when(r != c)
    def _():
        signal(c, r)

    @pl.when(c != 0)
    def _():
        signal(r, 0)

    @pl.when(c == 0)
    def _():
        for b in range(1, 16):
            signal(r, b)

    @pl.when(r > c)
    def _():
        for j in range(8):
            signal(2 * j + lax.rem(c, 2), r)

    for d in range(1, 16):
        signal(lax.rem(r + d, 16), c)

    greeted = 15 + 2 + 3 + jnp.where(r == c, 0, 1) + jnp.where(c == 0, 15, 1)
    greeted = greeted + lax.div(c - core + 1, 2)

    place_row = places(piv_row[...], rows)
    piv_col[...] = column(piv_row[...])
    spots = lax.broadcasted_iota(jnp.int32, (16 * CAP, width), 0)
    hall[...] = hot16(spots == place_row)
    spots = lax.broadcasted_iota(jnp.int32, (width, 16 * CAP), 1)
    hall_t[...] = hot16(spots == column(place_row))
    mine = order(r) * CAP
    left[...] = listed(place_row, piv_row[...], mine, CAP)
    load.wait()
    for t in range(CAP):
        local_row = jnp.sum(jnp.where(place_row == mine + t, piv_row[...] - r * rows, 0))
        picked[pl.ds(t, 1)] = block[pl.ds(jnp.clip(local_row, 0, rows - 1), 1)]
    picked[...] = jnp.where(left[...] >= 0, picked[...], 0.0)

    @pl.when(c == 0)
    def _():
        wbuf[core, q] = picked[:, :width]

    pl.semaphore_wait(barrier, greeted)

    def a_copy(d):
        p = lax.rem(q + d, 8)
        cut = pl.ds(pl.multiple_of(p * part, part), part)
        return remote(picked.at[:, cut], abuf.at[core, q], s_a.at[d], r_a.at[q], 2 * p + core, c)

    for d in range(1, 8):
        a_copy(d).start()

    def k_copy(i, b):
        src = wbuf.at[core, q] if i == 0 else corner
        return remote(src, src, s_k.at[i, b], r_k.at[i], r, b)

    def k_copies(i, act):
        for b in range(1, 16):
            act(k_copy(i, b))

    @pl.when(c == 0)
    def _():
        k_copies(0, start)

    def lead_copy(p):
        return remote(
            block.at[pl.ds(0, width), pl.ds(p * part, part)], lead, s_ld.at[p], r_ld.at[0], 2 * p, c
        )

    @pl.when(r == 0)
    def _():
        for p in range(1, 8):
            lead_copy(p).start()

    abuf[core, q] = picked[:, pl.ds(pl.multiple_of(q * part, part), part)]

    def w2_copies(act):
        for s in range(1, 16):
            src = w2out.at[(s % 2) * 8 + s // 2]
            act(remote(src, corner, s_w2.at[s], r_w2.at[0], s, 0))

    @pl.when((r == 0) & (c == 0))
    def _():
        w2out[...] = choose(hall[...], block[:width, :width]).reshape(16, CAP, width)
        w2_copies(start)
        corner[...] = w2out[0]

    def w0_copy(b):
        return remote(w0out, w0in.at[b], s_w0.at[0], r_w0.at[b], r, 0)

    here_piv = listed(place_row, piv_row[...], chunk * 128, 128)
    near = hot16(one_hot(here_piv, col_start, (128, cols), 1))
    w0out[...] = sum(dot16(term, near, ((1,), (1,))) for term in split(picked[...], 3))

    @pl.when(c != 0)
    def _():
        w0_copy(c).start()

    for d in range(1, 8):
        p = lax.rem(q + d, 8)
        arrived(abuf.at[core, p], r_a.at[p])
    a_sib = remote(abuf.at[core], abuf.at[core], s_sib.at[1], r_sib.at[1], sib, c)
    a_sib.start()
    arrived(abuf.at[1 - core], r_sib.at[1])

    def slot(k):
        return pl.ds(pl.multiple_of(k * half, half), half)

    piece[...] = choose(hall_t[slot(core)], abuf[...].reshape(16 * CAP, part))

    t_copy = remote(piece, qr.at[q, slot(core)], s_t.at[0], r_t.at[0], c, r)

    @pl.when(r != c)
    def _():
        t_copy.start()

    @pl.when(r == c)
    def _():
        qr[q, slot(core)] = piece[...]

    def wanted(p):
        return 2 * p + 1 >= c

    def b_copies(act):
        @pl.when(wanted(6 + 1 - zl))
        def _():
            act(
                remote(piece, qc.at[q, slot(core)], s_b.at[0], r_b.at[core, q], 2 * pair + core, c)
            )

        for d in range(1, 4):
            p = lax.rem(q + 2 * d, 8)

            @pl.when(wanted(p))
            def _():
                act(remote(piece, qc.at[q, slot(core)], s_b.at[d], r_b.at[core, q], 2 * p + core, c))

    def x_copies(act):
        for d in range(1, 4):
            p = lax.rem(q + 2 * d, 8)
            ref = qc.at[pair, slot(core)]

            @pl.when(wanted(p))
            def _():
                act(remote(ref, ref, s_x.at[d], r_b.at[core, pair], 2 * p + core, c))

    def f_copy(p):
        ref = qc.at[p, slot(core)]
        return remote(ref, ref, s_f.at[p], r_b.at[core, p], sib, c)

    def forward(p):
        @pl.when(sib >= c)
        def _():
            f_copy(p).start()

    b_copies(start)
    qc[q, slot(core)] = piece[...]
    forward(q)

    def w_copies(act, buf, ssem, rsem):
        for d in range(1, 8):
            p = lax.rem(q + d, 8)

            @pl.when(wanted(p))
            def _():
                act(
                    remote(buf.at[core, q], buf.at[core, q], ssem.at[d], rsem.at[q], 2 * p + core, c)
                )

    @pl.when(c != 0)
    def _():
        arrived(wbuf.at[core, q], r_k.at[0])

    w_copies(start, wbuf, s_w, r_w)

    lead_sib = remote(lead, lead, s_sib.at[0], r_sib.at[0], sib, c)

    @pl.when(r == 0)
    def _():
        lead[...] = block[:width, :part]

    @pl.when((core == 0) & (r != 0))
    def _():
        arrived(lead, r_ld.at[0])

    @pl.when(core == 0)
    def _():
        lead_sib.start()

    @pl.when(core == 1)
    def _():
        arrived(lead, r_sib.at[0])

    lists = hall[pl.ds(pl.multiple_of(core * 8 * CAP, 8 * CAP), 8 * CAP)]
    lout[...] = choose(lists, lead[...]).reshape(8, CAP, part)

    def l_copies(act, act_here):
        for j in range(8):
            s = 2 * j + core
            as_row = s >= c
            row, col = jnp.where(as_row, s, c), jnp.where(as_row, c, s)
            kind = jnp.where(as_row, 0, 1)
            here = as_row & (s == r)

            @pl.when(jnp.logical_not(here))
            def _():
                act(remote(lout.at[j], swaps.at[kind, q], s_l.at[j], r_l.at[kind, q], row, col))

            @pl.when(here)
            def _():
                act_here(j)

    def keep_lead(j):
        swaps[0, q] = lout[j]

    l_copies(start, keep_lead)

    @pl.when(c == 0)
    def _():
        @pl.when(r != 0)
        def _():
            arrived(corner, r_w2.at[0])

        k_copies(1, start)

    hot = one_hot(piv_col[...], col_start, (width, cols), 1).astype(F32)
    hit_col[...] = jnp.max(hot, axis=0, keepdims=True)
    spread[...] = hot.astype(BF16)

    def need(there):
        return 4 * there + zh <= r

    up, down, across = lax.rem(y + 1, 4), lax.rem(y + 3, 4), lax.rem(y + 2, 4)

    def y_ref(owner, k):
        j = lax.rem(zh + k, 4)
        return qr.at[2 * owner + lax.div(j, 2), slot(lax.rem(j, 2))]

    def z_copies(act):
        for d in (1, 3, 2):
            there = lax.rem(zh + d, 4)

            @pl.when(there <= r)
            def _():
                act(
                    remote(
                        y_ref(y, 0), y_ref(y, 0), s_z.at[d], r_z.at[(4 - d) % 4], r, 4 * y + there
                    )
                )

    def y_copies(k, act):
        onward = need(across)

        def one(way, to):
            ref = y_ref(y, k)
            act(remote(ref, ref, s_y.at[way, k], r_y.at[y, k], r, 4 * to + zh))

        @pl.when(need(up) | onward if k % 2 == 0 else need(up))
        def _():
            one(0, up)

        @pl.when(need(down) | onward if k % 2 == 1 else need(down))
        def _():
            one(1, down)

    def relay(k, act):
        owner, to = (down, up) if k % 2 == 0 else (up, down)
        ref = y_ref(owner, k)

        @pl.when(need(to))
        def _():
            act(remote(ref, ref, s_r.at[k], r_y.at[owner, k], r, 4 * to + zh))

    def run_relay(k):
        owner, to = (down, up) if k % 2 == 0 else (up, down)

        @pl.when(need(y) | need(to))
        def _():
            arrived(y_ref(owner, k), r_y.at[owner, k])

        relay(k, start)

    def run_y(k):
        @pl.when(zh <= r)
        def _():
            arrived(y_ref(y, k), r_z.at[k])

        y_copies(k, start)

    @pl.when(r != c)
    def _():
        arrived(y_ref(y, 0), r_t.at[0])

    y_copies(0, start)
    z_copies(start)

    @pl.when(wanted(6 + zl))
    def _():
        arrived(qc.at[pair, slot(core)], r_b.at[core, pair])

    x_copies(start)
    forward(pair)
    for d in range(1, 4):
        p = lax.rem(q + 2 * d, 8)

        @pl.when(wanted(q))
        def _():
            arrived(qc.at[p, slot(core)], r_b.at[core, p])

        forward(p)

    @pl.when(wanted(q))
    def _():
        for d in range(1, 8):
            p = lax.rem(q + d, 8)
            arrived(wbuf.at[core, p], r_w.at[p])

    w_sib = remote(wbuf.at[core], wbuf.at[core], s_sib.at[2], r_sib.at[2], sib, c)
    v_sib = remote(vbuf.at[core], vbuf.at[core], s_sib.at[3], r_sib.at[3], sib, c)

    @pl.when(sib >= c)
    def _():
        w_sib.start()

    @pl.when(c == 0)
    def _():
        for b in range(1, 16):
            arrived(w0in.at[b], r_w0.at[b])
        w0in[0] = w0out[...]
        total = jnp.zeros((CAP, width), F32)
        for j in range(4):
            listing = sum(
                w0in[b] for b in range(16) if ((b % 2) * 8 + b // 2) // 4 == j
            )
            hot = hall[128 * j : 128 * (j + 1)]
            total = total + sum(dot16(term, hot) for term in split(listing, 3))
        vbuf[core, q] = total
        w_copies(start, vbuf, s_v, r_v)

    run_relay(0)
    run_y(1)
    run_y(3)

    for d in range(1, 4):
        p = lax.rem(pair + 2 * d, 8)

        @pl.when(wanted(q))
        def _():
            arrived(qc.at[p, slot(core)], r_b.at[core, p])

        forward(p)

    @pl.when(c == 0)
    def _():
        for d in range(1, 8):
            p = lax.rem(q + d, 8)
            arrived(vbuf.at[core, p], r_v.at[p])
        v_sib.start()
        arrived(vbuf.at[1 - core], r_sib.at[3])
        w0[...] = choose(hall_t[...], vbuf[...].reshape(16 * CAP, width))

    @pl.when(c != 0)
    def _():
        arrived(corner, r_k.at[1])

    @pl.when(r < c)
    def _():
        out[...] = jnp.zeros_like(out)

    @pl.when(r >= c)
    def _():
        arrived(wbuf.at[1 - core], r_sib.at[2])
        w1 = choose(hall_t[...], wbuf[...].reshape(16 * CAP, width))
        for i, term in enumerate(split(w1, 3)):
            w1s[i] = term
        for p in range(8):
            arrived(qc.at[p, slot(1 - core)], r_b.at[1 - core, p])
        placed = [dot16(w1s[i], spread[...]) for i in range(2)]
        hit = hit_col[...] > 0
        for p in range(8):
            cut = slice(p * part, (p + 1) * part)
            value = qc[p]
            if p < width // part:
                value = jnp.where(c == 0, w0[:, cut], value)
            for j, term in enumerate(split(value, 2)):
                term = jnp.where(hit[:, cut], placed[j][:, cut], term.astype(F32))
                panel[j, :, cut] = term.astype(BF16)
        for p in range(8):
            @pl.when(p != q)
            def _():
                arrived(swaps.at[0, p], r_l.at[0, p])
        rows_in = jnp.concatenate([swaps[0, p] for p in range(8)], axis=1)
        placed = sum(dot16(term, spread[...]) for term in split(corner[...], 3))
        rows_in = jnp.where(hit, placed, rows_in)
        for j, term in enumerate(split(rows_in, 3)):
            right[j * CAP : (j + 1) * CAP] = term
        col_piv = listed(place_row, piv_row[...], order(c) * CAP, CAP)
        hot = hot16(one_hot(col_piv, col_start, (CAP, cols), 1))
        for j in range(3):
            right[(3 + j) * CAP : (4 + j) * CAP] = hot

    run_relay(1)
    run_relay(3)
    run_y(2)

    def tile_update(owner):
        row_start = r * rows + owner * tile
        hot = one_hot(left[...], row_start, (CAP, tile), 1).astype(F32)
        hit = jnp.max(hot, axis=0, keepdims=True)
        rows_t = jnp.concatenate([qr[2 * owner], qr[2 * owner + 1]], axis=1)
        near = hot16(one_hot(piv_col[...], row_start, (width, tile), 1))
        rows_t = jnp.where(hit > 0, sum(dot16(w1s[i], near) for i in range(3)), rows_t)
        rows_t = jnp.where((r == 0) & (c == 0) & (owner == 0), w0[...], rows_t)
        scaled = lax.dot_general(
            coupling[...], rows_t, (((0,), (0,)), ((), ())),
            precision=HIGHEST, preferred_element_type=F32,
        )
        s_hi, s_lo = split(scaled, 2)
        lanes = ((0,), (0,))
        change = dot16(s_hi, panel[0], lanes) + dot16(s_hi, panel[1], lanes)
        change = change + dot16(s_lo, panel[0], lanes)
        kind = jnp.where(r == c, 0, 1)
        cols_in = jnp.concatenate([swaps[kind, 2 * owner + i] for i in range(2)], axis=1)
        cols_in = jnp.where(hit > 0, 0.0, cols_in)
        hot = hot.astype(BF16)
        lhs = jnp.concatenate([hot, hot, hot] + split(cols_in, 3), axis=0)
        moved = dot16(lhs, right[...], lanes)
        at = pl.ds(pl.multiple_of(owner * tile, tile), tile)
        gone = (column(hit) > 0) | (hit_col[...] > 0)
        value = jnp.where(gone, 0.0, block[at]) + moved
        places_col = lax.broadcasted_iota(jnp.int32, (tile, cols), 1) + col_start
        below = lax.broadcasted_iota(jnp.int32, (tile, cols), 0) + row_start >= places_col
        out[at] = jnp.where(below, value - change, 0.0)

        @pl.when(c == 0)
        def _():
            out[at, :width] = jnp.where(below[:, :width], rows_t.T - change[:, :width], 0.0)

    @pl.when(r > c)
    def _():
        for p in range(8):
            arrived(swaps.at[1, p], r_l.at[1, p])

    @pl.when(r >= c)
    def _():
        tile_update(y)

    run_relay(2)

    @pl.when(r >= c)
    def _():
        for k in range(4):
            owner = up if k % 2 == 0 else down
            arrived(y_ref(owner, k), r_y.at[owner, k])

        def side(i, _):
            tile_update(jnp.where(i == 0, up, down))
            return 0

        lax.fori_loop(0, 2, side, 0)
        for k in range(4):
            arrived(y_ref(across, k), r_y.at[across, k])
        tile_update(across)

    @pl.when(c != 0)
    def _():
        w0_copy(c).wait_send()

    @pl.when(r == 0)
    def _():
        for p in range(1, 8):
            lead_copy(p).wait_send()

    @pl.when(core == 0)
    def _():
        lead_sib.wait_send()

    a_sib.wait_send()
    for d in range(1, 8):
        a_copy(d).wait_send()

    @pl.when(c == 0)
    def _():
        k_copies(0, sent)
        k_copies(1, sent)
        w_copies(sent, vbuf, s_v, r_v)
        v_sib.wait_send()

        @pl.when(r == 0)
        def _():
            w2_copies(sent)

    @pl.when(r != c)
    def _():
        t_copy.wait_send()

    b_copies(sent)
    x_copies(sent)
    w_copies(sent, wbuf, s_w, r_w)
    z_copies(sent)
    l_copies(sent, lambda j: None)
    for k in range(4):
        y_copies(k, sent)
        relay(k, sent)

    @pl.when(sib >= c)
    def _():
        w_sib.wait_send()
        for p in range(8):
            f_copy(p).wait_send()


def compact(matrix, piv_row, coupling):
    rows, cols = matrix.shape
    width = piv_row.shape[1]
    half, part = width // 2, cols // 8
    dma = pltpu.SemaphoreType.DMA
    vmem = pl.BlockSpec(memory_space=pltpu.VMEM)
    return pl.pallas_call(
        compact_kernel,
        out_shape=jax.ShapeDtypeStruct((rows, cols), F32),
        in_specs=[pl.BlockSpec(memory_space=pl.ANY), vmem, vmem],
        out_specs=vmem,
        scratch_shapes=[
            pltpu.VMEM((rows, cols), F32),
            pltpu.VMEM((CAP, cols), F32),
            pltpu.VMEM((16 * CAP, width), BF16),
            pltpu.VMEM((width, 16 * CAP), BF16),
            pltpu.VMEM((width, 1), jnp.int32),
            pltpu.VMEM((width, cols), BF16),
            pltpu.VMEM((1, cols), F32),
            pltpu.VMEM((2, 8, CAP, part), F32),
            pltpu.VMEM((width, part), F32),
            pltpu.VMEM((half, part), F32),
            pltpu.VMEM((2, 8, CAP, width), F32),
            pltpu.VMEM((2, 8, CAP, width), F32),
            pltpu.VMEM((CAP, 128), F32),
            pltpu.VMEM((16, CAP, 128), F32),
            pltpu.VMEM((16, CAP, width), F32),
            pltpu.VMEM((CAP, width), F32),
            pltpu.VMEM((8, CAP, part), F32),
            pltpu.VMEM((2, 8, CAP, part), F32),
            pltpu.VMEM((8, width, part), F32),
            pltpu.VMEM((8, width, part), F32),
            pltpu.VMEM((3, width, width), BF16),
            pltpu.VMEM((width, width), F32),
            pltpu.VMEM((2, width, cols), BF16),
            pltpu.VMEM((6 * CAP, cols), BF16),
            pltpu.VMEM((CAP, 1), jnp.int32),
            dma((8,)), dma((8,)), dma((4,)), dma((4,)), dma((8,)), dma((1,)),
            dma((2, 16)), dma((2,)), dma((1,)), dma((16,)), dma((16,)), dma((1,)),
            dma((8,)), dma((8,)), dma((8,)), dma((8,)), dma((8,)), dma((2, 8)),
            dma((4,)), dma((4,)), dma((2, 8)), dma((8,)), dma((1,)), dma((1,)), dma((4,)), dma((4,)),
            dma((2, 4)), dma((4,)), dma((4, 4)),
            dma((1,)),
        ],
        compiler_params=pltpu.CompilerParams(
            collective_id=1, has_side_effects=True, vmem_limit_bytes=40 * 1024 * 1024
        ),
        name="compact",
    )(matrix, piv_row, coupling)


def per_device(matrix, pivots, coupling):
    width = coupling.shape[0]
    rows = matrix.shape[0]
    piv_row = pivots.reshape(1, width)

    def few(matrix, pivots, coupling):
        return compact(matrix, piv_row, coupling)

    def general(matrix, pivots, coupling):
        piv_col = pivots.reshape(width, 1)
        picked = pick(matrix, pivots)
        qc, qr = exchange(picked, matrix, piv_col, piv_row)
        return update(piv_col, piv_row, matrix, qc, qr, coupling)

    blocks = jnp.arange(16, dtype=jnp.int32)[:, None]
    counts = jnp.sum((piv_row // rows == blocks).astype(jnp.int32), axis=1)
    return lax.cond(jnp.max(counts) <= CAP, few, general, matrix, pivots, coupling)


def solution(mesh):
    return jax.shard_map(
        per_device,
        mesh=mesh,
        in_specs=(P("row", "col"), P(), P()),
        out_specs=P("row", "col"),
        check_vma=False,
    )
```

```python
import functools

import jax
import jax.numpy as jnp
from jax import lax
from jax.experimental import pallas as pl
from jax.experimental.pallas import tpu as pltpu
from jax.sharding import PartitionSpec as P

MESH = pl.DeviceIdType.MESH
F32 = jnp.float32
BF16 = jnp.bfloat16
HIGHEST = lax.Precision.HIGHEST
CAP = 32


def one_hot(index, start, shape, axis):
    return lax.broadcasted_iota(jnp.int32, shape, axis) + start == index


def pick_kernel(piv, matrix, picked, sem):
    rows = matrix.shape[0]
    count = picked.shape[0]
    start = lax.axis_index("row") * rows
    picked[...] = jnp.zeros_like(picked)

    def copy(k):
        local = jnp.clip(piv[k] - start, 0, rows - 1)
        return pltpu.make_async_copy(matrix.at[pl.ds(local, 1)], picked.at[pl.ds(k, 1)], sem)

    def go(k, _):
        @pl.when((piv[k] >= start) & (piv[k] < start + rows))
        def _():
            copy(k).start()

        return 0

    def wait(k, _):
        @pl.when((piv[k] >= start) & (piv[k] < start + rows))
        def _():
            copy(k).wait()

        return 0

    lax.fori_loop(0, count, go, 0)
    lax.fori_loop(0, count, wait, 0)


def pick(matrix, pivots):
    return pl.pallas_call(
        pick_kernel,
        out_shape=jax.ShapeDtypeStruct((pivots.shape[0], matrix.shape[1]), F32),
        in_specs=[pl.BlockSpec(memory_space=pltpu.SMEM), pl.BlockSpec(memory_space=pl.ANY)],
        out_specs=pl.BlockSpec(memory_space=pltpu.VMEM),
        scratch_shapes=[pltpu.SemaphoreType.DMA],
        name="pick",
    )(pivots, matrix)


def exchange_kernel(
    picked, matrix, piv_col, piv_row, qc, qr,
    a1buf, sums, a2buf, raw, piece, corner, w0buf, w0mine,
    s_a1, r_a1, s_a2, r_a2, s_ld, r_ld, s_w, r_w, s_w0, r_w0,
    s_b, r_b, s_f, s_t, r_t, s_y, r_y, local,
):
    r, c = lax.axis_index("row"), lax.axis_index("col")
    width, cols = picked.shape
    own = raw.shape[1]
    q, core = lax.div(r, 2), lax.rem(r, 2)
    x, y, zh = lax.div(r, 4), lax.div(c, 4), lax.rem(c, 4)
    sib = r + 1 - 2 * core
    col_start = c * cols

    def remote(src, dst, ssem, rsem, row, col):
        return pltpu.make_async_remote_copy(
            src_ref=src, dst_ref=dst, send_sem=ssem, recv_sem=rsem,
            device_id=(row, col), device_id_type=MESH,
        )

    def arrived(dst, rsem):
        remote(dst, dst, rsem, rsem, sib, c).wait_recv()

    def signal(row, col):
        pl.semaphore_signal(barrier, inc=1, device_id=(row, col), device_id_type=MESH)

    def slots(g, n=1):
        return pl.ds(pl.multiple_of(g * own, own), n * own)

    barrier = pltpu.get_barrier_semaphore()
    for d in range(1, 16):
        signal(lax.rem(r + d, 16), c)
    for d in range(1, 4):
        signal(r, lax.rem(y + d, 4) * 4 + zh)
    for j in range(4):
        @pl.when((r != c) | (4 * y + j != r))
        def _():
            signal(4 * y + j, r)

    @pl.when(c != 0)
    def _():
        signal(r, 0)

    @pl.when(c == 0)
    def _():
        for b in range(1, 16):
            signal(r, b)

    greeted = 15 + 3 + 4 - jnp.where(r == c, 1, 0) + jnp.where(c == 0, 15, 1)
    pl.semaphore_wait(barrier, greeted)

    def lead_copies(act):
        @pl.when(r == 0)
        def _():
            for g in range(1, 16):
                act(remote(matrix.at[slots(g)], raw.at[1], s_ld.at[g], r_ld.at[0], g, c))
            act(pltpu.make_async_copy(matrix.at[slots(0)], raw.at[1], local.at[0]))

    lead_copies(lambda copy: copy.start())

    def a1(p):
        return remote(
            picked.at[slots(2 * p + 1 - core)], a1buf.at[p], s_a1.at[p], r_a1.at[p], sib, c
        )

    def a2(p):
        return remote(sums.at[p], a2buf.at[q], s_a2.at[p], r_a2.at[q], 2 * p + core, c)

    for d in range(1, 9):
        a1(lax.rem(q + d, 8)).start()
    for d in range(1, 9):
        p = lax.rem(q + d, 8)
        arrived(a1buf.at[p], r_a1.at[p])
        total = picked[slots(2 * p + core)] + a1buf[p]
        if d < 8:
            sums[p] = total
            a2(p).start()
        else:
            a2buf[q] = total

    hot_t = one_hot(piv_col[...], col_start, (width, cols), 1).astype(F32)
    swapped = jnp.max(hot_t, axis=0, keepdims=True) > 0

    def fixed(part):
        placed = jnp.dot(corner[part], hot_t, precision=HIGHEST, preferred_element_type=F32)
        return jnp.where(swapped, placed, raw[part])

    def send_corner(part, act):
        for b in range(1, 16):
            act(remote(corner.at[part], corner.at[part], s_w.at[part, b], r_w.at[part], r, b))

    def get_corner(part):
        @pl.when(c == 0)
        def _():
            corner[part] = raw[part, :, :width]
            send_corner(part, lambda copy: copy.start())

        @pl.when(c != 0)
        def _():
            arrived(corner.at[part], r_w.at[part])

    def b_copy(part, d):
        p = lax.rem(q + d, 8)
        return p, remote(
            piece.at[part], qc.at[part, slots(r)], s_b.at[part, d], r_b.at[part, r], 2 * p + core, c
        )

    def b_copies(part, act):
        for d in range(1, 8):
            p, copy = b_copy(part, d)

            @pl.when(2 * p + 1 >= c)
            def _():
                act(copy)

    def f_copy(part, d):
        if d == 0:
            return remote(
                piece.at[part], qc.at[part, slots(r)], s_f.at[part, 0], r_b.at[part, r], sib, c
            )
        g = 2 * lax.rem(q + d, 8) + core
        return remote(
            qc.at[part, slots(g)], qc.at[part, slots(g)], s_f.at[part, d], r_b.at[part, g], sib, c
        )

    def t_copies(part, act):
        for k in range(4):
            col = 4 * x + k
            here = (r == c) & (k == zh)

            @pl.when(jnp.logical_not(here))
            def _():
                act(
                    remote(
                        piece.at[part], qr.at[part, slots(r)],
                        s_t.at[part, k], r_t.at[part, lax.rem(r, 4)], c, col,
                    )
                )

            @pl.when(here)
            def _():
                act(
                    pltpu.make_async_copy(
                        piece.at[part], qr.at[part, slots(r)], local.at[3 + part]
                    )
                )

    def send_piece(part):
        b_copies(part, lambda copy: copy.start())
        t_copies(part, lambda copy: copy.start())

        @pl.when(sib >= c)
        def _():
            f_copy(part, 0).start()

        pltpu.make_async_copy(piece.at[part], qc.at[part, slots(r)], local.at[1 + part]).start()

    @pl.when(r == 0)
    def _():
        pltpu.make_async_copy(matrix.at[slots(0)], raw.at[1], local.at[0]).wait()

    @pl.when(r != 0)
    def _():
        arrived(raw.at[1], r_ld.at[0])

    get_corner(1)
    piece[1] = fixed(1)
    send_piece(1)

    for d in range(1, 8):
        p = lax.rem(q + d, 8)
        arrived(a2buf.at[p], r_a2.at[p])
    total = a2buf[0]
    for p in range(1, 8):
        total = total + a2buf[p]
    raw[0] = total
    get_corner(0)
    hot = one_hot(piv_row[...], col_start, (cols, width), 0).astype(F32)
    mine = jnp.dot(total, hot, precision=HIGHEST, preferred_element_type=F32)

    def w0_copy(col):
        return remote(w0mine, w0buf.at[col], s_w0.at[0], r_w0.at[col], r, 0)

    @pl.when(c != 0)
    def _():
        w0mine[...] = mine
        w0_copy(c).start()

    piece[0] = fixed(0)

    @pl.when(c == 0)
    def _():
        w0 = mine
        for b in range(1, 16):
            arrived(w0buf.at[b], r_w0.at[b])
            w0 = w0 + w0buf[b]
        piece[0, :, :width] = w0

    send_piece(0)

    def y_copies(part, act):
        for d in range(1, 4):
            col = lax.rem(y + d, 4) * 4 + zh

            @pl.when(col <= r)
            def _():
                block = qr.at[part, slots(4 * y, 4)]
                act(remote(block, block, s_y.at[part, d], r_y.at[part, y], r, col))

    def run_y(part):
        for j in range(4):
            here = (r == c) & (4 * y + j == r)

            @pl.when(jnp.logical_not(here))
            def _():
                arrived(qr.at[part, slots(4 * y + j)], r_t.at[part, j])

            @pl.when(here)
            def _():
                pltpu.make_async_copy(
                    piece.at[part], qr.at[part, slots(r)], local.at[3 + part]
                ).wait()

        y_copies(part, lambda copy: copy.start())

    def run_f(part):
        for d in range(1, 8):
            g = 2 * lax.rem(q + d, 8) + core

            @pl.when(2 * q + 1 >= c)
            def _():
                arrived(qc.at[part, slots(g)], r_b.at[part, g])

            @pl.when(sib >= c)
            def _():
                f_copy(part, d).start()

    run_y(1)
    run_y(0)
    run_f(1)
    run_f(0)

    for part in (1, 0):
        for d in range(8):
            g = 2 * lax.rem(q + d, 8) + 1 - core

            @pl.when(r >= c)
            def _():
                arrived(qc.at[part, slots(g)], r_b.at[part, g])

        for d in range(1, 4):
            there = lax.rem(y + d, 4)

            @pl.when(c <= r)
            def _():
                arrived(qr.at[part, slots(4 * there, 4)], r_y.at[part, there])

        pltpu.make_async_copy(piece.at[part], qc.at[part, slots(r)], local.at[1 + part]).wait()

    lead_copies(lambda copy: copy.wait_send() if copy.is_remote else None)
    for d in range(1, 9):
        a1(lax.rem(q + d, 8)).wait_send()
    for d in range(1, 8):
        a2(lax.rem(q + d, 8)).wait_send()

    @pl.when(c != 0)
    def _():
        w0_copy(c).wait_send()

    for part in (1, 0):
        @pl.when(c == 0)
        def _():
            send_corner(part, lambda copy: copy.wait_send())

        b_copies(part, lambda copy: copy.wait_send())
        t_copies(part, lambda copy: copy.wait_send() if copy.is_remote else None)
        y_copies(part, lambda copy: copy.wait_send())

        @pl.when(sib >= c)
        def _():
            for d in range(8):
                f_copy(part, d).wait_send()


def exchange(picked, matrix, piv_col, piv_row):
    width, cols = picked.shape
    own = width // 16
    dma = pltpu.SemaphoreType.DMA
    out = jax.ShapeDtypeStruct((2, width, cols), F32)
    any_spec = pl.BlockSpec(memory_space=pl.ANY)
    vmem = pl.BlockSpec(memory_space=pltpu.VMEM)
    return pl.pallas_call(
        exchange_kernel,
        out_shape=(out, out),
        in_specs=[vmem, any_spec, vmem, vmem],
        out_specs=(any_spec, any_spec),
        scratch_shapes=[
            pltpu.VMEM((8, own, cols), F32),
            pltpu.VMEM((8, own, cols), F32),
            pltpu.VMEM((8, own, cols), F32),
            pltpu.VMEM((2, own, cols), F32),
            pltpu.VMEM((2, own, cols), F32),
            pltpu.VMEM((2, own, width), F32),
            pltpu.VMEM((16, own, width), F32),
            pltpu.VMEM((own, width), F32),
            dma((8,)), dma((8,)), dma((8,)), dma((8,)),
            dma((16,)), dma((1,)), dma((2, 16)), dma((2,)), dma((1,)), dma((16,)),
            dma((2, 8)), dma((2, 16)), dma((2, 8)), dma((2, 4)), dma((2, 4)), dma((2, 4)), dma((2, 4)),
            dma((5,)),
        ],
        compiler_params=pltpu.CompilerParams(
            collective_id=0, has_side_effects=True, vmem_limit_bytes=32 * 1024 * 1024
        ),
        name="exchange",
    )(picked, matrix, piv_col, piv_row)


def split(value, n):
    terms = []
    for _ in range(n):
        term = value.astype(BF16)
        terms.append(term)
        value = value - term.astype(F32)
    return terms


def update_kernel(piv_col, piv_row, m, qc, qr, coupling, out, hot_t, panel, lead):
    r, c = lax.axis_index("row"), lax.axis_index("col")
    tile, cols = out.shape
    width = coupling.shape[0]
    step = pl.program_id(0)
    row_start = r * cols + step * tile
    col_start = c * cols

    @pl.when(r < c)
    def _():
        out[...] = jnp.zeros_like(out)

    @pl.when((r >= c) & (step == 0))
    def _():
        hot_t[...] = one_hot(piv_col[...], col_start, (width, cols), 1).astype(BF16)
        for i, term in enumerate(split(qc[0], 2)):
            panel[i] = term
        for i, term in enumerate(split(qc[1], 3)):
            lead[i] = term

    def dot(a, b):
        return jnp.dot(a, b, preferred_element_type=F32)

    @pl.when(r >= c)
    def _():
        panel_rows = qr[0].T
        scaled = jnp.dot(panel_rows, coupling[...], precision=HIGHEST, preferred_element_type=F32)
        s_hi, s_lo = split(scaled, 2)
        update = dot(s_hi, panel[0]) + dot(s_hi, panel[1]) + dot(s_lo, panel[0])
        hot = one_hot(piv_row[...], row_start, (tile, width), 0)
        hit_row = jnp.max(hot.astype(F32), axis=1, keepdims=True) > 0
        hit_col = jnp.max(hot_t[...].astype(F32), axis=0, keepdims=True) > 0
        hot = hot.astype(F32).astype(BF16)
        new_rows = dot(hot, lead[0]) + dot(hot, lead[1]) + dot(hot, lead[2])
        lead_cols = jnp.where(hit_row, 0.0, qr[1].T)
        new_cols = sum(dot(term, hot_t[...]) for term in split(lead_cols, 3))
        value = jnp.where(hit_row | hit_col, 0.0, m[...]) + new_rows + new_cols
        spread = jnp.concatenate([panel_rows, jnp.zeros((tile, cols - width), F32)], axis=1)
        places = lax.broadcasted_iota(jnp.int32, (tile, cols), 1)
        value = jnp.where((places < width) & (c == 0), spread, value)
        below = lax.broadcasted_iota(jnp.int32, (tile, cols), 0) + row_start >= places + col_start
        out[...] = jnp.where(below, value - update, 0.0)


def update(piv_col, piv_row, matrix, qc, qr, coupling):
    rows, cols = matrix.shape
    width = coupling.shape[0]
    tile = min(rows, 256)

    def whole(shape):
        return pl.BlockSpec(shape, lambda i: (0,) * len(shape))

    return pl.pallas_call(
        update_kernel,
        grid=(rows // tile,),
        out_shape=jax.ShapeDtypeStruct((rows, cols), F32),
        in_specs=[
            whole((width, 1)),
            whole((1, width)),
            pl.BlockSpec((tile, cols), lambda i: (i, 0)),
            whole((2, width, cols)),
            pl.BlockSpec((2, width, tile), lambda i: (0, 0, i)),
            whole((width, width)),
        ],
        out_specs=pl.BlockSpec((tile, cols), lambda i: (i, 0)),
        scratch_shapes=[
            pltpu.VMEM((width, cols), BF16),
            pltpu.VMEM((2, width, cols), BF16),
            pltpu.VMEM((3, width, cols), BF16),
        ],
        compiler_params=pltpu.CompilerParams(vmem_limit_bytes=48 * 1024 * 1024),
        name="update",
    )(piv_col, piv_row, matrix, qc, qr, coupling)


def order(s):
    return lax.rem(s, 2) * 8 + lax.div(s, 2)


def blocks_of(piv, rows):
    block = jnp.right_shift(piv, rows.bit_length() - 1)
    return jnp.bitwise_and(block, 1) * 8 + jnp.right_shift(block, 1)


def column(row):
    return jnp.broadcast_to(row, (8, row.shape[1])).T[:, :1]


def places(piv_row, rows):
    width = piv_row.shape[1]
    first = lax.broadcasted_iota(jnp.int32, (width, width), 0)
    second = lax.broadcasted_iota(jnp.int32, (width, width), 1)
    block_row = blocks_of(piv_row, rows)
    before = (column(block_row) == block_row) & (first < second)
    return block_row * CAP + jnp.sum(jnp.where(before, 1, 0), axis=0, keepdims=True)


def listed(place_row, piv_row, start, count):
    spot = lax.broadcasted_iota(jnp.int32, (count, place_row.shape[1]), 0) + start
    return jnp.sum(jnp.where(spot == place_row, piv_row + 1, 0), axis=1, keepdims=True) - 1


def hot16(mask):
    return mask.astype(F32).astype(BF16)


def dot16(a, b, dims=((1,), (0,))):
    return lax.dot_general(a, b, (dims, ((), ())), preferred_element_type=F32)


def choose(hot, value):
    return sum(dot16(hot, term) for term in split(value, 3))


def compact_kernel(
    matrix, piv_row, coupling, out,
    block, picked, hall, hall_t, piv_col, spread, hit_col,
    abuf, lead, piece, wbuf, vbuf, w0out, w0z, w0y, w2out, corner, lout, swaps, qc, qr,
    w1s, w0, panel, right, left,
    s_a, r_a, s_sib, r_sib, s_ld, r_ld, s_k, r_k, s_w0, r_w0, s_w2, r_w2, s_w, r_w, s_v, r_v,
    s_l, r_l, s_b, s_x, r_b, s_f, s_t, r_t, s_z, r_z, s_y, s_r, r_y, local,
):
    r, c = lax.axis_index("row"), lax.axis_index("col")
    rows, cols = matrix.shape
    width = piv_row.shape[1]
    half, part = width // 2, cols // 8
    tile = 2 * part
    q, core = lax.div(r, 2), lax.rem(r, 2)
    zl = lax.rem(q, 2)
    y, zh = lax.div(c, 4), lax.rem(c, 4)
    sib = r + 1 - 2 * core
    pair = q + 1 - 2 * zl
    chunk = lax.div(order(c), 4)
    col_start = c * cols

    def remote(src, dst, ssem, rsem, row, col):
        return pltpu.make_async_remote_copy(
            src_ref=src, dst_ref=dst, send_sem=ssem, recv_sem=rsem,
            device_id=(row, col), device_id_type=MESH,
        )

    def arrived(dst, rsem):
        remote(dst, dst, rsem, rsem, sib, c).wait_recv()

    def start(copy):
        copy.start()

    def sent(copy):
        copy.wait_send()

    load = pltpu.make_async_copy(matrix, block, local.at[0])
    load.start()

    barrier = pltpu.get_barrier_semaphore()

    def signal(row, col):
        pl.semaphore_signal(barrier, inc=1, device_id=(row, col), device_id_type=MESH)

    for d in (1, 2, 3):
        signal(r, lax.rem(y + d, 4) * 4 + zh)
    for d in (1, 2, 3):
        signal(r, 4 * y + lax.rem(zh + d, 4))

    @pl.when(r != c)
    def _():
        signal(c, r)

    @pl.when(r > c)
    def _():
        for j in range(8):
            signal(2 * j + lax.rem(c, 2), r)

    for d in range(1, 16):
        signal(lax.rem(r + d, 16), c)

    greeted = 15 + 3 + 3 + jnp.where(r == c, 0, 1)
    greeted = greeted + lax.div(c - core + 1, 2)

    place_row = places(piv_row[...], rows)
    piv_col[...] = column(piv_row[...])
    spots = lax.broadcasted_iota(jnp.int32, (16 * CAP, width), 0)
    hall[...] = hot16(spots == place_row)
    spots = lax.broadcasted_iota(jnp.int32, (width, 16 * CAP), 1)
    hall_t[...] = hot16(spots == column(place_row))
    mine = order(r) * CAP
    left[...] = listed(place_row, piv_row[...], mine, CAP)
    load.wait()
    for t in range(CAP):
        local_row = jnp.sum(jnp.where(place_row == mine + t, piv_row[...] - r * rows, 0))
        picked[pl.ds(t, 1)] = block[pl.ds(jnp.clip(local_row, 0, rows - 1), 1)]
    picked[...] = jnp.where(left[...] >= 0, picked[...], 0.0)

    @pl.when(c == 0)
    def _():
        wbuf[core, q] = picked[:, :width]

    pl.semaphore_wait(barrier, greeted)

    def a_copy(d):
        p = lax.rem(q + d, 8)
        cut = pl.ds(pl.multiple_of(p * part, part), part)
        return remote(picked.at[:, cut], abuf.at[core, q], s_a.at[d], r_a.at[q], 2 * p + core, c)

    for d in range(1, 8):
        a_copy(d).start()

    def k_copies(i, act, along):
        src = wbuf.at[core, q] if i == 0 else corner

        @pl.when((c == 0) if along == 0 else (zh == 0))
        def _():
            for d in (1, 2, 3):
                col = 4 * d if along == 0 else 4 * y + d
                act(remote(src, src, s_k.at[i, 3 * along + d - 1], r_k.at[i], r, col))

    k_copies(0, start, 0)

    def lead_copy(p):
        return remote(
            block.at[pl.ds(0, width), pl.ds(p * part, part)], lead, s_ld.at[p], r_ld.at[0], 2 * p, c
        )

    @pl.when(r == 0)
    def _():
        for p in range(1, 8):
            lead_copy(p).start()

    abuf[core, q] = picked[:, pl.ds(pl.multiple_of(q * part, part), part)]

    def w2_copies(act):
        for s in range(1, 16):
            src = w2out.at[(s % 2) * 8 + s // 2]
            act(remote(src, corner, s_w2.at[s], r_w2.at[0], s, 0))

    @pl.when((r == 0) & (c == 0))
    def _():
        w2out[...] = choose(hall[...], block[:width, :width]).reshape(16, CAP, width)
        w2_copies(start)
        corner[...] = w2out[0]

    w0_copy = remote(w0out, w0z.at[zh], s_w0.at[0], r_w0.at[0, zh], r, 4 * y)
    w0_pair = remote(w0z.at[pl.ds(0, 2)], w0y.at[y], s_w0.at[1], r_w0.at[1, y], r, 0)

    here_piv = listed(place_row, piv_row[...], chunk * 128, 128)
    near = hot16(one_hot(here_piv, col_start, (128, cols), 1))
    w0out[...] = sum(dot16(term, near, ((1,), (1,))) for term in split(picked[...], 3))

    @pl.when(zh != 0)
    def _():
        w0_copy.start()

    for d in range(1, 8):
        p = lax.rem(q + d, 8)
        arrived(abuf.at[core, p], r_a.at[p])
    a_sib = remote(abuf.at[core], abuf.at[core], s_sib.at[1], r_sib.at[1], sib, c)
    a_sib.start()
    arrived(abuf.at[1 - core], r_sib.at[1])

    def slot(k):
        return pl.ds(pl.multiple_of(k * half, half), half)

    piece[...] = choose(hall_t[slot(core)], abuf[...].reshape(16 * CAP, part))

    t_copy = remote(piece, qr.at[q, slot(core)], s_t.at[0], r_t.at[0], c, r)

    @pl.when(r != c)
    def _():
        t_copy.start()

    @pl.when(r == c)
    def _():
        qr[q, slot(core)] = piece[...]

    def wanted(p):
        return 2 * p + 1 >= c

    def b_copies(act):
        @pl.when(wanted(6 + 1 - zl))
        def _():
            act(
                remote(piece, qc.at[q, slot(core)], s_b.at[0], r_b.at[core, q], 2 * pair + core, c)
            )

        for d in range(1, 4):
            p = lax.rem(q + 2 * d, 8)

            @pl.when(wanted(p))
            def _():
                act(remote(piece, qc.at[q, slot(core)], s_b.at[d], r_b.at[core, q], 2 * p + core, c))

    def x_copies(act):
        for d in range(1, 4):
            p = lax.rem(q + 2 * d, 8)
            ref = qc.at[pair, slot(core)]

            @pl.when(wanted(p))
            def _():
                act(remote(ref, ref, s_x.at[d], r_b.at[core, pair], 2 * p + core, c))

    def f_copy(p):
        ref = qc.at[p, slot(core)]
        return remote(ref, ref, s_f.at[p], r_b.at[core, p], sib, c)

    def forward(p):
        @pl.when(sib >= c)
        def _():
            f_copy(p).start()

    b_copies(start)
    qc[q, slot(core)] = piece[...]
    forward(q)

    def w_copies(act, buf, ssem, rsem):
        for d in range(1, 8):
            p = lax.rem(q + d, 8)

            @pl.when(wanted(p))
            def _():
                act(
                    remote(buf.at[core, q], buf.at[core, q], ssem.at[d], rsem.at[q], 2 * p + core, c)
                )

    @pl.when(c != 0)
    def _():
        arrived(wbuf.at[core, q], r_k.at[0])

    k_copies(0, start, 1)
    w_copies(start, wbuf, s_w, r_w)

    lead_sib = remote(lead, lead, s_sib.at[0], r_sib.at[0], sib, c)

    @pl.when(r == 0)
    def _():
        lead[...] = block[:width, :part]

    @pl.when((core == 0) & (r != 0))
    def _():
        arrived(lead, r_ld.at[0])

    @pl.when(core == 0)
    def _():
        lead_sib.start()

    @pl.when(core == 1)
    def _():
        arrived(lead, r_sib.at[0])

    lists = hall[pl.ds(pl.multiple_of(core * 8 * CAP, 8 * CAP), 8 * CAP)]
    lout[...] = choose(lists, lead[...]).reshape(8, CAP, part)

    def l_copies(act, act_here):
        for j in range(8):
            s = 2 * j + core
            as_row = s >= c
            row, col = jnp.where(as_row, s, c), jnp.where(as_row, c, s)
            kind = jnp.where(as_row, 0, 1)
            here = as_row & (s == r)

            @pl.when(jnp.logical_not(here))
            def _():
                act(remote(lout.at[j], swaps.at[kind, q], s_l.at[j], r_l.at[kind, q], row, col))

            @pl.when(here)
            def _():
                act_here(j)

    def keep_lead(j):
        swaps[0, q] = lout[j]

    l_copies(start, keep_lead)

    hot = one_hot(piv_col[...], col_start, (width, cols), 1).astype(F32)
    hit_col[...] = jnp.max(hot, axis=0, keepdims=True)
    spread[...] = hot.astype(BF16)

    def need(there):
        return 4 * there + zh <= r

    up, down, across = lax.rem(y + 1, 4), lax.rem(y + 3, 4), lax.rem(y + 2, 4)

    def y_ref(owner, k):
        j = lax.rem(zh + k, 4)
        return qr.at[2 * owner + lax.div(j, 2), slot(lax.rem(j, 2))]

    def z_copies(act):
        for d in (1, 3, 2):
            there = lax.rem(zh + d, 4)

            @pl.when(there <= r)
            def _():
                act(
                    remote(
                        y_ref(y, 0), y_ref(y, 0), s_z.at[d], r_z.at[(4 - d) % 4], r, 4 * y + there
                    )
                )

    def y_copies(k, act):
        onward = need(across)

        def one(way, to):
            ref = y_ref(y, k)
            act(remote(ref, ref, s_y.at[way, k], r_y.at[y, k], r, 4 * to + zh))

        @pl.when(need(up) | onward if k % 2 == 0 else need(up))
        def _():
            one(0, up)

        @pl.when(need(down) | onward if k % 2 == 1 else need(down))
        def _():
            one(1, down)

    def relay(k, act):
        owner, to = (down, up) if k % 2 == 0 else (up, down)
        ref = y_ref(owner, k)

        @pl.when(need(to))
        def _():
            act(remote(ref, ref, s_r.at[k], r_y.at[owner, k], r, 4 * to + zh))

    def run_relay(k):
        owner, to = (down, up) if k % 2 == 0 else (up, down)

        @pl.when(need(y) | need(to))
        def _():
            arrived(y_ref(owner, k), r_y.at[owner, k])

        relay(k, start)

    def run_y(k):
        @pl.when(zh <= r)
        def _():
            arrived(y_ref(y, k), r_z.at[k])

        y_copies(k, start)

    @pl.when(r != c)
    def _():
        arrived(y_ref(y, 0), r_t.at[0])

    y_copies(0, start)
    z_copies(start)

    @pl.when((c == 0) & (r != 0))
    def _():
        arrived(corner, r_w2.at[0])

    k_copies(1, start, 0)

    @pl.when(zh == 0)
    def _():
        for d in (1, 2, 3):
            arrived(w0z.at[d], r_w0.at[0, d])
        w0z[0] = w0out[...] + w0z[2]
        w0z[1] = w0z[1] + w0z[3]

        @pl.when(y != 0)
        def _():
            w0_pair.start()

    @pl.when(wanted(6 + zl))
    def _():
        arrived(qc.at[pair, slot(core)], r_b.at[core, pair])

    x_copies(start)
    forward(pair)
    for d in range(1, 4):
        p = lax.rem(q + 2 * d, 8)

        @pl.when(wanted(q))
        def _():
            arrived(qc.at[p, slot(core)], r_b.at[core, p])

        forward(p)

    @pl.when(wanted(q))
    def _():
        for d in range(1, 8):
            p = lax.rem(q + d, 8)
            arrived(wbuf.at[core, p], r_w.at[p])

    w_sib = remote(wbuf.at[core], wbuf.at[core], s_sib.at[2], r_sib.at[2], sib, c)
    v_sib = remote(vbuf.at[core], vbuf.at[core], s_sib.at[3], r_sib.at[3], sib, c)

    @pl.when(sib >= c)
    def _():
        w_sib.start()

    @pl.when(c == 0)
    def _():
        for d in (1, 2, 3):
            arrived(w0y.at[d], r_w0.at[1, d])
        w0y[0] = w0z[:2]
        total = jnp.zeros((CAP, width), F32)
        for j in range(4):
            listing = w0y[2 * (j % 2), j // 2] + w0y[2 * (j % 2) + 1, j // 2]
            hot = hall[128 * j : 128 * (j + 1)]
            total = total + sum(dot16(term, hot) for term in split(listing, 3))
        vbuf[core, q] = total
        w_copies(start, vbuf, s_v, r_v)

    @pl.when((zh == 0) & (y != 0))
    def _():
        arrived(corner, r_k.at[1])

    k_copies(1, start, 1)
    run_relay(0)
    run_y(1)
    run_y(3)

    for d in range(1, 4):
        p = lax.rem(pair + 2 * d, 8)

        @pl.when(wanted(q))
        def _():
            arrived(qc.at[p, slot(core)], r_b.at[core, p])

        forward(p)

    @pl.when(c == 0)
    def _():
        for d in range(1, 8):
            p = lax.rem(q + d, 8)
            arrived(vbuf.at[core, p], r_v.at[p])
        v_sib.start()
        arrived(vbuf.at[1 - core], r_sib.at[3])
        w0[...] = choose(hall_t[...], vbuf[...].reshape(16 * CAP, width))

    @pl.when(zh != 0)
    def _():
        arrived(corner, r_k.at[1])

    @pl.when(r < c)
    def _():
        out[...] = jnp.zeros_like(out)

    @pl.when(r >= c)
    def _():
        arrived(wbuf.at[1 - core], r_sib.at[2])
        w1 = choose(hall_t[...], wbuf[...].reshape(16 * CAP, width))
        for i, term in enumerate(split(w1, 3)):
            w1s[i] = term
        for p in range(8):
            arrived(qc.at[p, slot(1 - core)], r_b.at[1 - core, p])
        placed = [dot16(w1s[i], spread[...]) for i in range(2)]
        hit = hit_col[...] > 0
        for p in range(8):
            cut = slice(p * part, (p + 1) * part)
            value = qc[p]
            if p < width // part:
                value = jnp.where(c == 0, w0[:, cut], value)
            for j, term in enumerate(split(value, 2)):
                term = jnp.where(hit[:, cut], placed[j][:, cut], term.astype(F32))
                panel[j, :, cut] = term.astype(BF16)
        for p in range(8):
            @pl.when(p != q)
            def _():
                arrived(swaps.at[0, p], r_l.at[0, p])
        rows_in = jnp.concatenate([swaps[0, p] for p in range(8)], axis=1)
        placed = sum(dot16(term, spread[...]) for term in split(corner[...], 3))
        rows_in = jnp.where(hit, placed, rows_in)
        for j, term in enumerate(split(rows_in, 3)):
            right[j * CAP : (j + 1) * CAP] = term
        col_piv = listed(place_row, piv_row[...], order(c) * CAP, CAP)
        hot = hot16(one_hot(col_piv, col_start, (CAP, cols), 1))
        for j in range(3):
            right[(3 + j) * CAP : (4 + j) * CAP] = hot

    run_relay(1)
    run_relay(3)
    run_y(2)

    def tile_update(owner):
        row_start = r * rows + owner * tile
        hot = one_hot(left[...], row_start, (CAP, tile), 1).astype(F32)
        hit = jnp.max(hot, axis=0, keepdims=True)
        rows_t = jnp.concatenate([qr[2 * owner], qr[2 * owner + 1]], axis=1)
        near = hot16(one_hot(piv_col[...], row_start, (width, tile), 1))
        rows_t = jnp.where(hit > 0, sum(dot16(w1s[i], near) for i in range(3)), rows_t)
        rows_t = jnp.where((r == 0) & (c == 0) & (owner == 0), w0[...], rows_t)
        scaled = lax.dot_general(
            coupling[...], rows_t, (((0,), (0,)), ((), ())),
            precision=HIGHEST, preferred_element_type=F32,
        )
        s_hi, s_lo = split(scaled, 2)
        lanes = ((0,), (0,))
        change = dot16(s_hi, panel[0], lanes) + dot16(s_hi, panel[1], lanes)
        change = change + dot16(s_lo, panel[0], lanes)
        kind = jnp.where(r == c, 0, 1)
        cols_in = jnp.concatenate([swaps[kind, 2 * owner + i] for i in range(2)], axis=1)
        cols_in = jnp.where(hit > 0, 0.0, cols_in)
        hot = hot.astype(BF16)
        lhs = jnp.concatenate([hot, hot, hot] + split(cols_in, 3), axis=0)
        moved = dot16(lhs, right[...], lanes)
        at = pl.ds(pl.multiple_of(owner * tile, tile), tile)
        gone = (column(hit) > 0) | (hit_col[...] > 0)
        value = jnp.where(gone, 0.0, block[at]) + moved
        places_col = lax.broadcasted_iota(jnp.int32, (tile, cols), 1) + col_start
        below = lax.broadcasted_iota(jnp.int32, (tile, cols), 0) + row_start >= places_col
        out[at] = jnp.where(below, value - change, 0.0)

        @pl.when(c == 0)
        def _():
            out[at, :width] = jnp.where(below[:, :width], rows_t.T - change[:, :width], 0.0)

    @pl.when(r > c)
    def _():
        for p in range(8):
            arrived(swaps.at[1, p], r_l.at[1, p])

    @pl.when(r >= c)
    def _():
        tile_update(y)

    run_relay(2)

    @pl.when(r >= c)
    def _():
        for k in range(4):
            owner = up if k % 2 == 0 else down
            arrived(y_ref(owner, k), r_y.at[owner, k])

        def side(i, _):
            tile_update(jnp.where(i == 0, up, down))
            return 0

        lax.fori_loop(0, 2, side, 0)
        for k in range(4):
            arrived(y_ref(across, k), r_y.at[across, k])
        tile_update(across)

    @pl.when(zh != 0)
    def _():
        w0_copy.wait_send()

    @pl.when((zh == 0) & (y != 0))
    def _():
        w0_pair.wait_send()

    for i in range(2):
        for along in range(2):
            k_copies(i, sent, along)

    @pl.when(r == 0)
    def _():
        for p in range(1, 8):
            lead_copy(p).wait_send()

    @pl.when(core == 0)
    def _():
        lead_sib.wait_send()

    a_sib.wait_send()
    for d in range(1, 8):
        a_copy(d).wait_send()

    @pl.when(c == 0)
    def _():
        w_copies(sent, vbuf, s_v, r_v)
        v_sib.wait_send()

        @pl.when(r == 0)
        def _():
            w2_copies(sent)

    @pl.when(r != c)
    def _():
        t_copy.wait_send()

    b_copies(sent)
    x_copies(sent)
    w_copies(sent, wbuf, s_w, r_w)
    z_copies(sent)
    l_copies(sent, lambda j: None)
    for k in range(4):
        y_copies(k, sent)
        relay(k, sent)

    @pl.when(sib >= c)
    def _():
        w_sib.wait_send()
        for p in range(8):
            f_copy(p).wait_send()


def compact(matrix, piv_row, coupling):
    rows, cols = matrix.shape
    width = piv_row.shape[1]
    half, part = width // 2, cols // 8
    dma = pltpu.SemaphoreType.DMA
    vmem = pl.BlockSpec(memory_space=pltpu.VMEM)
    return pl.pallas_call(
        compact_kernel,
        out_shape=jax.ShapeDtypeStruct((rows, cols), F32),
        in_specs=[pl.BlockSpec(memory_space=pl.ANY), vmem, vmem],
        out_specs=vmem,
        scratch_shapes=[
            pltpu.VMEM((rows, cols), F32),
            pltpu.VMEM((CAP, cols), F32),
            pltpu.VMEM((16 * CAP, width), BF16),
            pltpu.VMEM((width, 16 * CAP), BF16),
            pltpu.VMEM((width, 1), jnp.int32),
            pltpu.VMEM((width, cols), BF16),
            pltpu.VMEM((1, cols), F32),
            pltpu.VMEM((2, 8, CAP, part), F32),
            pltpu.VMEM((width, part), F32),
            pltpu.VMEM((half, part), F32),
            pltpu.VMEM((2, 8, CAP, width), F32),
            pltpu.VMEM((2, 8, CAP, width), F32),
            pltpu.VMEM((CAP, 128), F32),
            pltpu.VMEM((4, CAP, 128), F32),
            pltpu.VMEM((4, 2, CAP, 128), F32),
            pltpu.VMEM((16, CAP, width), F32),
            pltpu.VMEM((CAP, width), F32),
            pltpu.VMEM((8, CAP, part), F32),
            pltpu.VMEM((2, 8, CAP, part), F32),
            pltpu.VMEM((8, width, part), F32),
            pltpu.VMEM((8, width, part), F32),
            pltpu.VMEM((3, width, width), BF16),
            pltpu.VMEM((width, width), F32),
            pltpu.VMEM((2, width, cols), BF16),
            pltpu.VMEM((6 * CAP, cols), BF16),
            pltpu.VMEM((CAP, 1), jnp.int32),
            dma((8,)), dma((8,)), dma((4,)), dma((4,)), dma((8,)), dma((1,)),
            dma((2, 6)), dma((2,)), dma((2,)), dma((2, 4)), dma((16,)), dma((1,)),
            dma((8,)), dma((8,)), dma((8,)), dma((8,)), dma((8,)), dma((2, 8)),
            dma((4,)), dma((4,)), dma((2, 8)), dma((8,)), dma((1,)), dma((1,)), dma((4,)), dma((4,)),
            dma((2, 4)), dma((4,)), dma((4, 4)),
            dma((1,)),
        ],
        compiler_params=pltpu.CompilerParams(
            collective_id=1, has_side_effects=True, vmem_limit_bytes=40 * 1024 * 1024
        ),
        name="compact",
    )(matrix, piv_row, coupling)


def per_device(matrix, pivots, coupling):
    width = coupling.shape[0]
    rows = matrix.shape[0]
    piv_row = pivots.reshape(1, width)

    def few(matrix, pivots, coupling):
        return compact(matrix, piv_row, coupling)

    def general(matrix, pivots, coupling):
        piv_col = pivots.reshape(width, 1)
        picked = pick(matrix, pivots)
        qc, qr = exchange(picked, matrix, piv_col, piv_row)
        return update(piv_col, piv_row, matrix, qc, qr, coupling)

    blocks = jnp.arange(16, dtype=jnp.int32)[:, None]
    counts = jnp.sum((piv_row // rows == blocks).astype(jnp.int32), axis=1)
    return lax.cond(jnp.max(counts) <= CAP, few, general, matrix, pivots, coupling)


def solution(mesh):
    return jax.shard_map(
        per_device,
        mesh=mesh,
        in_specs=(P("row", "col"), P(), P()),
        out_specs=P("row", "col"),
        check_vma=False,
    )
```

```python
import functools

import jax
import jax.numpy as jnp
from jax import lax
from jax.experimental import pallas as pl
from jax.experimental.pallas import tpu as pltpu
from jax.sharding import PartitionSpec as P

MESH = pl.DeviceIdType.MESH
F32 = jnp.float32
BF16 = jnp.bfloat16
HIGHEST = lax.Precision.HIGHEST
CAP = 32


def one_hot(index, start, shape, axis):
    return lax.broadcasted_iota(jnp.int32, shape, axis) + start == index


def pick_kernel(piv, matrix, picked, sem):
    rows = matrix.shape[0]
    count = picked.shape[0]
    start = lax.axis_index("row") * rows
    picked[...] = jnp.zeros_like(picked)

    def copy(k):
        local = jnp.clip(piv[k] - start, 0, rows - 1)
        return pltpu.make_async_copy(matrix.at[pl.ds(local, 1)], picked.at[pl.ds(k, 1)], sem)

    def go(k, _):
        @pl.when((piv[k] >= start) & (piv[k] < start + rows))
        def _():
            copy(k).start()

        return 0

    def wait(k, _):
        @pl.when((piv[k] >= start) & (piv[k] < start + rows))
        def _():
            copy(k).wait()

        return 0

    lax.fori_loop(0, count, go, 0)
    lax.fori_loop(0, count, wait, 0)


def pick(matrix, pivots):
    return pl.pallas_call(
        pick_kernel,
        out_shape=jax.ShapeDtypeStruct((pivots.shape[0], matrix.shape[1]), F32),
        in_specs=[pl.BlockSpec(memory_space=pltpu.SMEM), pl.BlockSpec(memory_space=pl.ANY)],
        out_specs=pl.BlockSpec(memory_space=pltpu.VMEM),
        scratch_shapes=[pltpu.SemaphoreType.DMA],
        name="pick",
    )(pivots, matrix)


def exchange_kernel(
    picked, matrix, piv_col, piv_row, qc, qr,
    a1buf, sums, a2buf, raw, piece, corner, w0buf, w0mine,
    s_a1, r_a1, s_a2, r_a2, s_ld, r_ld, s_w, r_w, s_w0, r_w0,
    s_b, r_b, s_f, s_t, r_t, s_y, r_y, local,
):
    r, c = lax.axis_index("row"), lax.axis_index("col")
    width, cols = picked.shape
    own = raw.shape[1]
    q, core = lax.div(r, 2), lax.rem(r, 2)
    x, y, zh = lax.div(r, 4), lax.div(c, 4), lax.rem(c, 4)
    sib = r + 1 - 2 * core
    col_start = c * cols

    def remote(src, dst, ssem, rsem, row, col):
        return pltpu.make_async_remote_copy(
            src_ref=src, dst_ref=dst, send_sem=ssem, recv_sem=rsem,
            device_id=(row, col), device_id_type=MESH,
        )

    def arrived(dst, rsem):
        remote(dst, dst, rsem, rsem, sib, c).wait_recv()

    def signal(row, col):
        pl.semaphore_signal(barrier, inc=1, device_id=(row, col), device_id_type=MESH)

    def slots(g, n=1):
        return pl.ds(pl.multiple_of(g * own, own), n * own)

    barrier = pltpu.get_barrier_semaphore()
    for d in range(1, 16):
        signal(lax.rem(r + d, 16), c)
    for d in range(1, 4):
        signal(r, lax.rem(y + d, 4) * 4 + zh)
    for j in range(4):
        @pl.when((r != c) | (4 * y + j != r))
        def _():
            signal(4 * y + j, r)

    @pl.when(c != 0)
    def _():
        signal(r, 0)

    @pl.when(c == 0)
    def _():
        for b in range(1, 16):
            signal(r, b)

    greeted = 15 + 3 + 4 - jnp.where(r == c, 1, 0) + jnp.where(c == 0, 15, 1)
    pl.semaphore_wait(barrier, greeted)

    def lead_copies(act):
        @pl.when(r == 0)
        def _():
            for g in range(1, 16):
                act(remote(matrix.at[slots(g)], raw.at[1], s_ld.at[g], r_ld.at[0], g, c))
            act(pltpu.make_async_copy(matrix.at[slots(0)], raw.at[1], local.at[0]))

    lead_copies(lambda copy: copy.start())

    def a1(p):
        return remote(
            picked.at[slots(2 * p + 1 - core)], a1buf.at[p], s_a1.at[p], r_a1.at[p], sib, c
        )

    def a2(p):
        return remote(sums.at[p], a2buf.at[q], s_a2.at[p], r_a2.at[q], 2 * p + core, c)

    for d in range(1, 9):
        a1(lax.rem(q + d, 8)).start()
    for d in range(1, 9):
        p = lax.rem(q + d, 8)
        arrived(a1buf.at[p], r_a1.at[p])
        total = picked[slots(2 * p + core)] + a1buf[p]
        if d < 8:
            sums[p] = total
            a2(p).start()
        else:
            a2buf[q] = total

    hot_t = one_hot(piv_col[...], col_start, (width, cols), 1).astype(F32)
    swapped = jnp.max(hot_t, axis=0, keepdims=True) > 0

    def fixed(part):
        placed = jnp.dot(corner[part], hot_t, precision=HIGHEST, preferred_element_type=F32)
        return jnp.where(swapped, placed, raw[part])

    def send_corner(part, act):
        for b in range(1, 16):
            act(remote(corner.at[part], corner.at[part], s_w.at[part, b], r_w.at[part], r, b))

    def get_corner(part):
        @pl.when(c == 0)
        def _():
            corner[part] = raw[part, :, :width]
            send_corner(part, lambda copy: copy.start())

        @pl.when(c != 0)
        def _():
            arrived(corner.at[part], r_w.at[part])

    def b_copy(part, d):
        p = lax.rem(q + d, 8)
        return p, remote(
            piece.at[part], qc.at[part, slots(r)], s_b.at[part, d], r_b.at[part, r], 2 * p + core, c
        )

    def b_copies(part, act):
        for d in range(1, 8):
            p, copy = b_copy(part, d)

            @pl.when(2 * p + 1 >= c)
            def _():
                act(copy)

    def f_copy(part, d):
        if d == 0:
            return remote(
                piece.at[part], qc.at[part, slots(r)], s_f.at[part, 0], r_b.at[part, r], sib, c
            )
        g = 2 * lax.rem(q + d, 8) + core
        return remote(
            qc.at[part, slots(g)], qc.at[part, slots(g)], s_f.at[part, d], r_b.at[part, g], sib, c
        )

    def t_copies(part, act):
        for k in range(4):
            col = 4 * x + k
            here = (r == c) & (k == zh)

            @pl.when(jnp.logical_not(here))
            def _():
                act(
                    remote(
                        piece.at[part], qr.at[part, slots(r)],
                        s_t.at[part, k], r_t.at[part, lax.rem(r, 4)], c, col,
                    )
                )

            @pl.when(here)
            def _():
                act(
                    pltpu.make_async_copy(
                        piece.at[part], qr.at[part, slots(r)], local.at[3 + part]
                    )
                )

    def send_piece(part):
        b_copies(part, lambda copy: copy.start())
        t_copies(part, lambda copy: copy.start())

        @pl.when(sib >= c)
        def _():
            f_copy(part, 0).start()

        pltpu.make_async_copy(piece.at[part], qc.at[part, slots(r)], local.at[1 + part]).start()

    @pl.when(r == 0)
    def _():
        pltpu.make_async_copy(matrix.at[slots(0)], raw.at[1], local.at[0]).wait()

    @pl.when(r != 0)
    def _():
        arrived(raw.at[1], r_ld.at[0])

    get_corner(1)
    piece[1] = fixed(1)
    send_piece(1)

    for d in range(1, 8):
        p = lax.rem(q + d, 8)
        arrived(a2buf.at[p], r_a2.at[p])
    total = a2buf[0]
    for p in range(1, 8):
        total = total + a2buf[p]
    raw[0] = total
    get_corner(0)
    hot = one_hot(piv_row[...], col_start, (cols, width), 0).astype(F32)
    mine = jnp.dot(total, hot, precision=HIGHEST, preferred_element_type=F32)

    def w0_copy(col):
        return remote(w0mine, w0buf.at[col], s_w0.at[0], r_w0.at[col], r, 0)

    @pl.when(c != 0)
    def _():
        w0mine[...] = mine
        w0_copy(c).start()

    piece[0] = fixed(0)

    @pl.when(c == 0)
    def _():
        w0 = mine
        for b in range(1, 16):
            arrived(w0buf.at[b], r_w0.at[b])
            w0 = w0 + w0buf[b]
        piece[0, :, :width] = w0

    send_piece(0)

    def y_copies(part, act):
        for d in range(1, 4):
            col = lax.rem(y + d, 4) * 4 + zh

            @pl.when(col <= r)
            def _():
                block = qr.at[part, slots(4 * y, 4)]
                act(remote(block, block, s_y.at[part, d], r_y.at[part, y], r, col))

    def run_y(part):
        for j in range(4):
            here = (r == c) & (4 * y + j == r)

            @pl.when(jnp.logical_not(here))
            def _():
                arrived(qr.at[part, slots(4 * y + j)], r_t.at[part, j])

            @pl.when(here)
            def _():
                pltpu.make_async_copy(
                    piece.at[part], qr.at[part, slots(r)], local.at[3 + part]
                ).wait()

        y_copies(part, lambda copy: copy.start())

    def run_f(part):
        for d in range(1, 8):
            g = 2 * lax.rem(q + d, 8) + core

            @pl.when(2 * q + 1 >= c)
            def _():
                arrived(qc.at[part, slots(g)], r_b.at[part, g])

            @pl.when(sib >= c)
            def _():
                f_copy(part, d).start()

    run_y(1)
    run_y(0)
    run_f(1)
    run_f(0)

    for part in (1, 0):
        for d in range(8):
            g = 2 * lax.rem(q + d, 8) + 1 - core

            @pl.when(r >= c)
            def _():
                arrived(qc.at[part, slots(g)], r_b.at[part, g])

        for d in range(1, 4):
            there = lax.rem(y + d, 4)

            @pl.when(c <= r)
            def _():
                arrived(qr.at[part, slots(4 * there, 4)], r_y.at[part, there])

        pltpu.make_async_copy(piece.at[part], qc.at[part, slots(r)], local.at[1 + part]).wait()

    lead_copies(lambda copy: copy.wait_send() if copy.is_remote else None)
    for d in range(1, 9):
        a1(lax.rem(q + d, 8)).wait_send()
    for d in range(1, 8):
        a2(lax.rem(q + d, 8)).wait_send()

    @pl.when(c != 0)
    def _():
        w0_copy(c).wait_send()

    for part in (1, 0):
        @pl.when(c == 0)
        def _():
            send_corner(part, lambda copy: copy.wait_send())

        b_copies(part, lambda copy: copy.wait_send())
        t_copies(part, lambda copy: copy.wait_send() if copy.is_remote else None)
        y_copies(part, lambda copy: copy.wait_send())

        @pl.when(sib >= c)
        def _():
            for d in range(8):
                f_copy(part, d).wait_send()


def exchange(picked, matrix, piv_col, piv_row):
    width, cols = picked.shape
    own = width // 16
    dma = pltpu.SemaphoreType.DMA
    out = jax.ShapeDtypeStruct((2, width, cols), F32)
    any_spec = pl.BlockSpec(memory_space=pl.ANY)
    vmem = pl.BlockSpec(memory_space=pltpu.VMEM)
    return pl.pallas_call(
        exchange_kernel,
        out_shape=(out, out),
        in_specs=[vmem, any_spec, vmem, vmem],
        out_specs=(any_spec, any_spec),
        scratch_shapes=[
            pltpu.VMEM((8, own, cols), F32),
            pltpu.VMEM((8, own, cols), F32),
            pltpu.VMEM((8, own, cols), F32),
            pltpu.VMEM((2, own, cols), F32),
            pltpu.VMEM((2, own, cols), F32),
            pltpu.VMEM((2, own, width), F32),
            pltpu.VMEM((16, own, width), F32),
            pltpu.VMEM((own, width), F32),
            dma((8,)), dma((8,)), dma((8,)), dma((8,)),
            dma((16,)), dma((1,)), dma((2, 16)), dma((2,)), dma((1,)), dma((16,)),
            dma((2, 8)), dma((2, 16)), dma((2, 8)), dma((2, 4)), dma((2, 4)), dma((2, 4)), dma((2, 4)),
            dma((5,)),
        ],
        compiler_params=pltpu.CompilerParams(
            collective_id=0, has_side_effects=True, vmem_limit_bytes=32 * 1024 * 1024
        ),
        name="exchange",
    )(picked, matrix, piv_col, piv_row)


def split(value, n):
    terms = []
    for _ in range(n):
        term = value.astype(BF16)
        terms.append(term)
        value = value - term.astype(F32)
    return terms


def update_kernel(piv_col, piv_row, m, qc, qr, coupling, out, hot_t, panel, lead):
    r, c = lax.axis_index("row"), lax.axis_index("col")
    tile, cols = out.shape
    width = coupling.shape[0]
    step = pl.program_id(0)
    row_start = r * cols + step * tile
    col_start = c * cols

    @pl.when(r < c)
    def _():
        out[...] = jnp.zeros_like(out)

    @pl.when((r >= c) & (step == 0))
    def _():
        hot_t[...] = one_hot(piv_col[...], col_start, (width, cols), 1).astype(BF16)
        for i, term in enumerate(split(qc[0], 2)):
            panel[i] = term
        for i, term in enumerate(split(qc[1], 3)):
            lead[i] = term

    def dot(a, b):
        return jnp.dot(a, b, preferred_element_type=F32)

    @pl.when(r >= c)
    def _():
        panel_rows = qr[0].T
        scaled = jnp.dot(panel_rows, coupling[...], precision=HIGHEST, preferred_element_type=F32)
        s_hi, s_lo = split(scaled, 2)
        update = dot(s_hi, panel[0]) + dot(s_hi, panel[1]) + dot(s_lo, panel[0])
        hot = one_hot(piv_row[...], row_start, (tile, width), 0)
        hit_row = jnp.max(hot.astype(F32), axis=1, keepdims=True) > 0
        hit_col = jnp.max(hot_t[...].astype(F32), axis=0, keepdims=True) > 0
        hot = hot.astype(F32).astype(BF16)
        new_rows = dot(hot, lead[0]) + dot(hot, lead[1]) + dot(hot, lead[2])
        lead_cols = jnp.where(hit_row, 0.0, qr[1].T)
        new_cols = sum(dot(term, hot_t[...]) for term in split(lead_cols, 3))
        value = jnp.where(hit_row | hit_col, 0.0, m[...]) + new_rows + new_cols
        spread = jnp.concatenate([panel_rows, jnp.zeros((tile, cols - width), F32)], axis=1)
        places = lax.broadcasted_iota(jnp.int32, (tile, cols), 1)
        value = jnp.where((places < width) & (c == 0), spread, value)
        below = lax.broadcasted_iota(jnp.int32, (tile, cols), 0) + row_start >= places + col_start
        out[...] = jnp.where(below, value - update, 0.0)


def update(piv_col, piv_row, matrix, qc, qr, coupling):
    rows, cols = matrix.shape
    width = coupling.shape[0]
    tile = min(rows, 256)

    def whole(shape):
        return pl.BlockSpec(shape, lambda i: (0,) * len(shape))

    return pl.pallas_call(
        update_kernel,
        grid=(rows // tile,),
        out_shape=jax.ShapeDtypeStruct((rows, cols), F32),
        in_specs=[
            whole((width, 1)),
            whole((1, width)),
            pl.BlockSpec((tile, cols), lambda i: (i, 0)),
            whole((2, width, cols)),
            pl.BlockSpec((2, width, tile), lambda i: (0, 0, i)),
            whole((width, width)),
        ],
        out_specs=pl.BlockSpec((tile, cols), lambda i: (i, 0)),
        scratch_shapes=[
            pltpu.VMEM((width, cols), BF16),
            pltpu.VMEM((2, width, cols), BF16),
            pltpu.VMEM((3, width, cols), BF16),
        ],
        compiler_params=pltpu.CompilerParams(vmem_limit_bytes=48 * 1024 * 1024),
        name="update",
    )(piv_col, piv_row, matrix, qc, qr, coupling)


def order(s):
    return lax.rem(s, 2) * 8 + lax.div(s, 2)


def blocks_of(piv, rows):
    block = jnp.right_shift(piv, rows.bit_length() - 1)
    return jnp.bitwise_and(block, 1) * 8 + jnp.right_shift(block, 1)


def column(row):
    return jnp.broadcast_to(row, (8, row.shape[1])).T[:, :1]


def places(piv_row, rows):
    width = piv_row.shape[1]
    first = lax.broadcasted_iota(jnp.int32, (width, width), 0)
    second = lax.broadcasted_iota(jnp.int32, (width, width), 1)
    block_row = blocks_of(piv_row, rows)
    before = (column(block_row) == block_row) & (first < second)
    return block_row * CAP + jnp.sum(jnp.where(before, 1, 0), axis=0, keepdims=True)


def listed(place_row, piv_row, start, count):
    spot = lax.broadcasted_iota(jnp.int32, (count, place_row.shape[1]), 0) + start
    return jnp.sum(jnp.where(spot == place_row, piv_row + 1, 0), axis=1, keepdims=True) - 1


def hot16(mask):
    return mask.astype(F32).astype(BF16)


def dot16(a, b, dims=((1,), (0,))):
    return lax.dot_general(a, b, (dims, ((), ())), preferred_element_type=F32)


def choose(hot, value):
    return sum(dot16(hot, term) for term in split(value, 3))


def compact_kernel(
    matrix, piv_row, coupling, out,
    block, picked, hall, hall_t, piv_col, spread, hit_col,
    abuf, lead, piece, wbuf, vbuf, w0out, w0z, w0y, w2out, corner, lout, swaps, qc, qr,
    w1s, w0, panel, right, left,
    s_a, r_a, s_sib, r_sib, s_ld, r_ld, s_k, r_k, s_w0, r_w0, s_w2, r_w2, s_w, r_w, s_v, r_v,
    s_l, r_l, s_b, s_x, r_b, s_f, s_t, r_t, s_z, r_z, s_y, s_r, r_y, local,
):
    r, c = lax.axis_index("row"), lax.axis_index("col")
    rows, cols = matrix.shape
    width = piv_row.shape[1]
    half, part = width // 2, cols // 8
    tile = 2 * part
    q, core = lax.div(r, 2), lax.rem(r, 2)
    zl = lax.rem(q, 2)
    x, y, zh = lax.div(r, 4), lax.div(c, 4), lax.rem(c, 4)
    sib = r + 1 - 2 * core
    pair = q + 1 - 2 * zl
    chunk = lax.div(order(c), 4)
    col_start = c * cols

    def remote(src, dst, ssem, rsem, row, col):
        return pltpu.make_async_remote_copy(
            src_ref=src, dst_ref=dst, send_sem=ssem, recv_sem=rsem,
            device_id=(row, col), device_id_type=MESH,
        )

    def arrived(dst, rsem):
        remote(dst, dst, rsem, rsem, sib, c).wait_recv()

    def start(copy):
        copy.start()

    def sent(copy):
        copy.wait_send()

    load = pltpu.make_async_copy(matrix, block, local.at[0])
    load.start()

    barrier = pltpu.get_barrier_semaphore()

    def signal(row, col):
        pl.semaphore_signal(barrier, inc=1, device_id=(row, col), device_id_type=MESH)

    for d in (1, 2, 3):
        signal(r, lax.rem(y + d, 4) * 4 + zh)
    for d in (1, 2, 3):
        signal(r, 4 * y + lax.rem(zh + d, 4))

    @pl.when(r != c)
    def _():
        signal(c, r)

    @pl.when(r > c)
    def _():
        for j in range(8):
            signal(2 * j + lax.rem(c, 2), r)

    for d in range(1, 16):
        signal(lax.rem(r + d, 16), c)

    greeted = 15 + 3 + 3 + jnp.where(r == c, 0, 1)
    greeted = greeted + lax.div(c - core + 1, 2)

    place_row = places(piv_row[...], rows)
    piv_col[...] = column(piv_row[...])
    spots = lax.broadcasted_iota(jnp.int32, (16 * CAP, width), 0)
    hall[...] = hot16(spots == place_row)
    spots = lax.broadcasted_iota(jnp.int32, (width, 16 * CAP), 1)
    hall_t[...] = hot16(spots == column(place_row))
    mine = order(r) * CAP
    left[...] = listed(place_row, piv_row[...], mine, CAP)
    load.wait()
    for t in range(CAP):
        local_row = jnp.sum(jnp.where(place_row == mine + t, piv_row[...] - r * rows, 0))
        picked[pl.ds(t, 1)] = block[pl.ds(jnp.clip(local_row, 0, rows - 1), 1)]
    picked[...] = jnp.where(left[...] >= 0, picked[...], 0.0)

    @pl.when(c == 0)
    def _():
        wbuf[core, q] = picked[:, :width]

    pl.semaphore_wait(barrier, greeted)

    def a_copy(d):
        p = lax.rem(q + d, 8)
        cut = pl.ds(pl.multiple_of(p * part, part), part)
        return remote(picked.at[:, cut], abuf.at[core, q], s_a.at[d], r_a.at[q], 2 * p + core, c)

    for d in range(1, 8):
        a_copy(d).start()

    def k_copies(i, act, along):
        src = wbuf.at[core, q] if i == 0 else corner

        @pl.when((c == 0) if along == 0 else (zh == 0))
        def _():
            for d in (1, 2, 3):
                col = 4 * d if along == 0 else 4 * y + d
                act(remote(src, src, s_k.at[i, 3 * along + d - 1], r_k.at[i], r, col))

    k_copies(0, start, 0)

    def lead_copy(p):
        return remote(
            block.at[pl.ds(0, width), pl.ds(p * part, part)], lead, s_ld.at[p], r_ld.at[0], 2 * p, c
        )

    @pl.when(r == 0)
    def _():
        for p in range(1, 8):
            lead_copy(p).start()

    abuf[core, q] = picked[:, pl.ds(pl.multiple_of(q * part, part), part)]

    def w2_copies(act):
        for s in range(1, 16):
            src = w2out.at[(s % 2) * 8 + s // 2]
            act(remote(src, corner, s_w2.at[s], r_w2.at[0], s, 0))

    @pl.when((r == 0) & (c == 0))
    def _():
        w2out[...] = choose(hall[...], block[:width, :width]).reshape(16, CAP, width)
        w2_copies(start)
        corner[...] = w2out[0]

    w0_copy = remote(w0out, w0z.at[zh], s_w0.at[0], r_w0.at[0, zh], r, 4 * y)
    w0_pair = remote(w0z.at[pl.ds(0, 2)], w0y.at[y], s_w0.at[1], r_w0.at[1, y], r, 0)

    here_piv = listed(place_row, piv_row[...], chunk * 128, 128)
    near = hot16(one_hot(here_piv, col_start, (128, cols), 1))
    w0out[...] = sum(dot16(term, near, ((1,), (1,))) for term in split(picked[...], 3))

    @pl.when(zh != 0)
    def _():
        w0_copy.start()

    for d in range(1, 8):
        p = lax.rem(q + d, 8)
        arrived(abuf.at[core, p], r_a.at[p])
    a_sib = remote(abuf.at[core], abuf.at[core], s_sib.at[1], r_sib.at[1], sib, c)
    a_sib.start()
    arrived(abuf.at[1 - core], r_sib.at[1])

    def slot(k):
        return pl.ds(pl.multiple_of(k * half, half), half)

    piece[...] = choose(hall_t[slot(core)], abuf[...].reshape(16 * CAP, part))

    t_copy = remote(piece, qr.at[q, slot(core)], s_t.at[0], r_t.at[0], c, r)

    @pl.when(r != c)
    def _():
        t_copy.start()

    @pl.when(r == c)
    def _():
        qr[q, slot(core)] = piece[...]

    def wanted(p):
        return 2 * p + 1 >= c

    def b_copies(act):
        @pl.when(wanted(6 + 1 - zl))
        def _():
            act(
                remote(piece, qc.at[q, slot(core)], s_b.at[0], r_b.at[core, q], 2 * pair + core, c)
            )

        for d in range(1, 4):
            p = lax.rem(q + 2 * d, 8)

            @pl.when(wanted(p))
            def _():
                act(remote(piece, qc.at[q, slot(core)], s_b.at[d], r_b.at[core, q], 2 * p + core, c))

    def x_copies(act):
        for d in range(1, 4):
            p = lax.rem(q + 2 * d, 8)
            ref = qc.at[pair, slot(core)]

            @pl.when(wanted(p))
            def _():
                act(remote(ref, ref, s_x.at[d], r_b.at[core, pair], 2 * p + core, c))

    def f_copy(p):
        ref = qc.at[p, slot(core)]
        return remote(ref, ref, s_f.at[p], r_b.at[core, p], sib, c)

    def forward(p):
        @pl.when(sib >= c)
        def _():
            f_copy(p).start()

    b_copies(start)
    qc[q, slot(core)] = piece[...]
    forward(q)

    def w_copies(act, buf, ssem, rsem):
        for d in range(1, 8):
            p = lax.rem(q + d, 8)

            @pl.when(wanted(p))
            def _():
                act(
                    remote(buf.at[core, q], buf.at[core, q], ssem.at[d], rsem.at[q], 2 * p + core, c)
                )

    @pl.when(c != 0)
    def _():
        arrived(wbuf.at[core, q], r_k.at[0])

    k_copies(0, start, 1)
    w_copies(start, wbuf, s_w, r_w)

    hot = one_hot(piv_col[...], col_start, (width, cols), 1).astype(F32)
    hit_col[...] = jnp.max(hot, axis=0, keepdims=True)
    spread[...] = hot.astype(BF16)

    def need(there):
        return 4 * there + zh <= r

    up, down, across = lax.rem(y + 1, 4), lax.rem(y + 3, 4), lax.rem(y + 2, 4)

    def y_ref(owner, k):
        j = lax.rem(zh + k, 4)
        return qr.at[2 * owner + lax.div(j, 2), slot(lax.rem(j, 2))]

    def z_copies(act):
        for d in (1, 3, 2):
            there = lax.rem(zh + d, 4)

            @pl.when(there <= r)
            def _():
                act(
                    remote(
                        y_ref(y, 0), y_ref(y, 0), s_z.at[d], r_z.at[(4 - d) % 4], r, 4 * y + there
                    )
                )

    def relays(node, k, way):
        off = lax.rem(node + 4 - x, 4)
        return (off == 2) | ((off != 0) & (way == k % 2))

    def y_copies(k, act):
        for way, to in ((0, up), (1, down)):
            ref = y_ref(y, k)

            @pl.when(need(to) | (need(across) & relays(to, k, way)))
            def _():
                act(remote(ref, ref, s_y.at[way, k], r_y.at[y, k], r, 4 * to + zh))

    def relay(k, act):
        for way, owner, to in ((0, down, up), (1, up, down)):
            ref = y_ref(owner, k)

            @pl.when(need(to) & relays(y, k, way))
            def _():
                act(remote(ref, ref, s_r.at[way, k], r_y.at[owner, k], r, 4 * to + zh))

    def run_relay(k):
        for way, owner, to in ((0, down, up), (1, up, down)):
            @pl.when(relays(y, k, way) & (need(y) | need(to)))
            def _():
                arrived(y_ref(owner, k), r_y.at[owner, k])

        relay(k, start)

    def run_y(k):
        @pl.when(zh <= r)
        def _():
            arrived(y_ref(y, k), r_z.at[k])

        y_copies(k, start)

    @pl.when((c == 0) & (r != 0))
    def _():
        arrived(corner, r_w2.at[0])

    k_copies(1, start, 0)

    @pl.when(zh == 0)
    def _():
        for d in (1, 2, 3):
            arrived(w0z.at[d], r_w0.at[0, d])
        w0z[0] = w0out[...] + w0z[2]
        w0z[1] = w0z[1] + w0z[3]

        @pl.when(y != 0)
        def _():
            w0_pair.start()

    @pl.when(r != c)
    def _():
        arrived(y_ref(y, 0), r_t.at[0])

    y_copies(0, start)
    z_copies(start)

    @pl.when(wanted(6 + zl))
    def _():
        arrived(qc.at[pair, slot(core)], r_b.at[core, pair])

    x_copies(start)
    forward(pair)
    run_relay(0)

    @pl.when(c == 0)
    def _():
        for d in (1, 2, 3):
            arrived(w0y.at[d], r_w0.at[1, d])
        w0y[0] = w0z[:2]
        total = jnp.zeros((CAP, width), F32)
        for j in range(4):
            listing = w0y[2 * (j % 2), j // 2] + w0y[2 * (j % 2) + 1, j // 2]
            hot = hall[128 * j : 128 * (j + 1)]
            total = total + sum(dot16(term, hot) for term in split(listing, 3))
        vbuf[core, q] = total
        w_copies(start, vbuf, s_v, r_v)

    run_y(1)
    run_y(3)
    lead_sib = remote(lead, lead, s_sib.at[0], r_sib.at[0], sib, c)

    @pl.when(r == 0)
    def _():
        lead[...] = block[:width, :part]

    @pl.when((core == 0) & (r != 0))
    def _():
        arrived(lead, r_ld.at[0])

    @pl.when(core == 0)
    def _():
        lead_sib.start()

    @pl.when(core == 1)
    def _():
        arrived(lead, r_sib.at[0])

    lists = hall[pl.ds(pl.multiple_of(core * 8 * CAP, 8 * CAP), 8 * CAP)]
    lout[...] = choose(lists, lead[...]).reshape(8, CAP, part)

    def l_copies(act, act_here):
        for d in range(8):
            j = lax.rem(q + d, 8)
            s = 2 * j + core
            as_row = s >= c
            row, col = jnp.where(as_row, s, c), jnp.where(as_row, c, s)
            kind = jnp.where(as_row, 0, 1)
            here = as_row & (s == r)

            @pl.when(jnp.logical_not(here))
            def _():
                act(remote(lout.at[j], swaps.at[kind, q], s_l.at[j], r_l.at[kind, q], row, col))

            @pl.when(here)
            def _():
                act_here(j)

    def keep_lead(j):
        swaps[0, q] = lout[j]

    l_copies(start, keep_lead)


    w_sib = remote(wbuf.at[core], wbuf.at[core], s_sib.at[2], r_sib.at[2], sib, c)
    v_sib = remote(vbuf.at[core], vbuf.at[core], s_sib.at[3], r_sib.at[3], sib, c)

    @pl.when((zh == 0) & (y != 0))
    def _():
        arrived(corner, r_k.at[1])

    k_copies(1, start, 1)
    for d in range(1, 4):
        p = lax.rem(q + 2 * d, 8)

        @pl.when(wanted(q))
        def _():
            arrived(qc.at[p, slot(core)], r_b.at[core, p])

        forward(p)

    @pl.when(wanted(q))
    def _():
        for d in range(1, 8):
            p = lax.rem(q + d, 8)
            arrived(wbuf.at[core, p], r_w.at[p])

    @pl.when(sib >= c)
    def _():
        w_sib.start()

    run_relay(1)
    run_relay(3)
    run_y(2)

    for d in range(1, 4):
        p = lax.rem(pair + 2 * d, 8)

        @pl.when(wanted(q))
        def _():
            arrived(qc.at[p, slot(core)], r_b.at[core, p])

        forward(p)

    @pl.when(c == 0)
    def _():
        for d in range(1, 8):
            p = lax.rem(q + d, 8)
            arrived(vbuf.at[core, p], r_v.at[p])
        v_sib.start()
        arrived(vbuf.at[1 - core], r_sib.at[3])
        w0[...] = choose(hall_t[...], vbuf[...].reshape(16 * CAP, width))

    @pl.when(zh != 0)
    def _():
        arrived(corner, r_k.at[1])

    @pl.when(r < c)
    def _():
        out[...] = jnp.zeros_like(out)

    @pl.when(r >= c)
    def _():
        arrived(wbuf.at[1 - core], r_sib.at[2])
        w1 = choose(hall_t[...], wbuf[...].reshape(16 * CAP, width))
        for i, term in enumerate(split(w1, 3)):
            w1s[i] = term
        for p in range(8):
            arrived(qc.at[p, slot(1 - core)], r_b.at[1 - core, p])
        placed = [dot16(w1s[i], spread[...]) for i in range(2)]
        hit = hit_col[...] > 0
        for p in range(8):
            cut = slice(p * part, (p + 1) * part)
            value = qc[p]
            if p < width // part:
                value = jnp.where(c == 0, w0[:, cut], value)
            for j, term in enumerate(split(value, 2)):
                term = jnp.where(hit[:, cut], placed[j][:, cut], term.astype(F32))
                panel[j, :, cut] = term.astype(BF16)
        for p in range(8):
            @pl.when(p != q)
            def _():
                arrived(swaps.at[0, p], r_l.at[0, p])
        rows_in = jnp.concatenate([swaps[0, p] for p in range(8)], axis=1)
        placed = sum(dot16(term, spread[...]) for term in split(corner[...], 3))
        rows_in = jnp.where(hit, placed, rows_in)
        for j, term in enumerate(split(rows_in, 3)):
            right[j * CAP : (j + 1) * CAP] = term
        col_piv = listed(place_row, piv_row[...], order(c) * CAP, CAP)
        hot = hot16(one_hot(col_piv, col_start, (CAP, cols), 1))
        for j in range(3):
            right[(3 + j) * CAP : (4 + j) * CAP] = hot


    def tile_update(owner):
        row_start = r * rows + owner * tile
        hot = one_hot(left[...], row_start, (CAP, tile), 1).astype(F32)
        hit = jnp.max(hot, axis=0, keepdims=True)
        rows_t = jnp.concatenate([qr[2 * owner], qr[2 * owner + 1]], axis=1)
        near = hot16(one_hot(piv_col[...], row_start, (width, tile), 1))
        rows_t = jnp.where(hit > 0, sum(dot16(w1s[i], near) for i in range(3)), rows_t)
        rows_t = jnp.where((r == 0) & (c == 0) & (owner == 0), w0[...], rows_t)
        scaled = lax.dot_general(
            coupling[...], rows_t, (((0,), (0,)), ((), ())),
            precision=HIGHEST, preferred_element_type=F32,
        )
        s_hi, s_lo = split(scaled, 2)
        lanes = ((0,), (0,))
        change = dot16(s_hi, panel[0], lanes) + dot16(s_hi, panel[1], lanes)
        change = change + dot16(s_lo, panel[0], lanes)
        kind = jnp.where(r == c, 0, 1)
        cols_in = jnp.concatenate([swaps[kind, 2 * owner + i] for i in range(2)], axis=1)
        cols_in = jnp.where(hit > 0, 0.0, cols_in)
        hot = hot.astype(BF16)
        lhs = jnp.concatenate([hot, hot, hot] + split(cols_in, 3), axis=0)
        moved = dot16(lhs, right[...], lanes)
        at = pl.ds(pl.multiple_of(owner * tile, tile), tile)
        gone = (column(hit) > 0) | (hit_col[...] > 0)
        value = jnp.where(gone, 0.0, block[at]) + moved
        places_col = lax.broadcasted_iota(jnp.int32, (tile, cols), 1) + col_start
        below = lax.broadcasted_iota(jnp.int32, (tile, cols), 0) + row_start >= places_col
        out[at] = jnp.where(below, value - change, 0.0)

        @pl.when(c == 0)
        def _():
            out[at, :width] = jnp.where(below[:, :width], rows_t.T - change[:, :width], 0.0)

    @pl.when(r > c)
    def _():
        for p in range(8):
            arrived(swaps.at[1, p], r_l.at[1, p])

    @pl.when(r >= c)
    def _():
        tile_update(y)

    run_relay(2)

    @pl.when(r >= c)
    def _():
        for k in range(4):
            for way, owner in ((0, down), (1, up)):
                @pl.when(jnp.logical_not(relays(y, k, way)))
                def _():
                    arrived(y_ref(owner, k), r_y.at[owner, k])

        def side(i, _):
            tile_update(jnp.where(i == 0, up, down))
            return 0

        lax.fori_loop(0, 2, side, 0)
        for k in range(4):
            arrived(y_ref(across, k), r_y.at[across, k])
        tile_update(across)

    @pl.when(zh != 0)
    def _():
        w0_copy.wait_send()

    @pl.when((zh == 0) & (y != 0))
    def _():
        w0_pair.wait_send()

    for i in range(2):
        for along in range(2):
            k_copies(i, sent, along)

    @pl.when(r == 0)
    def _():
        for p in range(1, 8):
            lead_copy(p).wait_send()

    @pl.when(core == 0)
    def _():
        lead_sib.wait_send()

    a_sib.wait_send()
    for d in range(1, 8):
        a_copy(d).wait_send()

    @pl.when(c == 0)
    def _():
        w_copies(sent, vbuf, s_v, r_v)
        v_sib.wait_send()

        @pl.when(r == 0)
        def _():
            w2_copies(sent)

    @pl.when(r != c)
    def _():
        t_copy.wait_send()

    b_copies(sent)
    x_copies(sent)
    w_copies(sent, wbuf, s_w, r_w)
    z_copies(sent)
    l_copies(sent, lambda j: None)
    for k in range(4):
        y_copies(k, sent)
        relay(k, sent)

    @pl.when(sib >= c)
    def _():
        w_sib.wait_send()
        for p in range(8):
            f_copy(p).wait_send()


def compact(matrix, piv_row, coupling):
    rows, cols = matrix.shape
    width = piv_row.shape[1]
    half, part = width // 2, cols // 8
    dma = pltpu.SemaphoreType.DMA
    vmem = pl.BlockSpec(memory_space=pltpu.VMEM)
    return pl.pallas_call(
        compact_kernel,
        out_shape=jax.ShapeDtypeStruct((rows, cols), F32),
        in_specs=[pl.BlockSpec(memory_space=pl.ANY), vmem, vmem],
        out_specs=vmem,
        scratch_shapes=[
            pltpu.VMEM((rows, cols), F32),
            pltpu.VMEM((CAP, cols), F32),
            pltpu.VMEM((16 * CAP, width), BF16),
            pltpu.VMEM((width, 16 * CAP), BF16),
            pltpu.VMEM((width, 1), jnp.int32),
            pltpu.VMEM((width, cols), BF16),
            pltpu.VMEM((1, cols), F32),
            pltpu.VMEM((2, 8, CAP, part), F32),
            pltpu.VMEM((width, part), F32),
            pltpu.VMEM((half, part), F32),
            pltpu.VMEM((2, 8, CAP, width), F32),
            pltpu.VMEM((2, 8, CAP, width), F32),
            pltpu.VMEM((CAP, 128), F32),
            pltpu.VMEM((4, CAP, 128), F32),
            pltpu.VMEM((4, 2, CAP, 128), F32),
            pltpu.VMEM((16, CAP, width), F32),
            pltpu.VMEM((CAP, width), F32),
            pltpu.VMEM((8, CAP, part), F32),
            pltpu.VMEM((2, 8, CAP, part), F32),
            pltpu.VMEM((8, width, part), F32),
            pltpu.VMEM((8, width, part), F32),
            pltpu.VMEM((3, width, width), BF16),
            pltpu.VMEM((width, width), F32),
            pltpu.VMEM((2, width, cols), BF16),
            pltpu.VMEM((6 * CAP, cols), BF16),
            pltpu.VMEM((CAP, 1), jnp.int32),
            dma((8,)), dma((8,)), dma((4,)), dma((4,)), dma((8,)), dma((1,)),
            dma((2, 6)), dma((2,)), dma((2,)), dma((2, 4)), dma((16,)), dma((1,)),
            dma((8,)), dma((8,)), dma((8,)), dma((8,)), dma((8,)), dma((2, 8)),
            dma((4,)), dma((4,)), dma((2, 8)), dma((8,)), dma((1,)), dma((1,)), dma((4,)), dma((4,)),
            dma((2, 4)), dma((2, 4)), dma((4, 4)),
            dma((1,)),
        ],
        compiler_params=pltpu.CompilerParams(
            collective_id=1, has_side_effects=True, vmem_limit_bytes=40 * 1024 * 1024
        ),
        name="compact",
    )(matrix, piv_row, coupling)


def per_device(matrix, pivots, coupling):
    width = coupling.shape[0]
    rows = matrix.shape[0]
    piv_row = pivots.reshape(1, width)

    def few(matrix, pivots, coupling):
        return compact(matrix, piv_row, coupling)

    def general(matrix, pivots, coupling):
        piv_col = pivots.reshape(width, 1)
        picked = pick(matrix, pivots)
        qc, qr = exchange(picked, matrix, piv_col, piv_row)
        return update(piv_col, piv_row, matrix, qc, qr, coupling)

    blocks = jnp.arange(16, dtype=jnp.int32)[:, None]
    block = jnp.right_shift(piv_row, rows.bit_length() - 1)
    counts = jnp.sum((block == blocks).astype(jnp.int32), axis=1)
    return lax.cond(jnp.max(counts) <= CAP, few, general, matrix, pivots, coupling)


def solution(mesh):
    return jax.shard_map(
        per_device,
        mesh=mesh,
        in_specs=(P("row", "col"), P(), P()),
        out_specs=P("row", "col"),
        check_vma=False,
    )
```

```python
import functools

import jax
import jax.numpy as jnp
from jax import lax
from jax.experimental import pallas as pl
from jax.experimental.pallas import tpu as pltpu
from jax.sharding import PartitionSpec as P

MESH = pl.DeviceIdType.MESH
F32 = jnp.float32
BF16 = jnp.bfloat16
HIGHEST = lax.Precision.HIGHEST
CAP = 32


def one_hot(index, start, shape, axis):
    return lax.broadcasted_iota(jnp.int32, shape, axis) + start == index


def pick_kernel(piv, matrix, picked, sem):
    rows = matrix.shape[0]
    count = picked.shape[0]
    start = lax.axis_index("row") * rows
    picked[...] = jnp.zeros_like(picked)

    def copy(k):
        local = jnp.clip(piv[k] - start, 0, rows - 1)
        return pltpu.make_async_copy(matrix.at[pl.ds(local, 1)], picked.at[pl.ds(k, 1)], sem)

    def go(k, _):
        @pl.when((piv[k] >= start) & (piv[k] < start + rows))
        def _():
            copy(k).start()

        return 0

    def wait(k, _):
        @pl.when((piv[k] >= start) & (piv[k] < start + rows))
        def _():
            copy(k).wait()

        return 0

    lax.fori_loop(0, count, go, 0)
    lax.fori_loop(0, count, wait, 0)


def pick(matrix, pivots):
    return pl.pallas_call(
        pick_kernel,
        out_shape=jax.ShapeDtypeStruct((pivots.shape[0], matrix.shape[1]), F32),
        in_specs=[pl.BlockSpec(memory_space=pltpu.SMEM), pl.BlockSpec(memory_space=pl.ANY)],
        out_specs=pl.BlockSpec(memory_space=pltpu.VMEM),
        scratch_shapes=[pltpu.SemaphoreType.DMA],
        name="pick",
    )(pivots, matrix)


def exchange_kernel(
    picked, matrix, piv_col, piv_row, qc, qr,
    a1buf, sums, a2buf, raw, piece, corner, w0buf, w0mine,
    s_a1, r_a1, s_a2, r_a2, s_ld, r_ld, s_w, r_w, s_w0, r_w0,
    s_b, r_b, s_f, s_t, r_t, s_y, r_y, local,
):
    r, c = lax.axis_index("row"), lax.axis_index("col")
    width, cols = picked.shape
    own = raw.shape[1]
    q, core = lax.div(r, 2), lax.rem(r, 2)
    x, y, zh = lax.div(r, 4), lax.div(c, 4), lax.rem(c, 4)
    sib = r + 1 - 2 * core
    col_start = c * cols

    def remote(src, dst, ssem, rsem, row, col):
        return pltpu.make_async_remote_copy(
            src_ref=src, dst_ref=dst, send_sem=ssem, recv_sem=rsem,
            device_id=(row, col), device_id_type=MESH,
        )

    def arrived(dst, rsem):
        remote(dst, dst, rsem, rsem, sib, c).wait_recv()

    def signal(row, col):
        pl.semaphore_signal(barrier, inc=1, device_id=(row, col), device_id_type=MESH)

    def slots(g, n=1):
        return pl.ds(pl.multiple_of(g * own, own), n * own)

    barrier = pltpu.get_barrier_semaphore()
    for d in range(1, 16):
        signal(lax.rem(r + d, 16), c)
    for d in range(1, 4):
        signal(r, lax.rem(y + d, 4) * 4 + zh)
    for j in range(4):
        @pl.when((r != c) | (4 * y + j != r))
        def _():
            signal(4 * y + j, r)

    @pl.when(c != 0)
    def _():
        signal(r, 0)

    @pl.when(c == 0)
    def _():
        for b in range(1, 16):
            signal(r, b)

    greeted = 15 + 3 + 4 - jnp.where(r == c, 1, 0) + jnp.where(c == 0, 15, 1)
    pl.semaphore_wait(barrier, greeted)

    def lead_copies(act):
        @pl.when(r == 0)
        def _():
            for g in range(1, 16):
                act(remote(matrix.at[slots(g)], raw.at[1], s_ld.at[g], r_ld.at[0], g, c))
            act(pltpu.make_async_copy(matrix.at[slots(0)], raw.at[1], local.at[0]))

    lead_copies(lambda copy: copy.start())

    def a1(p):
        return remote(
            picked.at[slots(2 * p + 1 - core)], a1buf.at[p], s_a1.at[p], r_a1.at[p], sib, c
        )

    def a2(p):
        return remote(sums.at[p], a2buf.at[q], s_a2.at[p], r_a2.at[q], 2 * p + core, c)

    for d in range(1, 9):
        a1(lax.rem(q + d, 8)).start()
    for d in range(1, 9):
        p = lax.rem(q + d, 8)
        arrived(a1buf.at[p], r_a1.at[p])
        total = picked[slots(2 * p + core)] + a1buf[p]
        if d < 8:
            sums[p] = total
            a2(p).start()
        else:
            a2buf[q] = total

    hot_t = one_hot(piv_col[...], col_start, (width, cols), 1).astype(F32)
    swapped = jnp.max(hot_t, axis=0, keepdims=True) > 0

    def fixed(part):
        placed = jnp.dot(corner[part], hot_t, precision=HIGHEST, preferred_element_type=F32)
        return jnp.where(swapped, placed, raw[part])

    def send_corner(part, act):
        for b in range(1, 16):
            act(remote(corner.at[part], corner.at[part], s_w.at[part, b], r_w.at[part], r, b))

    def get_corner(part):
        @pl.when(c == 0)
        def _():
            corner[part] = raw[part, :, :width]
            send_corner(part, lambda copy: copy.start())

        @pl.when(c != 0)
        def _():
            arrived(corner.at[part], r_w.at[part])

    def b_copy(part, d):
        p = lax.rem(q + d, 8)
        return p, remote(
            piece.at[part], qc.at[part, slots(r)], s_b.at[part, d], r_b.at[part, r], 2 * p + core, c
        )

    def b_copies(part, act):
        for d in range(1, 8):
            p, copy = b_copy(part, d)

            @pl.when(2 * p + 1 >= c)
            def _():
                act(copy)

    def f_copy(part, d):
        if d == 0:
            return remote(
                piece.at[part], qc.at[part, slots(r)], s_f.at[part, 0], r_b.at[part, r], sib, c
            )
        g = 2 * lax.rem(q + d, 8) + core
        return remote(
            qc.at[part, slots(g)], qc.at[part, slots(g)], s_f.at[part, d], r_b.at[part, g], sib, c
        )

    def t_copies(part, act):
        for k in range(4):
            col = 4 * x + k
            here = (r == c) & (k == zh)

            @pl.when(jnp.logical_not(here))
            def _():
                act(
                    remote(
                        piece.at[part], qr.at[part, slots(r)],
                        s_t.at[part, k], r_t.at[part, lax.rem(r, 4)], c, col,
                    )
                )

            @pl.when(here)
            def _():
                act(
                    pltpu.make_async_copy(
                        piece.at[part], qr.at[part, slots(r)], local.at[3 + part]
                    )
                )

    def send_piece(part):
        b_copies(part, lambda copy: copy.start())
        t_copies(part, lambda copy: copy.start())

        @pl.when(sib >= c)
        def _():
            f_copy(part, 0).start()

        pltpu.make_async_copy(piece.at[part], qc.at[part, slots(r)], local.at[1 + part]).start()

    @pl.when(r == 0)
    def _():
        pltpu.make_async_copy(matrix.at[slots(0)], raw.at[1], local.at[0]).wait()

    @pl.when(r != 0)
    def _():
        arrived(raw.at[1], r_ld.at[0])

    get_corner(1)
    piece[1] = fixed(1)
    send_piece(1)

    for d in range(1, 8):
        p = lax.rem(q + d, 8)
        arrived(a2buf.at[p], r_a2.at[p])
    total = a2buf[0]
    for p in range(1, 8):
        total = total + a2buf[p]
    raw[0] = total
    get_corner(0)
    hot = one_hot(piv_row[...], col_start, (cols, width), 0).astype(F32)
    mine = jnp.dot(total, hot, precision=HIGHEST, preferred_element_type=F32)

    def w0_copy(col):
        return remote(w0mine, w0buf.at[col], s_w0.at[0], r_w0.at[col], r, 0)

    @pl.when(c != 0)
    def _():
        w0mine[...] = mine
        w0_copy(c).start()

    piece[0] = fixed(0)

    @pl.when(c == 0)
    def _():
        w0 = mine
        for b in range(1, 16):
            arrived(w0buf.at[b], r_w0.at[b])
            w0 = w0 + w0buf[b]
        piece[0, :, :width] = w0

    send_piece(0)

    def y_copies(part, act):
        for d in range(1, 4):
            col = lax.rem(y + d, 4) * 4 + zh

            @pl.when(col <= r)
            def _():
                block = qr.at[part, slots(4 * y, 4)]
                act(remote(block, block, s_y.at[part, d], r_y.at[part, y], r, col))

    def run_y(part):
        for j in range(4):
            here = (r == c) & (4 * y + j == r)

            @pl.when(jnp.logical_not(here))
            def _():
                arrived(qr.at[part, slots(4 * y + j)], r_t.at[part, j])

            @pl.when(here)
            def _():
                pltpu.make_async_copy(
                    piece.at[part], qr.at[part, slots(r)], local.at[3 + part]
                ).wait()

        y_copies(part, lambda copy: copy.start())

    def run_f(part):
        for d in range(1, 8):
            g = 2 * lax.rem(q + d, 8) + core

            @pl.when(2 * q + 1 >= c)
            def _():
                arrived(qc.at[part, slots(g)], r_b.at[part, g])

            @pl.when(sib >= c)
            def _():
                f_copy(part, d).start()

    run_y(1)
    run_y(0)
    run_f(1)
    run_f(0)

    for part in (1, 0):
        for d in range(8):
            g = 2 * lax.rem(q + d, 8) + 1 - core

            @pl.when(r >= c)
            def _():
                arrived(qc.at[part, slots(g)], r_b.at[part, g])

        for d in range(1, 4):
            there = lax.rem(y + d, 4)

            @pl.when(c <= r)
            def _():
                arrived(qr.at[part, slots(4 * there, 4)], r_y.at[part, there])

        pltpu.make_async_copy(piece.at[part], qc.at[part, slots(r)], local.at[1 + part]).wait()

    lead_copies(lambda copy: copy.wait_send() if copy.is_remote else None)
    for d in range(1, 9):
        a1(lax.rem(q + d, 8)).wait_send()
    for d in range(1, 8):
        a2(lax.rem(q + d, 8)).wait_send()

    @pl.when(c != 0)
    def _():
        w0_copy(c).wait_send()

    for part in (1, 0):
        @pl.when(c == 0)
        def _():
            send_corner(part, lambda copy: copy.wait_send())

        b_copies(part, lambda copy: copy.wait_send())
        t_copies(part, lambda copy: copy.wait_send() if copy.is_remote else None)
        y_copies(part, lambda copy: copy.wait_send())

        @pl.when(sib >= c)
        def _():
            for d in range(8):
                f_copy(part, d).wait_send()


def exchange(picked, matrix, piv_col, piv_row):
    width, cols = picked.shape
    own = width // 16
    dma = pltpu.SemaphoreType.DMA
    out = jax.ShapeDtypeStruct((2, width, cols), F32)
    any_spec = pl.BlockSpec(memory_space=pl.ANY)
    vmem = pl.BlockSpec(memory_space=pltpu.VMEM)
    return pl.pallas_call(
        exchange_kernel,
        out_shape=(out, out),
        in_specs=[vmem, any_spec, vmem, vmem],
        out_specs=(any_spec, any_spec),
        scratch_shapes=[
            pltpu.VMEM((8, own, cols), F32),
            pltpu.VMEM((8, own, cols), F32),
            pltpu.VMEM((8, own, cols), F32),
            pltpu.VMEM((2, own, cols), F32),
            pltpu.VMEM((2, own, cols), F32),
            pltpu.VMEM((2, own, width), F32),
            pltpu.VMEM((16, own, width), F32),
            pltpu.VMEM((own, width), F32),
            dma((8,)), dma((8,)), dma((8,)), dma((8,)),
            dma((16,)), dma((1,)), dma((2, 16)), dma((2,)), dma((1,)), dma((16,)),
            dma((2, 8)), dma((2, 16)), dma((2, 8)), dma((2, 4)), dma((2, 4)), dma((2, 4)), dma((2, 4)),
            dma((5,)),
        ],
        compiler_params=pltpu.CompilerParams(
            collective_id=0, has_side_effects=True, vmem_limit_bytes=32 * 1024 * 1024
        ),
        name="exchange",
    )(picked, matrix, piv_col, piv_row)


def split(value, n):
    terms = []
    for _ in range(n):
        term = value.astype(BF16)
        terms.append(term)
        value = value - term.astype(F32)
    return terms


def update_kernel(piv_col, piv_row, m, qc, qr, coupling, out, hot_t, panel, lead):
    r, c = lax.axis_index("row"), lax.axis_index("col")
    tile, cols = out.shape
    width = coupling.shape[0]
    step = pl.program_id(0)
    row_start = r * cols + step * tile
    col_start = c * cols

    @pl.when(r < c)
    def _():
        out[...] = jnp.zeros_like(out)

    @pl.when((r >= c) & (step == 0))
    def _():
        hot_t[...] = one_hot(piv_col[...], col_start, (width, cols), 1).astype(BF16)
        for i, term in enumerate(split(qc[0], 2)):
            panel[i] = term
        for i, term in enumerate(split(qc[1], 3)):
            lead[i] = term

    def dot(a, b):
        return jnp.dot(a, b, preferred_element_type=F32)

    @pl.when(r >= c)
    def _():
        panel_rows = qr[0].T
        scaled = jnp.dot(panel_rows, coupling[...], precision=HIGHEST, preferred_element_type=F32)
        s_hi, s_lo = split(scaled, 2)
        update = dot(s_hi, panel[0]) + dot(s_hi, panel[1]) + dot(s_lo, panel[0])
        hot = one_hot(piv_row[...], row_start, (tile, width), 0)
        hit_row = jnp.max(hot.astype(F32), axis=1, keepdims=True) > 0
        hit_col = jnp.max(hot_t[...].astype(F32), axis=0, keepdims=True) > 0
        hot = hot.astype(F32).astype(BF16)
        new_rows = dot(hot, lead[0]) + dot(hot, lead[1]) + dot(hot, lead[2])
        lead_cols = jnp.where(hit_row, 0.0, qr[1].T)
        new_cols = sum(dot(term, hot_t[...]) for term in split(lead_cols, 3))
        value = jnp.where(hit_row | hit_col, 0.0, m[...]) + new_rows + new_cols
        spread = jnp.concatenate([panel_rows, jnp.zeros((tile, cols - width), F32)], axis=1)
        places = lax.broadcasted_iota(jnp.int32, (tile, cols), 1)
        value = jnp.where((places < width) & (c == 0), spread, value)
        below = lax.broadcasted_iota(jnp.int32, (tile, cols), 0) + row_start >= places + col_start
        out[...] = jnp.where(below, value - update, 0.0)


def update(piv_col, piv_row, matrix, qc, qr, coupling):
    rows, cols = matrix.shape
    width = coupling.shape[0]
    tile = min(rows, 256)

    def whole(shape):
        return pl.BlockSpec(shape, lambda i: (0,) * len(shape))

    return pl.pallas_call(
        update_kernel,
        grid=(rows // tile,),
        out_shape=jax.ShapeDtypeStruct((rows, cols), F32),
        in_specs=[
            whole((width, 1)),
            whole((1, width)),
            pl.BlockSpec((tile, cols), lambda i: (i, 0)),
            whole((2, width, cols)),
            pl.BlockSpec((2, width, tile), lambda i: (0, 0, i)),
            whole((width, width)),
        ],
        out_specs=pl.BlockSpec((tile, cols), lambda i: (i, 0)),
        scratch_shapes=[
            pltpu.VMEM((width, cols), BF16),
            pltpu.VMEM((2, width, cols), BF16),
            pltpu.VMEM((3, width, cols), BF16),
        ],
        compiler_params=pltpu.CompilerParams(vmem_limit_bytes=48 * 1024 * 1024),
        name="update",
    )(piv_col, piv_row, matrix, qc, qr, coupling)


def order(s):
    return lax.rem(s, 2) * 8 + lax.div(s, 2)


def blocks_of(piv, rows):
    block = jnp.right_shift(piv, rows.bit_length() - 1)
    return jnp.bitwise_and(block, 1) * 8 + jnp.right_shift(block, 1)


def column(row):
    return jnp.broadcast_to(row, (8, row.shape[1])).T[:, :1]


def places(piv_row, rows):
    width = piv_row.shape[1]
    first = lax.broadcasted_iota(jnp.int32, (width, width), 0)
    second = lax.broadcasted_iota(jnp.int32, (width, width), 1)
    block_row = blocks_of(piv_row, rows)
    before = (column(block_row) == block_row) & (first < second)
    return block_row * CAP + jnp.sum(jnp.where(before, 1, 0), axis=0, keepdims=True)


def listed(place_row, piv_row, start, count):
    spot = lax.broadcasted_iota(jnp.int32, (count, place_row.shape[1]), 0) + start
    return jnp.sum(jnp.where(spot == place_row, piv_row + 1, 0), axis=1, keepdims=True) - 1


def hot16(mask):
    return mask.astype(F32).astype(BF16)


def dot16(a, b, dims=((1,), (0,))):
    return lax.dot_general(a, b, (dims, ((), ())), preferred_element_type=F32)


def choose(hot, value):
    return sum(dot16(hot, term) for term in split(value, 3))


def compact_kernel(
    matrix, piv_row, coupling, out,
    block, picked, hall, hall_t, piv_col, spread, hit_col,
    abuf, lead, piece, wbuf, vbuf, w0out, w0z, w0y, w2out, corner, lout, swaps, qc, qr,
    w1s, w0, panel, right, left,
    s_a, r_a, s_sib, r_sib, s_ld, r_ld, s_k, r_k, s_w0, r_w0, s_w2, r_w2, s_w, r_w, s_v, r_v,
    s_l, r_l, s_b, s_x, r_b, s_f, s_t, r_t, s_z, r_z, s_y, s_r, r_y, local,
):
    r, c = lax.axis_index("row"), lax.axis_index("col")
    rows, cols = matrix.shape
    width = piv_row.shape[1]
    half, part = width // 2, cols // 8
    tile = 2 * part
    q, core = lax.div(r, 2), lax.rem(r, 2)
    zl = lax.rem(q, 2)
    x, y, zh = lax.div(r, 4), lax.div(c, 4), lax.rem(c, 4)
    sib = r + 1 - 2 * core
    pair = q + 1 - 2 * zl
    chunk = lax.div(order(c), 4)
    col_start = c * cols

    def remote(src, dst, ssem, rsem, row, col):
        return pltpu.make_async_remote_copy(
            src_ref=src, dst_ref=dst, send_sem=ssem, recv_sem=rsem,
            device_id=(row, col), device_id_type=MESH,
        )

    def arrived(dst, rsem):
        remote(dst, dst, rsem, rsem, sib, c).wait_recv()

    def start(copy):
        copy.start()

    def sent(copy):
        copy.wait_send()

    load = pltpu.make_async_copy(matrix, block, local.at[0])
    load.start()

    barrier = pltpu.get_barrier_semaphore()

    def signal(row, col):
        pl.semaphore_signal(barrier, inc=1, device_id=(row, col), device_id_type=MESH)

    for d in (1, 2, 3):
        signal(r, lax.rem(y + d, 4) * 4 + zh)
    for d in (1, 2, 3):
        signal(r, 4 * y + lax.rem(zh + d, 4))

    @pl.when(r != c)
    def _():
        signal(c, r)

    @pl.when(r > c)
    def _():
        for j in range(8):
            signal(2 * j + lax.rem(c, 2), r)

    for d in range(1, 16):
        signal(lax.rem(r + d, 16), c)

    greeted = 15 + 3 + 3 + jnp.where(r == c, 0, 1)
    greeted = greeted + lax.div(c - core + 1, 2)

    place_row = places(piv_row[...], rows)
    piv_col[...] = column(piv_row[...])
    spots = lax.broadcasted_iota(jnp.int32, (16 * CAP, width), 0)
    hall[...] = hot16(spots == place_row)
    spots = lax.broadcasted_iota(jnp.int32, (width, 16 * CAP), 1)
    hall_t[...] = hot16(spots == column(place_row))
    mine = order(r) * CAP
    left[...] = listed(place_row, piv_row[...], mine, CAP)
    load.wait()
    for t in range(CAP):
        local_row = jnp.sum(jnp.where(place_row == mine + t, piv_row[...] - r * rows, 0))
        picked[pl.ds(t, 1)] = block[pl.ds(jnp.clip(local_row, 0, rows - 1), 1)]
    picked[...] = jnp.where(left[...] >= 0, picked[...], 0.0)

    @pl.when(c == 0)
    def _():
        wbuf[core, q] = picked[:, :width]

    pl.semaphore_wait(barrier, greeted)

    def a_copy(d):
        p = lax.rem(q + d, 8)
        cut = pl.ds(pl.multiple_of(p * part, part), part)
        return remote(picked.at[:, cut], abuf.at[core, q], s_a.at[d], r_a.at[q], 2 * p + core, c)

    for d in range(1, 8):
        a_copy(d).start()

    def k_copies(i, act, along):
        src = wbuf.at[core, q] if i == 0 else corner

        @pl.when((c == 0) if along == 0 else (zh == 0))
        def _():
            for d in (1, 2, 3):
                col = 4 * d if along == 0 else 4 * y + d
                act(remote(src, src, s_k.at[i, 3 * along + d - 1], r_k.at[i], r, col))

    k_copies(0, start, 0)

    def lead_copy(p):
        return remote(
            block.at[pl.ds(0, width), pl.ds(p * part, part)], lead, s_ld.at[p], r_ld.at[0], 2 * p, c
        )

    @pl.when(r == 0)
    def _():
        for p in range(1, 8):
            lead_copy(p).start()

    abuf[core, q] = picked[:, pl.ds(pl.multiple_of(q * part, part), part)]

    def w2_copies(act):
        for s in range(1, 16):
            src = w2out.at[(s % 2) * 8 + s // 2]
            act(remote(src, corner, s_w2.at[s], r_w2.at[0], s, 0))

    @pl.when((r == 0) & (c == 0))
    def _():
        w2out[...] = choose(hall[...], block[:width, :width]).reshape(16, CAP, width)
        w2_copies(start)
        corner[...] = w2out[0]

    w0_copy = remote(w0out, w0z.at[zh], s_w0.at[0], r_w0.at[0, zh], r, 4 * y)
    w0_pair = remote(w0z.at[pl.ds(0, 2)], w0y.at[y], s_w0.at[1], r_w0.at[1, y], r, 0)

    here_piv = listed(place_row, piv_row[...], chunk * 128, 128)
    near = hot16(one_hot(here_piv, col_start, (128, cols), 1))
    w0out[...] = sum(dot16(term, near, ((1,), (1,))) for term in split(picked[...], 3))

    @pl.when(zh != 0)
    def _():
        w0_copy.start()

    for d in range(1, 8):
        p = lax.rem(q + d, 8)
        arrived(abuf.at[core, p], r_a.at[p])
    a_sib = remote(abuf.at[core], abuf.at[core], s_sib.at[1], r_sib.at[1], sib, c)
    a_sib.start()
    arrived(abuf.at[1 - core], r_sib.at[1])

    def slot(k):
        return pl.ds(pl.multiple_of(k * half, half), half)

    piece[...] = choose(hall_t[slot(core)], abuf[...].reshape(16 * CAP, part))

    t_copy = remote(piece, qr.at[q, slot(core)], s_t.at[0], r_t.at[0], c, r)

    @pl.when(r != c)
    def _():
        t_copy.start()

    @pl.when(r == c)
    def _():
        qr[q, slot(core)] = piece[...]

    def wanted(p):
        return 2 * p + 1 >= c

    def b_copies(act):
        @pl.when(wanted(6 + 1 - zl))
        def _():
            act(
                remote(piece, qc.at[q, slot(core)], s_b.at[0], r_b.at[core, q], 2 * pair + core, c)
            )

        for d in range(1, 4):
            p = lax.rem(q + 2 * d, 8)

            @pl.when(wanted(p))
            def _():
                act(remote(piece, qc.at[q, slot(core)], s_b.at[d], r_b.at[core, q], 2 * p + core, c))

    def x_copies(act):
        for d in range(1, 4):
            p = lax.rem(q + 2 * d, 8)
            ref = qc.at[pair, slot(core)]

            @pl.when(wanted(p))
            def _():
                act(remote(ref, ref, s_x.at[d], r_b.at[core, pair], 2 * p + core, c))

    def f_copy(p):
        ref = qc.at[p, slot(core)]
        return remote(ref, ref, s_f.at[p], r_b.at[core, p], sib, c)

    def forward(p):
        @pl.when(sib >= c)
        def _():
            f_copy(p).start()

    b_copies(start)
    qc[q, slot(core)] = piece[...]
    forward(q)

    def w_copies(act, buf, ssem, rsem):
        for d in range(1, 8):
            p = lax.rem(q + d, 8)

            @pl.when(wanted(p))
            def _():
                act(
                    remote(buf.at[core, q], buf.at[core, q], ssem.at[d], rsem.at[q], 2 * p + core, c)
                )

    @pl.when(c != 0)
    def _():
        arrived(wbuf.at[core, q], r_k.at[0])

    k_copies(0, start, 1)
    w_copies(start, wbuf, s_w, r_w)

    hot = one_hot(piv_col[...], col_start, (width, cols), 1).astype(F32)
    hit_col[...] = jnp.max(hot, axis=0, keepdims=True)
    spread[...] = hot.astype(BF16)

    def need(there):
        return 4 * there + zh <= r

    up, down, across = lax.rem(y + 1, 4), lax.rem(y + 3, 4), lax.rem(y + 2, 4)

    def y_ref(owner, k):
        j = lax.rem(zh + k, 4)
        return qr.at[2 * owner + lax.div(j, 2), slot(lax.rem(j, 2))]

    def z_copies(act):
        for d in (1, 3, 2):
            there = lax.rem(zh + d, 4)

            @pl.when(there <= r)
            def _():
                act(
                    remote(
                        y_ref(y, 0), y_ref(y, 0), s_z.at[d], r_z.at[(4 - d) % 4], r, 4 * y + there
                    )
                )

    def relays(node, k, way):
        off = lax.rem(node + 4 - x, 4)
        return (off == 2) | ((off != 0) & (way == k % 2))

    def y_copies(k, act):
        for way, to in ((0, up), (1, down)):
            ref = y_ref(y, k)

            @pl.when(need(to) | (need(across) & relays(to, k, way)))
            def _():
                act(remote(ref, ref, s_y.at[way, k], r_y.at[y, k], r, 4 * to + zh))

    def relay(k, act):
        for way, owner, to in ((0, down, up), (1, up, down)):
            ref = y_ref(owner, k)

            @pl.when(need(to) & relays(y, k, way))
            def _():
                act(remote(ref, ref, s_r.at[way, k], r_y.at[owner, k], r, 4 * to + zh))

    def run_relay(k):
        for way, owner, to in ((0, down, up), (1, up, down)):
            @pl.when(relays(y, k, way) & (need(y) | need(to)))
            def _():
                arrived(y_ref(owner, k), r_y.at[owner, k])

        relay(k, start)

    def run_y(k):
        @pl.when(zh <= r)
        def _():
            arrived(y_ref(y, k), r_z.at[k])

        y_copies(k, start)

    @pl.when((c == 0) & (r != 0))
    def _():
        arrived(corner, r_w2.at[0])

    k_copies(1, start, 0)

    @pl.when(zh == 0)
    def _():
        for d in (1, 2, 3):
            arrived(w0z.at[d], r_w0.at[0, d])
        w0z[0] = w0out[...] + w0z[2]
        w0z[1] = w0z[1] + w0z[3]

        @pl.when(y != 0)
        def _():
            w0_pair.start()

    @pl.when(r != c)
    def _():
        arrived(y_ref(y, 0), r_t.at[0])

    y_copies(0, start)
    z_copies(start)

    @pl.when(wanted(6 + zl))
    def _():
        arrived(qc.at[pair, slot(core)], r_b.at[core, pair])

    x_copies(start)
    forward(pair)
    run_relay(0)

    @pl.when(c == 0)
    def _():
        for d in (1, 2, 3):
            arrived(w0y.at[d], r_w0.at[1, d])
        w0y[0] = w0z[:2]
        total = jnp.zeros((CAP, width), F32)
        for j in range(4):
            listing = w0y[2 * (j % 2), j // 2] + w0y[2 * (j % 2) + 1, j // 2]
            hot = hall[128 * j : 128 * (j + 1)]
            total = total + sum(dot16(term, hot) for term in split(listing, 3))
        vbuf[core, q] = total
        w_copies(start, vbuf, s_v, r_v)

    run_y(1)
    run_y(3)
    lead_sib = remote(lead, lead, s_sib.at[0], r_sib.at[0], sib, c)

    @pl.when(r == 0)
    def _():
        lead[...] = block[:width, :part]

    @pl.when((core == 0) & (r != 0))
    def _():
        arrived(lead, r_ld.at[0])

    @pl.when(core == 0)
    def _():
        lead_sib.start()

    @pl.when(core == 1)
    def _():
        arrived(lead, r_sib.at[0])

    lists = hall[pl.ds(pl.multiple_of(core * 8 * CAP, 8 * CAP), 8 * CAP)]
    lout[...] = choose(lists, lead[...]).reshape(8, CAP, part)

    def l_copies(act, act_here):
        for d in range(8):
            j = lax.rem(q + d, 8)
            s = 2 * j + core
            as_row = s >= c
            row, col = jnp.where(as_row, s, c), jnp.where(as_row, c, s)
            kind = jnp.where(as_row, 0, 1)
            here = as_row & (s == r)

            @pl.when(jnp.logical_not(here))
            def _():
                act(remote(lout.at[j], swaps.at[kind, q], s_l.at[j], r_l.at[kind, q], row, col))

            @pl.when(here)
            def _():
                act_here(j)

    def keep_lead(j):
        swaps[0, q] = lout[j]

    l_copies(start, keep_lead)


    w_sib = remote(wbuf.at[core], wbuf.at[core], s_sib.at[2], r_sib.at[2], sib, c)
    v_sib = remote(vbuf.at[core], vbuf.at[core], s_sib.at[3], r_sib.at[3], sib, c)

    @pl.when((zh == 0) & (y != 0))
    def _():
        arrived(corner, r_k.at[1])

    k_copies(1, start, 1)
    for d in range(1, 4):
        p = lax.rem(q + 2 * d, 8)

        @pl.when(wanted(q))
        def _():
            arrived(qc.at[p, slot(core)], r_b.at[core, p])

        forward(p)

    @pl.when(wanted(q))
    def _():
        for d in range(1, 8):
            p = lax.rem(q + d, 8)
            arrived(wbuf.at[core, p], r_w.at[p])

    @pl.when(sib >= c)
    def _():
        w_sib.start()

    run_relay(1)
    run_relay(3)
    run_y(2)

    for d in range(1, 4):
        p = lax.rem(pair + 2 * d, 8)

        @pl.when(wanted(q))
        def _():
            arrived(qc.at[p, slot(core)], r_b.at[core, p])

        forward(p)

    @pl.when(c == 0)
    def _():
        for d in range(1, 8):
            p = lax.rem(q + d, 8)
            arrived(vbuf.at[core, p], r_v.at[p])
        v_sib.start()
        arrived(vbuf.at[1 - core], r_sib.at[3])
        w0[...] = choose(hall_t[...], vbuf[...].reshape(16 * CAP, width))

    @pl.when(zh != 0)
    def _():
        arrived(corner, r_k.at[1])

    @pl.when(r < c)
    def _():
        out[...] = jnp.zeros_like(out)

    @pl.when(r >= c)
    def _():
        arrived(wbuf.at[1 - core], r_sib.at[2])
        w1 = choose(hall_t[...], wbuf[...].reshape(16 * CAP, width))
        for i, term in enumerate(split(w1, 3)):
            w1s[i] = term
        for p in range(8):
            arrived(qc.at[p, slot(1 - core)], r_b.at[1 - core, p])
        placed = [dot16(w1s[i], spread[...]) for i in range(2)]
        hit = hit_col[...] > 0
        for p in range(8):
            cut = slice(p * part, (p + 1) * part)
            value = qc[p]
            if p < width // part:
                value = jnp.where(c == 0, w0[:, cut], value)
            for j, term in enumerate(split(value, 2)):
                term = jnp.where(hit[:, cut], placed[j][:, cut], term.astype(F32))
                panel[j, :, cut] = term.astype(BF16)
        for p in range(8):
            @pl.when(p != q)
            def _():
                arrived(swaps.at[0, p], r_l.at[0, p])
        rows_in = jnp.concatenate([swaps[0, p] for p in range(8)], axis=1)
        placed = sum(dot16(term, spread[...]) for term in split(corner[...], 3))
        rows_in = jnp.where(hit, placed, rows_in)
        for j, term in enumerate(split(rows_in, 3)):
            right[j * CAP : (j + 1) * CAP] = term
        col_piv = listed(place_row, piv_row[...], order(c) * CAP, CAP)
        hot = hot16(one_hot(col_piv, col_start, (CAP, cols), 1))
        for j in range(3):
            right[(3 + j) * CAP : (4 + j) * CAP] = hot


    def tile_update(owner):
        row_start = r * rows + owner * tile
        hot = one_hot(left[...], row_start, (CAP, tile), 1).astype(F32)
        hit = jnp.max(hot, axis=0, keepdims=True)
        rows_t = jnp.concatenate([qr[2 * owner], qr[2 * owner + 1]], axis=1)
        near = hot16(one_hot(piv_col[...], row_start, (width, tile), 1))
        rows_t = jnp.where(hit > 0, sum(dot16(w1s[i], near) for i in range(3)), rows_t)
        rows_t = jnp.where((r == 0) & (c == 0) & (owner == 0), w0[...], rows_t)
        scaled = lax.dot_general(
            coupling[...], rows_t, (((0,), (0,)), ((), ())),
            precision=HIGHEST, preferred_element_type=F32,
        )
        s_hi, s_lo = split(scaled, 2)
        lanes = ((0,), (0,))
        change = dot16(s_hi, panel[0], lanes) + dot16(s_hi, panel[1], lanes)
        change = change + dot16(s_lo, panel[0], lanes)
        kind = jnp.where(r == c, 0, 1)
        cols_in = jnp.concatenate([swaps[kind, 2 * owner + i] for i in range(2)], axis=1)
        cols_in = jnp.where(hit > 0, 0.0, cols_in)
        hot = hot.astype(BF16)
        lhs = jnp.concatenate([hot, hot, hot] + split(cols_in, 3), axis=0)
        moved = dot16(lhs, right[...], lanes)
        at = pl.ds(pl.multiple_of(owner * tile, tile), tile)
        gone = (column(hit) > 0) | (hit_col[...] > 0)
        value = jnp.where(gone, 0.0, block[at]) + moved
        places_col = lax.broadcasted_iota(jnp.int32, (1, cols), 1) + col_start
        below = lax.broadcasted_iota(jnp.int32, (tile, 1), 0) + row_start >= places_col
        out[at] = jnp.where(below, value - change, 0.0)

        @pl.when(c == 0)
        def _():
            out[at, :width] = jnp.where(below[:, :width], rows_t.T - change[:, :width], 0.0)

    @pl.when(r > c)
    def _():
        for p in range(8):
            arrived(swaps.at[1, p], r_l.at[1, p])

    @pl.when(r >= c)
    def _():
        tile_update(y)

    run_relay(2)

    @pl.when(r >= c)
    def _():
        for k in range(4):
            for way, owner in ((0, down), (1, up)):
                @pl.when(jnp.logical_not(relays(y, k, way)))
                def _():
                    arrived(y_ref(owner, k), r_y.at[owner, k])

        def side(i, _):
            tile_update(jnp.where(i == 0, up, down))
            return 0

        lax.fori_loop(0, 2, side, 0)
        for k in range(4):
            arrived(y_ref(across, k), r_y.at[across, k])
        tile_update(across)

    @pl.when(zh != 0)
    def _():
        w0_copy.wait_send()

    @pl.when((zh == 0) & (y != 0))
    def _():
        w0_pair.wait_send()

    for i in range(2):
        for along in range(2):
            k_copies(i, sent, along)

    @pl.when(r == 0)
    def _():
        for p in range(1, 8):
            lead_copy(p).wait_send()

    @pl.when(core == 0)
    def _():
        lead_sib.wait_send()

    a_sib.wait_send()
    for d in range(1, 8):
        a_copy(d).wait_send()

    @pl.when(c == 0)
    def _():
        w_copies(sent, vbuf, s_v, r_v)
        v_sib.wait_send()

        @pl.when(r == 0)
        def _():
            w2_copies(sent)

    @pl.when(r != c)
    def _():
        t_copy.wait_send()

    b_copies(sent)
    x_copies(sent)
    w_copies(sent, wbuf, s_w, r_w)
    z_copies(sent)
    l_copies(sent, lambda j: None)
    for k in range(4):
        y_copies(k, sent)
        relay(k, sent)

    @pl.when(sib >= c)
    def _():
        w_sib.wait_send()
        for p in range(8):
            f_copy(p).wait_send()


def compact(matrix, piv_row, coupling):
    rows, cols = matrix.shape
    width = piv_row.shape[1]
    half, part = width // 2, cols // 8
    dma = pltpu.SemaphoreType.DMA
    vmem = pl.BlockSpec(memory_space=pltpu.VMEM)
    return pl.pallas_call(
        compact_kernel,
        out_shape=jax.ShapeDtypeStruct((rows, cols), F32),
        in_specs=[pl.BlockSpec(memory_space=pl.ANY), vmem, vmem],
        out_specs=vmem,
        scratch_shapes=[
            pltpu.VMEM((rows, cols), F32),
            pltpu.VMEM((CAP, cols), F32),
            pltpu.VMEM((16 * CAP, width), BF16),
            pltpu.VMEM((width, 16 * CAP), BF16),
            pltpu.VMEM((width, 1), jnp.int32),
            pltpu.VMEM((width, cols), BF16),
            pltpu.VMEM((1, cols), F32),
            pltpu.VMEM((2, 8, CAP, part), F32),
            pltpu.VMEM((width, part), F32),
            pltpu.VMEM((half, part), F32),
            pltpu.VMEM((2, 8, CAP, width), F32),
            pltpu.VMEM((2, 8, CAP, width), F32),
            pltpu.VMEM((CAP, 128), F32),
            pltpu.VMEM((4, CAP, 128), F32),
            pltpu.VMEM((4, 2, CAP, 128), F32),
            pltpu.VMEM((16, CAP, width), F32),
            pltpu.VMEM((CAP, width), F32),
            pltpu.VMEM((8, CAP, part), F32),
            pltpu.VMEM((2, 8, CAP, part), F32),
            pltpu.VMEM((8, width, part), F32),
            pltpu.VMEM((8, width, part), F32),
            pltpu.VMEM((3, width, width), BF16),
            pltpu.VMEM((width, width), F32),
            pltpu.VMEM((2, width, cols), BF16),
            pltpu.VMEM((6 * CAP, cols), BF16),
            pltpu.VMEM((CAP, 1), jnp.int32),
            dma((8,)), dma((8,)), dma((4,)), dma((4,)), dma((8,)), dma((1,)),
            dma((2, 6)), dma((2,)), dma((2,)), dma((2, 4)), dma((16,)), dma((1,)),
            dma((8,)), dma((8,)), dma((8,)), dma((8,)), dma((8,)), dma((2, 8)),
            dma((4,)), dma((4,)), dma((2, 8)), dma((8,)), dma((1,)), dma((1,)), dma((4,)), dma((4,)),
            dma((2, 4)), dma((2, 4)), dma((4, 4)),
            dma((1,)),
        ],
        compiler_params=pltpu.CompilerParams(
            collective_id=1, has_side_effects=True, vmem_limit_bytes=40 * 1024 * 1024
        ),
        name="compact",
    )(matrix, piv_row, coupling)


def per_device(matrix, pivots, coupling):
    width = coupling.shape[0]
    rows = matrix.shape[0]
    piv_row = pivots.reshape(1, width)

    def few(matrix, pivots, coupling):
        return compact(matrix, piv_row, coupling)

    def general(matrix, pivots, coupling):
        piv_col = pivots.reshape(width, 1)
        picked = pick(matrix, pivots)
        qc, qr = exchange(picked, matrix, piv_col, piv_row)
        return update(piv_col, piv_row, matrix, qc, qr, coupling)

    blocks = jnp.arange(16, dtype=jnp.int32)[:, None]
    inside = (piv_row >= blocks * rows) & (piv_row < (blocks + 1) * rows)
    counts = jnp.sum(inside.astype(jnp.int32), axis=1)
    return lax.cond(jnp.max(counts) <= CAP, few, general, matrix, pivots, coupling)


def solution(mesh):
    return jax.shard_map(
        per_device,
        mesh=mesh,
        in_specs=(P("row", "col"), P(), P()),
        out_specs=P("row", "col"),
        check_vma=False,
    )
```

```python
import functools

import jax
import jax.numpy as jnp
from jax import lax
from jax.experimental import pallas as pl
from jax.experimental.pallas import tpu as pltpu
from jax.sharding import PartitionSpec as P

MESH = pl.DeviceIdType.MESH
F32 = jnp.float32
BF16 = jnp.bfloat16
HIGHEST = lax.Precision.HIGHEST
CAP = 32


def one_hot(index, start, shape, axis):
    return lax.broadcasted_iota(jnp.int32, shape, axis) + start == index


def pick_kernel(piv, matrix, picked, sem):
    rows = matrix.shape[0]
    count = picked.shape[0]
    start = lax.axis_index("row") * rows
    picked[...] = jnp.zeros_like(picked)

    def copy(k):
        local = jnp.clip(piv[k] - start, 0, rows - 1)
        return pltpu.make_async_copy(matrix.at[pl.ds(local, 1)], picked.at[pl.ds(k, 1)], sem)

    def go(k, _):
        @pl.when((piv[k] >= start) & (piv[k] < start + rows))
        def _():
            copy(k).start()

        return 0

    def wait(k, _):
        @pl.when((piv[k] >= start) & (piv[k] < start + rows))
        def _():
            copy(k).wait()

        return 0

    lax.fori_loop(0, count, go, 0)
    lax.fori_loop(0, count, wait, 0)


def pick(matrix, pivots):
    return pl.pallas_call(
        pick_kernel,
        out_shape=jax.ShapeDtypeStruct((pivots.shape[0], matrix.shape[1]), F32),
        in_specs=[pl.BlockSpec(memory_space=pltpu.SMEM), pl.BlockSpec(memory_space=pl.ANY)],
        out_specs=pl.BlockSpec(memory_space=pltpu.VMEM),
        scratch_shapes=[pltpu.SemaphoreType.DMA],
        name="pick",
    )(pivots, matrix)


def exchange_kernel(
    picked, matrix, piv_col, piv_row, qc, qr,
    a1buf, sums, a2buf, raw, piece, corner, w0buf, w0mine,
    s_a1, r_a1, s_a2, r_a2, s_ld, r_ld, s_w, r_w, s_w0, r_w0,
    s_b, r_b, s_f, s_t, r_t, s_y, r_y, local,
):
    r, c = lax.axis_index("row"), lax.axis_index("col")
    width, cols = picked.shape
    own = raw.shape[1]
    q, core = lax.div(r, 2), lax.rem(r, 2)
    x, y, zh = lax.div(r, 4), lax.div(c, 4), lax.rem(c, 4)
    sib = r + 1 - 2 * core
    col_start = c * cols

    def remote(src, dst, ssem, rsem, row, col):
        return pltpu.make_async_remote_copy(
            src_ref=src, dst_ref=dst, send_sem=ssem, recv_sem=rsem,
            device_id=(row, col), device_id_type=MESH,
        )

    def arrived(dst, rsem):
        remote(dst, dst, rsem, rsem, sib, c).wait_recv()

    def signal(row, col):
        pl.semaphore_signal(barrier, inc=1, device_id=(row, col), device_id_type=MESH)

    def slots(g, n=1):
        return pl.ds(pl.multiple_of(g * own, own), n * own)

    barrier = pltpu.get_barrier_semaphore()
    for d in range(1, 16):
        signal(lax.rem(r + d, 16), c)
    for d in range(1, 4):
        signal(r, lax.rem(y + d, 4) * 4 + zh)
    for j in range(4):
        @pl.when((r != c) | (4 * y + j != r))
        def _():
            signal(4 * y + j, r)

    @pl.when(c != 0)
    def _():
        signal(r, 0)

    @pl.when(c == 0)
    def _():
        for b in range(1, 16):
            signal(r, b)

    greeted = 15 + 3 + 4 - jnp.where(r == c, 1, 0) + jnp.where(c == 0, 15, 1)
    pl.semaphore_wait(barrier, greeted)

    def lead_copies(act):
        @pl.when(r == 0)
        def _():
            for g in range(1, 16):
                act(remote(matrix.at[slots(g)], raw.at[1], s_ld.at[g], r_ld.at[0], g, c))
            act(pltpu.make_async_copy(matrix.at[slots(0)], raw.at[1], local.at[0]))

    lead_copies(lambda copy: copy.start())

    def a1(p):
        return remote(
            picked.at[slots(2 * p + 1 - core)], a1buf.at[p], s_a1.at[p], r_a1.at[p], sib, c
        )

    def a2(p):
        return remote(sums.at[p], a2buf.at[q], s_a2.at[p], r_a2.at[q], 2 * p + core, c)

    for d in range(1, 9):
        a1(lax.rem(q + d, 8)).start()
    for d in range(1, 9):
        p = lax.rem(q + d, 8)
        arrived(a1buf.at[p], r_a1.at[p])
        total = picked[slots(2 * p + core)] + a1buf[p]
        if d < 8:
            sums[p] = total
            a2(p).start()
        else:
            a2buf[q] = total

    hot_t = one_hot(piv_col[...], col_start, (width, cols), 1).astype(F32)
    swapped = jnp.max(hot_t, axis=0, keepdims=True) > 0

    def fixed(part):
        placed = jnp.dot(corner[part], hot_t, precision=HIGHEST, preferred_element_type=F32)
        return jnp.where(swapped, placed, raw[part])

    def send_corner(part, act):
        for b in range(1, 16):
            act(remote(corner.at[part], corner.at[part], s_w.at[part, b], r_w.at[part], r, b))

    def get_corner(part):
        @pl.when(c == 0)
        def _():
            corner[part] = raw[part, :, :width]
            send_corner(part, lambda copy: copy.start())

        @pl.when(c != 0)
        def _():
            arrived(corner.at[part], r_w.at[part])

    def b_copy(part, d):
        p = lax.rem(q + d, 8)
        return p, remote(
            piece.at[part], qc.at[part, slots(r)], s_b.at[part, d], r_b.at[part, r], 2 * p + core, c
        )

    def b_copies(part, act):
        for d in range(1, 8):
            p, copy = b_copy(part, d)

            @pl.when(2 * p + 1 >= c)
            def _():
                act(copy)

    def f_copy(part, d):
        if d == 0:
            return remote(
                piece.at[part], qc.at[part, slots(r)], s_f.at[part, 0], r_b.at[part, r], sib, c
            )
        g = 2 * lax.rem(q + d, 8) + core
        return remote(
            qc.at[part, slots(g)], qc.at[part, slots(g)], s_f.at[part, d], r_b.at[part, g], sib, c
        )

    def t_copies(part, act):
        for k in range(4):
            col = 4 * x + k
            here = (r == c) & (k == zh)

            @pl.when(jnp.logical_not(here))
            def _():
                act(
                    remote(
                        piece.at[part], qr.at[part, slots(r)],
                        s_t.at[part, k], r_t.at[part, lax.rem(r, 4)], c, col,
                    )
                )

            @pl.when(here)
            def _():
                act(
                    pltpu.make_async_copy(
                        piece.at[part], qr.at[part, slots(r)], local.at[3 + part]
                    )
                )

    def send_piece(part):
        b_copies(part, lambda copy: copy.start())
        t_copies(part, lambda copy: copy.start())

        @pl.when(sib >= c)
        def _():
            f_copy(part, 0).start()

        pltpu.make_async_copy(piece.at[part], qc.at[part, slots(r)], local.at[1 + part]).start()

    @pl.when(r == 0)
    def _():
        pltpu.make_async_copy(matrix.at[slots(0)], raw.at[1], local.at[0]).wait()

    @pl.when(r != 0)
    def _():
        arrived(raw.at[1], r_ld.at[0])

    get_corner(1)
    piece[1] = fixed(1)
    send_piece(1)

    for d in range(1, 8):
        p = lax.rem(q + d, 8)
        arrived(a2buf.at[p], r_a2.at[p])
    total = a2buf[0]
    for p in range(1, 8):
        total = total + a2buf[p]
    raw[0] = total
    get_corner(0)
    hot = one_hot(piv_row[...], col_start, (cols, width), 0).astype(F32)
    mine = jnp.dot(total, hot, precision=HIGHEST, preferred_element_type=F32)

    def w0_copy(col):
        return remote(w0mine, w0buf.at[col], s_w0.at[0], r_w0.at[col], r, 0)

    @pl.when(c != 0)
    def _():
        w0mine[...] = mine
        w0_copy(c).start()

    piece[0] = fixed(0)

    @pl.when(c == 0)
    def _():
        w0 = mine
        for b in range(1, 16):
            arrived(w0buf.at[b], r_w0.at[b])
            w0 = w0 + w0buf[b]
        piece[0, :, :width] = w0

    send_piece(0)

    def y_copies(part, act):
        for d in range(1, 4):
            col = lax.rem(y + d, 4) * 4 + zh

            @pl.when(col <= r)
            def _():
                block = qr.at[part, slots(4 * y, 4)]
                act(remote(block, block, s_y.at[part, d], r_y.at[part, y], r, col))

    def run_y(part):
        for j in range(4):
            here = (r == c) & (4 * y + j == r)

            @pl.when(jnp.logical_not(here))
            def _():
                arrived(qr.at[part, slots(4 * y + j)], r_t.at[part, j])

            @pl.when(here)
            def _():
                pltpu.make_async_copy(
                    piece.at[part], qr.at[part, slots(r)], local.at[3 + part]
                ).wait()

        y_copies(part, lambda copy: copy.start())

    def run_f(part):
        for d in range(1, 8):
            g = 2 * lax.rem(q + d, 8) + core

            @pl.when(2 * q + 1 >= c)
            def _():
                arrived(qc.at[part, slots(g)], r_b.at[part, g])

            @pl.when(sib >= c)
            def _():
                f_copy(part, d).start()

    run_y(1)
    run_y(0)
    run_f(1)
    run_f(0)

    for part in (1, 0):
        for d in range(8):
            g = 2 * lax.rem(q + d, 8) + 1 - core

            @pl.when(r >= c)
            def _():
                arrived(qc.at[part, slots(g)], r_b.at[part, g])

        for d in range(1, 4):
            there = lax.rem(y + d, 4)

            @pl.when(c <= r)
            def _():
                arrived(qr.at[part, slots(4 * there, 4)], r_y.at[part, there])

        pltpu.make_async_copy(piece.at[part], qc.at[part, slots(r)], local.at[1 + part]).wait()

    lead_copies(lambda copy: copy.wait_send() if copy.is_remote else None)
    for d in range(1, 9):
        a1(lax.rem(q + d, 8)).wait_send()
    for d in range(1, 8):
        a2(lax.rem(q + d, 8)).wait_send()

    @pl.when(c != 0)
    def _():
        w0_copy(c).wait_send()

    for part in (1, 0):
        @pl.when(c == 0)
        def _():
            send_corner(part, lambda copy: copy.wait_send())

        b_copies(part, lambda copy: copy.wait_send())
        t_copies(part, lambda copy: copy.wait_send() if copy.is_remote else None)
        y_copies(part, lambda copy: copy.wait_send())

        @pl.when(sib >= c)
        def _():
            for d in range(8):
                f_copy(part, d).wait_send()


def exchange(picked, matrix, piv_col, piv_row):
    width, cols = picked.shape
    own = width // 16
    dma = pltpu.SemaphoreType.DMA
    out = jax.ShapeDtypeStruct((2, width, cols), F32)
    any_spec = pl.BlockSpec(memory_space=pl.ANY)
    vmem = pl.BlockSpec(memory_space=pltpu.VMEM)
    return pl.pallas_call(
        exchange_kernel,
        out_shape=(out, out),
        in_specs=[vmem, any_spec, vmem, vmem],
        out_specs=(any_spec, any_spec),
        scratch_shapes=[
            pltpu.VMEM((8, own, cols), F32),
            pltpu.VMEM((8, own, cols), F32),
            pltpu.VMEM((8, own, cols), F32),
            pltpu.VMEM((2, own, cols), F32),
            pltpu.VMEM((2, own, cols), F32),
            pltpu.VMEM((2, own, width), F32),
            pltpu.VMEM((16, own, width), F32),
            pltpu.VMEM((own, width), F32),
            dma((8,)), dma((8,)), dma((8,)), dma((8,)),
            dma((16,)), dma((1,)), dma((2, 16)), dma((2,)), dma((1,)), dma((16,)),
            dma((2, 8)), dma((2, 16)), dma((2, 8)), dma((2, 4)), dma((2, 4)), dma((2, 4)), dma((2, 4)),
            dma((5,)),
        ],
        compiler_params=pltpu.CompilerParams(
            collective_id=0, has_side_effects=True, vmem_limit_bytes=32 * 1024 * 1024
        ),
        name="exchange",
    )(picked, matrix, piv_col, piv_row)


def split(value, n):
    terms = []
    for _ in range(n):
        term = value.astype(BF16)
        terms.append(term)
        value = value - term.astype(F32)
    return terms


def update_kernel(piv_col, piv_row, m, qc, qr, coupling, out, hot_t, panel, lead):
    r, c = lax.axis_index("row"), lax.axis_index("col")
    tile, cols = out.shape
    width = coupling.shape[0]
    step = pl.program_id(0)
    row_start = r * cols + step * tile
    col_start = c * cols

    @pl.when(r < c)
    def _():
        out[...] = jnp.zeros_like(out)

    @pl.when((r >= c) & (step == 0))
    def _():
        hot_t[...] = one_hot(piv_col[...], col_start, (width, cols), 1).astype(BF16)
        for i, term in enumerate(split(qc[0], 2)):
            panel[i] = term
        for i, term in enumerate(split(qc[1], 3)):
            lead[i] = term

    def dot(a, b):
        return jnp.dot(a, b, preferred_element_type=F32)

    @pl.when(r >= c)
    def _():
        panel_rows = qr[0].T
        scaled = jnp.dot(panel_rows, coupling[...], precision=HIGHEST, preferred_element_type=F32)
        s_hi, s_lo = split(scaled, 2)
        update = dot(s_hi, panel[0]) + dot(s_hi, panel[1]) + dot(s_lo, panel[0])
        hot = one_hot(piv_row[...], row_start, (tile, width), 0)
        hit_row = jnp.max(hot.astype(F32), axis=1, keepdims=True) > 0
        hit_col = jnp.max(hot_t[...].astype(F32), axis=0, keepdims=True) > 0
        hot = hot.astype(F32).astype(BF16)
        new_rows = dot(hot, lead[0]) + dot(hot, lead[1]) + dot(hot, lead[2])
        lead_cols = jnp.where(hit_row, 0.0, qr[1].T)
        new_cols = sum(dot(term, hot_t[...]) for term in split(lead_cols, 3))
        value = jnp.where(hit_row | hit_col, 0.0, m[...]) + new_rows + new_cols
        spread = jnp.concatenate([panel_rows, jnp.zeros((tile, cols - width), F32)], axis=1)
        places = lax.broadcasted_iota(jnp.int32, (tile, cols), 1)
        value = jnp.where((places < width) & (c == 0), spread, value)
        below = lax.broadcasted_iota(jnp.int32, (tile, cols), 0) + row_start >= places + col_start
        out[...] = jnp.where(below, value - update, 0.0)


def update(piv_col, piv_row, matrix, qc, qr, coupling):
    rows, cols = matrix.shape
    width = coupling.shape[0]
    tile = min(rows, 256)

    def whole(shape):
        return pl.BlockSpec(shape, lambda i: (0,) * len(shape))

    return pl.pallas_call(
        update_kernel,
        grid=(rows // tile,),
        out_shape=jax.ShapeDtypeStruct((rows, cols), F32),
        in_specs=[
            whole((width, 1)),
            whole((1, width)),
            pl.BlockSpec((tile, cols), lambda i: (i, 0)),
            whole((2, width, cols)),
            pl.BlockSpec((2, width, tile), lambda i: (0, 0, i)),
            whole((width, width)),
        ],
        out_specs=pl.BlockSpec((tile, cols), lambda i: (i, 0)),
        scratch_shapes=[
            pltpu.VMEM((width, cols), BF16),
            pltpu.VMEM((2, width, cols), BF16),
            pltpu.VMEM((3, width, cols), BF16),
        ],
        compiler_params=pltpu.CompilerParams(vmem_limit_bytes=48 * 1024 * 1024),
        name="update",
    )(piv_col, piv_row, matrix, qc, qr, coupling)


def order(s):
    return lax.rem(s, 2) * 8 + lax.div(s, 2)


def blocks_of(piv, rows):
    block = jnp.right_shift(piv, rows.bit_length() - 1)
    return jnp.bitwise_and(block, 1) * 8 + jnp.right_shift(block, 1)


def column(row):
    return jnp.broadcast_to(row, (8, row.shape[1])).T[:, :1]


def places(piv_row, rows):
    width = piv_row.shape[1]
    first = lax.broadcasted_iota(jnp.int32, (width, width), 0)
    second = lax.broadcasted_iota(jnp.int32, (width, width), 1)
    block_row = blocks_of(piv_row, rows)
    before = (column(block_row) == block_row) & (first < second)
    return block_row * CAP + jnp.sum(jnp.where(before, 1, 0), axis=0, keepdims=True)


def listed(place_row, piv_row, start, count):
    spot = lax.broadcasted_iota(jnp.int32, (count, place_row.shape[1]), 0) + start
    return jnp.sum(jnp.where(spot == place_row, piv_row + 1, 0), axis=1, keepdims=True) - 1


def hot16(mask):
    return mask.astype(F32).astype(BF16)


def dot16(a, b, dims=((1,), (0,))):
    return lax.dot_general(a, b, (dims, ((), ())), preferred_element_type=F32)


def choose(hot, value):
    return sum(dot16(hot, term) for term in split(value, 3))


def compact_kernel(
    matrix, piv_row, coupling, out,
    block, picked, hall, hall_t, piv_col, spread, hit_col,
    abuf, lead, piece, wbuf, vbuf, w0out, w0z, w0y, w2out, corner, lout, swaps, qc, qr,
    w1s, w0, panel, right, left,
    s_a, r_a, s_sib, r_sib, s_ld, r_ld, s_k, r_k, s_w0, r_w0, s_w2, r_w2, s_w, r_w, s_v, r_v,
    s_l, r_l, s_b, s_x, r_b, s_f, s_t, r_t, s_z, r_z, s_y, s_r, r_y, local,
):
    r, c = lax.axis_index("row"), lax.axis_index("col")
    rows, cols = matrix.shape
    width = piv_row.shape[1]
    half, part = width // 2, cols // 8
    tile = 2 * part
    q, core = lax.div(r, 2), lax.rem(r, 2)
    zl = lax.rem(q, 2)
    x, y, zh = lax.div(r, 4), lax.div(c, 4), lax.rem(c, 4)
    sib = r + 1 - 2 * core
    pair = q + 1 - 2 * zl
    chunk = lax.div(order(c), 4)
    col_start = c * cols

    def remote(src, dst, ssem, rsem, row, col):
        return pltpu.make_async_remote_copy(
            src_ref=src, dst_ref=dst, send_sem=ssem, recv_sem=rsem,
            device_id=(row, col), device_id_type=MESH,
        )

    def arrived(dst, rsem):
        remote(dst, dst, rsem, rsem, sib, c).wait_recv()

    def start(copy):
        copy.start()

    def sent(copy):
        copy.wait_send()

    load = pltpu.make_async_copy(matrix, block, local.at[0])
    load.start()

    barrier = pltpu.get_barrier_semaphore()

    def signal(row, col):
        pl.semaphore_signal(barrier, inc=1, device_id=(row, col), device_id_type=MESH)

    for d in (1, 2, 3):
        signal(r, lax.rem(y + d, 4) * 4 + zh)
    for d in (1, 2, 3):
        signal(r, 4 * y + lax.rem(zh + d, 4))

    @pl.when(r != c)
    def _():
        signal(c, r)

    @pl.when(r > c)
    def _():
        for j in range(8):
            signal(2 * j + lax.rem(c, 2), r)

    for d in range(1, 16):
        signal(lax.rem(r + d, 16), c)

    greeted = 15 + 3 + 3 + jnp.where(r == c, 0, 1)
    greeted = greeted + lax.div(c - core + 1, 2)

    place_row = places(piv_row[...], rows)
    piv_col[...] = column(piv_row[...])
    spots = lax.broadcasted_iota(jnp.int32, (16 * CAP, width), 0)
    hall[...] = hot16(spots == place_row)
    spots = lax.broadcasted_iota(jnp.int32, (width, 16 * CAP), 1)
    hall_t[...] = hot16(spots == column(place_row))
    mine = order(r) * CAP
    left[...] = listed(place_row, piv_row[...], mine, CAP)
    load.wait()
    for t in range(CAP):
        local_row = jnp.sum(jnp.where(place_row == mine + t, piv_row[...] - r * rows, 0))
        picked[pl.ds(t, 1)] = block[pl.ds(jnp.clip(local_row, 0, rows - 1), 1)]
    picked[...] = jnp.where(left[...] >= 0, picked[...], 0.0)

    @pl.when(c == 0)
    def _():
        wbuf[core, q] = picked[:, :width]

    pl.semaphore_wait(barrier, greeted)

    def a_copy(d):
        p = lax.rem(q + d, 8)
        cut = pl.ds(pl.multiple_of(p * part, part), part)
        return remote(picked.at[:, cut], abuf.at[core, q], s_a.at[d], r_a.at[q], 2 * p + core, c)

    for d in range(1, 8):
        a_copy(d).start()

    def k_copies(i, act, along):
        src = wbuf.at[core, q] if i == 0 else corner

        @pl.when((c == 0) if along == 0 else (zh == 0))
        def _():
            for d in (1, 2, 3):
                col = 4 * d if along == 0 else 4 * y + d
                act(remote(src, src, s_k.at[i, 3 * along + d - 1], r_k.at[i], r, col))

    k_copies(0, start, 0)

    def lead_copy(p):
        return remote(
            block.at[pl.ds(0, width), pl.ds(p * part, part)], lead, s_ld.at[p], r_ld.at[0], 2 * p, c
        )

    @pl.when(r == 0)
    def _():
        for p in range(1, 8):
            lead_copy(p).start()

    abuf[core, q] = picked[:, pl.ds(pl.multiple_of(q * part, part), part)]

    def w2_copies(act):
        for s in range(1, 16):
            src = w2out.at[(s % 2) * 8 + s // 2]
            act(remote(src, corner, s_w2.at[s], r_w2.at[0], s, 0))

    @pl.when((r == 0) & (c == 0))
    def _():
        w2out[...] = choose(hall[...], block[:width, :width]).reshape(16, CAP, width)
        w2_copies(start)
        corner[...] = w2out[0]

    w0_copy = remote(w0out, w0z.at[zh], s_w0.at[0], r_w0.at[0, zh], r, 4 * y)
    w0_pair = remote(w0z.at[pl.ds(0, 2)], w0y.at[y], s_w0.at[1], r_w0.at[1, y], r, 0)

    here_piv = listed(place_row, piv_row[...], chunk * 128, 128)
    near = hot16(one_hot(here_piv, col_start, (128, cols), 1))
    w0out[...] = sum(dot16(term, near, ((1,), (1,))) for term in split(picked[...], 3))

    @pl.when(zh != 0)
    def _():
        w0_copy.start()

    for d in range(1, 8):
        p = lax.rem(q + d, 8)
        arrived(abuf.at[core, p], r_a.at[p])
    a_sib = remote(abuf.at[core], abuf.at[core], s_sib.at[1], r_sib.at[1], sib, c)
    a_sib.start()
    arrived(abuf.at[1 - core], r_sib.at[1])

    def slot(k):
        return pl.ds(pl.multiple_of(k * half, half), half)

    piece[...] = choose(hall_t[slot(core)], abuf[...].reshape(16 * CAP, part))

    t_copy = remote(piece, qr.at[q, slot(core)], s_t.at[0], r_t.at[0], c, r)

    @pl.when(r != c)
    def _():
        t_copy.start()

    @pl.when(r == c)
    def _():
        qr[q, slot(core)] = piece[...]

    def wanted(p):
        return 2 * p + 1 >= c

    def b_copies(act):
        @pl.when(wanted(6 + 1 - zl))
        def _():
            act(
                remote(piece, qc.at[q, slot(core)], s_b.at[0], r_b.at[core, q], 2 * pair + core, c)
            )

        for d in range(1, 4):
            p = lax.rem(q + 2 * d, 8)

            @pl.when(wanted(p))
            def _():
                act(remote(piece, qc.at[q, slot(core)], s_b.at[d], r_b.at[core, q], 2 * p + core, c))

    def x_copies(act):
        for d in range(1, 4):
            p = lax.rem(q + 2 * d, 8)
            ref = qc.at[pair, slot(core)]

            @pl.when(wanted(p))
            def _():
                act(remote(ref, ref, s_x.at[d], r_b.at[core, pair], 2 * p + core, c))

    def f_copy(p):
        ref = qc.at[p, slot(core)]
        return remote(ref, ref, s_f.at[p], r_b.at[core, p], sib, c)

    def forward(p):
        @pl.when(sib >= c)
        def _():
            f_copy(p).start()

    b_copies(start)
    qc[q, slot(core)] = piece[...]
    forward(q)

    def w_copies(act, buf, ssem, rsem):
        for d in range(1, 8):
            p = lax.rem(q + d, 8)

            @pl.when(wanted(p))
            def _():
                act(
                    remote(buf.at[core, q], buf.at[core, q], ssem.at[d], rsem.at[q], 2 * p + core, c)
                )

    @pl.when(c != 0)
    def _():
        arrived(wbuf.at[core, q], r_k.at[0])

    k_copies(0, start, 1)

    hot = one_hot(piv_col[...], col_start, (width, cols), 1).astype(F32)
    hit_col[...] = jnp.max(hot, axis=0, keepdims=True)
    spread[...] = hot.astype(BF16)

    def need(there):
        return 4 * there + zh <= r

    up, down, across = lax.rem(y + 1, 4), lax.rem(y + 3, 4), lax.rem(y + 2, 4)

    def y_ref(owner, k):
        j = lax.rem(zh + k, 4)
        return qr.at[2 * owner + lax.div(j, 2), slot(lax.rem(j, 2))]

    def z_copies(act):
        for d in (1, 3, 2):
            there = lax.rem(zh + d, 4)

            @pl.when(there <= r)
            def _():
                act(
                    remote(
                        y_ref(y, 0), y_ref(y, 0), s_z.at[d], r_z.at[(4 - d) % 4], r, 4 * y + there
                    )
                )

    def relays(node, k, way):
        off = lax.rem(node + 4 - x, 4)
        return (off == 2) | ((off != 0) & (way == k % 2))

    def y_copies(k, act):
        for way, to in ((0, up), (1, down)):
            ref = y_ref(y, k)

            @pl.when(need(to) | (need(across) & relays(to, k, way)))
            def _():
                act(remote(ref, ref, s_y.at[way, k], r_y.at[y, k], r, 4 * to + zh))

    def relay(k, act):
        for way, owner, to in ((0, down, up), (1, up, down)):
            ref = y_ref(owner, k)

            @pl.when(need(to) & relays(y, k, way))
            def _():
                act(remote(ref, ref, s_r.at[way, k], r_y.at[owner, k], r, 4 * to + zh))

    def run_relay(k):
        for way, owner, to in ((0, down, up), (1, up, down)):
            @pl.when(relays(y, k, way) & (need(y) | need(to)))
            def _():
                arrived(y_ref(owner, k), r_y.at[owner, k])

        relay(k, start)

    def run_y(k):
        @pl.when(zh <= r)
        def _():
            arrived(y_ref(y, k), r_z.at[k])

        y_copies(k, start)

    @pl.when((c == 0) & (r != 0))
    def _():
        arrived(corner, r_w2.at[0])

    k_copies(1, start, 0)

    @pl.when(zh == 0)
    def _():
        for d in (1, 2, 3):
            arrived(w0z.at[d], r_w0.at[0, d])
        w0z[0] = w0out[...] + w0z[2]
        w0z[1] = w0z[1] + w0z[3]

        @pl.when(y != 0)
        def _():
            w0_pair.start()

    @pl.when(r != c)
    def _():
        arrived(y_ref(y, 0), r_t.at[0])

    y_copies(0, start)
    z_copies(start)

    @pl.when(wanted(6 + zl))
    def _():
        arrived(qc.at[pair, slot(core)], r_b.at[core, pair])

    x_copies(start)
    forward(pair)
    w_copies(start, wbuf, s_w, r_w)
    run_relay(0)

    @pl.when(c == 0)
    def _():
        for d in (1, 2, 3):
            arrived(w0y.at[d], r_w0.at[1, d])
        w0y[0] = w0z[:2]
        total = jnp.zeros((CAP, width), F32)
        for j in range(4):
            listing = w0y[2 * (j % 2), j // 2] + w0y[2 * (j % 2) + 1, j // 2]
            hot = hall[128 * j : 128 * (j + 1)]
            total = total + sum(dot16(term, hot) for term in split(listing, 3))
        vbuf[core, q] = total
        w_copies(start, vbuf, s_v, r_v)

    run_y(1)
    run_y(3)
    lead_sib = remote(lead, lead, s_sib.at[0], r_sib.at[0], sib, c)

    @pl.when(r == 0)
    def _():
        lead[...] = block[:width, :part]

    @pl.when((core == 0) & (r != 0))
    def _():
        arrived(lead, r_ld.at[0])

    @pl.when(core == 0)
    def _():
        lead_sib.start()

    @pl.when(core == 1)
    def _():
        arrived(lead, r_sib.at[0])

    lists = hall[pl.ds(pl.multiple_of(core * 8 * CAP, 8 * CAP), 8 * CAP)]
    lout[...] = choose(lists, lead[...]).reshape(8, CAP, part)

    def l_copies(act, act_here):
        for d in range(8):
            j = lax.rem(q + d, 8)
            s = 2 * j + core
            as_row = s >= c
            row, col = jnp.where(as_row, s, c), jnp.where(as_row, c, s)
            kind = jnp.where(as_row, 0, 1)
            here = as_row & (s == r)

            @pl.when(jnp.logical_not(here))
            def _():
                act(remote(lout.at[j], swaps.at[kind, q], s_l.at[j], r_l.at[kind, q], row, col))

            @pl.when(here)
            def _():
                act_here(j)

    def keep_lead(j):
        swaps[0, q] = lout[j]

    l_copies(start, keep_lead)


    w_sib = remote(wbuf.at[core], wbuf.at[core], s_sib.at[2], r_sib.at[2], sib, c)
    v_sib = remote(vbuf.at[core], vbuf.at[core], s_sib.at[3], r_sib.at[3], sib, c)

    @pl.when((zh == 0) & (y != 0))
    def _():
        arrived(corner, r_k.at[1])

    k_copies(1, start, 1)
    for d in range(1, 4):
        p = lax.rem(q + 2 * d, 8)

        @pl.when(wanted(q))
        def _():
            arrived(qc.at[p, slot(core)], r_b.at[core, p])

        forward(p)

    @pl.when(wanted(q))
    def _():
        for d in range(1, 8):
            p = lax.rem(q + d, 8)
            arrived(wbuf.at[core, p], r_w.at[p])

    @pl.when(sib >= c)
    def _():
        w_sib.start()

    run_relay(1)
    run_relay(3)
    run_y(2)

    for d in range(1, 4):
        p = lax.rem(pair + 2 * d, 8)

        @pl.when(wanted(q))
        def _():
            arrived(qc.at[p, slot(core)], r_b.at[core, p])

        forward(p)

    @pl.when(c == 0)
    def _():
        for d in range(1, 8):
            p = lax.rem(q + d, 8)
            arrived(vbuf.at[core, p], r_v.at[p])
        v_sib.start()
        arrived(vbuf.at[1 - core], r_sib.at[3])
        w0[...] = choose(hall_t[...], vbuf[...].reshape(16 * CAP, width))

    @pl.when(zh != 0)
    def _():
        arrived(corner, r_k.at[1])

    @pl.when(r < c)
    def _():
        out[...] = jnp.zeros_like(out)

    @pl.when(r >= c)
    def _():
        arrived(wbuf.at[1 - core], r_sib.at[2])
        w1 = choose(hall_t[...], wbuf[...].reshape(16 * CAP, width))
        for i, term in enumerate(split(w1, 3)):
            w1s[i] = term
        for p in range(8):
            arrived(qc.at[p, slot(1 - core)], r_b.at[1 - core, p])
        placed = [dot16(w1s[i], spread[...]) for i in range(2)]
        hit = hit_col[...] > 0
        for p in range(8):
            cut = slice(p * part, (p + 1) * part)
            value = qc[p]
            if p < width // part:
                value = jnp.where(c == 0, w0[:, cut], value)
            for j, term in enumerate(split(value, 2)):
                term = jnp.where(hit[:, cut], placed[j][:, cut], term.astype(F32))
                panel[j, :, cut] = term.astype(BF16)
        for p in range(8):
            @pl.when(p != q)
            def _():
                arrived(swaps.at[0, p], r_l.at[0, p])
        rows_in = jnp.concatenate([swaps[0, p] for p in range(8)], axis=1)
        placed = sum(dot16(term, spread[...]) for term in split(corner[...], 3))
        rows_in = jnp.where(hit, placed, rows_in)
        for j, term in enumerate(split(rows_in, 3)):
            right[j * CAP : (j + 1) * CAP] = term
        col_piv = listed(place_row, piv_row[...], order(c) * CAP, CAP)
        hot = hot16(one_hot(col_piv, col_start, (CAP, cols), 1))
        for j in range(3):
            right[(3 + j) * CAP : (4 + j) * CAP] = hot


    def tile_update(owner):
        row_start = r * rows + owner * tile
        hot = one_hot(left[...], row_start, (CAP, tile), 1).astype(F32)
        hit = jnp.max(hot, axis=0, keepdims=True)
        rows_t = jnp.concatenate([qr[2 * owner], qr[2 * owner + 1]], axis=1)
        near = hot16(one_hot(piv_col[...], row_start, (width, tile), 1))
        rows_t = jnp.where(hit > 0, sum(dot16(w1s[i], near) for i in range(3)), rows_t)
        rows_t = jnp.where((r == 0) & (c == 0) & (owner == 0), w0[...], rows_t)
        scaled = lax.dot_general(
            coupling[...], rows_t, (((0,), (0,)), ((), ())),
            precision=HIGHEST, preferred_element_type=F32,
        )
        s_hi, s_lo = split(scaled, 2)
        lanes = ((0,), (0,))
        change = dot16(s_hi, panel[0], lanes) + dot16(s_hi, panel[1], lanes)
        change = change + dot16(s_lo, panel[0], lanes)
        kind = jnp.where(r == c, 0, 1)
        cols_in = jnp.concatenate([swaps[kind, 2 * owner + i] for i in range(2)], axis=1)
        cols_in = jnp.where(hit > 0, 0.0, cols_in)
        hot = hot.astype(BF16)
        lhs = jnp.concatenate([hot, hot, hot] + split(cols_in, 3), axis=0)
        moved = dot16(lhs, right[...], lanes)
        at = pl.ds(pl.multiple_of(owner * tile, tile), tile)
        gone = (column(hit) > 0) | (hit_col[...] > 0)
        value = jnp.where(gone, 0.0, block[at]) + moved
        places_col = lax.broadcasted_iota(jnp.int32, (1, cols), 1) + col_start
        below = lax.broadcasted_iota(jnp.int32, (tile, 1), 0) + row_start >= places_col
        out[at] = jnp.where(below, value - change, 0.0)

        @pl.when(c == 0)
        def _():
            out[at, :width] = jnp.where(below[:, :width], rows_t.T - change[:, :width], 0.0)

    @pl.when(r > c)
    def _():
        for p in range(8):
            arrived(swaps.at[1, p], r_l.at[1, p])

    @pl.when(r >= c)
    def _():
        tile_update(y)

    run_relay(2)

    @pl.when(r >= c)
    def _():
        for k in range(4):
            for way, owner in ((0, down), (1, up)):
                @pl.when(jnp.logical_not(relays(y, k, way)))
                def _():
                    arrived(y_ref(owner, k), r_y.at[owner, k])

        def side(i, _):
            tile_update(jnp.where(i == 0, up, down))
            return 0

        lax.fori_loop(0, 2, side, 0)
        for k in range(4):
            arrived(y_ref(across, k), r_y.at[across, k])
        tile_update(across)

    @pl.when(zh != 0)
    def _():
        w0_copy.wait_send()

    @pl.when((zh == 0) & (y != 0))
    def _():
        w0_pair.wait_send()

    for i in range(2):
        for along in range(2):
            k_copies(i, sent, along)

    @pl.when(r == 0)
    def _():
        for p in range(1, 8):
            lead_copy(p).wait_send()

    @pl.when(core == 0)
    def _():
        lead_sib.wait_send()

    a_sib.wait_send()
    for d in range(1, 8):
        a_copy(d).wait_send()

    @pl.when(c == 0)
    def _():
        w_copies(sent, vbuf, s_v, r_v)
        v_sib.wait_send()

        @pl.when(r == 0)
        def _():
            w2_copies(sent)

    @pl.when(r != c)
    def _():
        t_copy.wait_send()

    b_copies(sent)
    x_copies(sent)
    w_copies(sent, wbuf, s_w, r_w)
    z_copies(sent)
    l_copies(sent, lambda j: None)
    for k in range(4):
        y_copies(k, sent)
        relay(k, sent)

    @pl.when(sib >= c)
    def _():
        w_sib.wait_send()
        for p in range(8):
            f_copy(p).wait_send()


def compact(matrix, piv_row, coupling):
    rows, cols = matrix.shape
    width = piv_row.shape[1]
    half, part = width // 2, cols // 8
    dma = pltpu.SemaphoreType.DMA
    vmem = pl.BlockSpec(memory_space=pltpu.VMEM)
    return pl.pallas_call(
        compact_kernel,
        out_shape=jax.ShapeDtypeStruct((rows, cols), F32),
        in_specs=[pl.BlockSpec(memory_space=pl.ANY), vmem, vmem],
        out_specs=vmem,
        scratch_shapes=[
            pltpu.VMEM((rows, cols), F32),
            pltpu.VMEM((CAP, cols), F32),
            pltpu.VMEM((16 * CAP, width), BF16),
            pltpu.VMEM((width, 16 * CAP), BF16),
            pltpu.VMEM((width, 1), jnp.int32),
            pltpu.VMEM((width, cols), BF16),
            pltpu.VMEM((1, cols), F32),
            pltpu.VMEM((2, 8, CAP, part), F32),
            pltpu.VMEM((width, part), F32),
            pltpu.VMEM((half, part), F32),
            pltpu.VMEM((2, 8, CAP, width), F32),
            pltpu.VMEM((2, 8, CAP, width), F32),
            pltpu.VMEM((CAP, 128), F32),
            pltpu.VMEM((4, CAP, 128), F32),
            pltpu.VMEM((4, 2, CAP, 128), F32),
            pltpu.VMEM((16, CAP, width), F32),
            pltpu.VMEM((CAP, width), F32),
            pltpu.VMEM((8, CAP, part), F32),
            pltpu.VMEM((2, 8, CAP, part), F32),
            pltpu.VMEM((8, width, part), F32),
            pltpu.VMEM((8, width, part), F32),
            pltpu.VMEM((3, width, width), BF16),
            pltpu.VMEM((width, width), F32),
            pltpu.VMEM((2, width, cols), BF16),
            pltpu.VMEM((6 * CAP, cols), BF16),
            pltpu.VMEM((CAP, 1), jnp.int32),
            dma((8,)), dma((8,)), dma((4,)), dma((4,)), dma((8,)), dma((1,)),
            dma((2, 6)), dma((2,)), dma((2,)), dma((2, 4)), dma((16,)), dma((1,)),
            dma((8,)), dma((8,)), dma((8,)), dma((8,)), dma((8,)), dma((2, 8)),
            dma((4,)), dma((4,)), dma((2, 8)), dma((8,)), dma((1,)), dma((1,)), dma((4,)), dma((4,)),
            dma((2, 4)), dma((2, 4)), dma((4, 4)),
            dma((1,)),
        ],
        compiler_params=pltpu.CompilerParams(
            collective_id=1, has_side_effects=True, vmem_limit_bytes=40 * 1024 * 1024
        ),
        name="compact",
    )(matrix, piv_row, coupling)


def per_device(matrix, pivots, coupling):
    width = coupling.shape[0]
    rows = matrix.shape[0]
    piv_row = pivots.reshape(1, width)

    def few(matrix, pivots, coupling):
        return compact(matrix, piv_row, coupling)

    def general(matrix, pivots, coupling):
        piv_col = pivots.reshape(width, 1)
        picked = pick(matrix, pivots)
        qc, qr = exchange(picked, matrix, piv_col, piv_row)
        return update(piv_col, piv_row, matrix, qc, qr, coupling)

    blocks = jnp.arange(16, dtype=jnp.int32)[:, None]
    inside = (piv_row >= blocks * rows) & (piv_row < (blocks + 1) * rows)
    counts = jnp.sum(inside.astype(jnp.int32), axis=1)
    return lax.cond(jnp.max(counts) <= CAP, few, general, matrix, pivots, coupling)


def solution(mesh):
    return jax.shard_map(
        per_device,
        mesh=mesh,
        in_specs=(P("row", "col"), P(), P()),
        out_specs=P("row", "col"),
        check_vma=False,
    )
```
